32 devices in a mesh: dp: 8 (over z, y), tp: 4 (over x, core).
Axes of the slice: x: 2, y: 2, z: 4, core: 2. Of those that a mesh axis runs over, the one named last changes fastest.
Arguments:
- cell_inputs: bfloat16 [512, 64, 1120], P('dp', 'tp'), may hold values from -6 to 6
- out_grad: bfloat16 [512, 64, 1120], P('dp', 'tp'), may hold values from -6 to 6
- lengths: int32 [512], P('dp'), may hold values from 0 to 64, as said below
- datasets: int32 [512], P('dp'), may hold values from 0 to 31
- norm_gain: bfloat16 [2, 1120], replicated, may hold values from 0.5 to 1.5
- norm_bias: bfloat16 [2, 1120], replicated, may hold values from -1.5 to 1.5
- qkv_weight: bfloat16 [1120, 3, 1120], P(None, None, 'tp'), may hold values from -0.1875 to 0.1875
- qv_bias: bfloat16 [2, 1120], P(None, 'tp'), may hold values from -3 to 3
- out_weight: bfloat16 [1120, 1120], P('tp'), may hold values from -0.75 to 0.75
- out_bias: bfloat16 [2, 1120], replicated, may hold values from -1.5 to 1.5
- up_weight: bfloat16 [1120, 4480], P(None, 'tp'), may hold values from -0.1875 to 0.1875
- up_bias: bfloat16 [4480], P('tp'), may hold values from -3 to 3
- down_weight: bfloat16 [4480, 1120], P('tp'), may hold values from -0.09375 to 0.09375
- dataset_table: bfloat16 [32, 1120], replicated, may hold values from -3 to 3
Outputs:
- cell_outputs: bfloat16 [512, 64, 1120], P('dp', 'tp')
- input_grad: bfloat16 [512, 64, 1120], P('dp', 'tp')
- norm_gain_grad: float32 [2, 1120], replicated
- norm_bias_grad: float32 [2, 1120], replicated
- qkv_weight_grad: float32 [1120, 3, 1120], P(None, None, 'tp')
- qv_bias_grad: float32 [2, 1120], P(None, 'tp')
- out_weight_grad: float32 [1120, 1120], P('tp')
- out_bias_grad: float32 [2, 1120], replicated
- up_weight_grad: float32 [1120, 4480], P(None, 'tp')
- up_bias_grad: float32 [4480], P('tp')
- down_weight_grad: float32 [4480, 1120], P('tp')
- table_grad: float32 [32, 1120], replicated
The draws below stay inside these ranges and needn't reach their ends.
Inputs may be any that keep to these rules, and one draw needn't show every extreme that they name: `lengths`: the 64 consecutive entries of one dp group hold its cells; the cells with tokens occupy the group's first slots and have 64 // 4 to 64 tokens, slot 0 of every group exactly 64; the other slots have length 0. Each group has 4 to 60 cells with tokens, one group exactly 60, and all groups together have exactly 256.
All inputs are finite; a program needn't handle non-finite values.
Results may differ from the reference program's by a relative error of at most 0.012.
Values may be sent and summed in bfloat16 or wider, within the bound.
No kernel may reach another device: no remote copies, remote signals or barrier semaphores. Data moves between devices by JAX's collectives and lax.ppermute only.
A program may use at most 192 MiB of HBM per device.

```python
import math
import jax
import jax.numpy as jnp
from jax import lax

D = 1120
HEADS = 20
HEAD_DIM = 56
FF = 4480
NDATA = 32
CELL = 64
SLOTS = 64
HELD = 32
CELLS = 512


def draw_lengths(key, part):
    key = jax.random.fold_in(key, 11)
    key_live, key_order, key_sizes = jax.random.split(key, 3)
    groups = CELLS // SLOTS
    half_groups = groups // 2
    spread = jax.random.randint(key_live, (half_groups,), 0, HELD - 3)
    spread = spread.at[0].set(HELD - 4)
    live_count = jnp.concatenate([HELD + spread, HELD - spread])
    permuted = jax.random.permutation(key_order, groups)
    live_count = live_count[permuted]
    cell_sizes = jax.random.randint(key_sizes, (groups, SLOTS), CELL // 4, CELL + 1)
    cell_sizes = cell_sizes.at[:, 0].set(CELL)
    slot_index = jnp.arange(SLOTS, dtype=jnp.int32)[None, :]
    filled = jnp.where(slot_index < live_count[:, None], cell_sizes, 0)
    return filled.reshape(-1).astype(jnp.int32)


def touch_ends(entries, key, low, high):
    index_at = [jax.random.randint(jax.random.fold_in(key, axis), (), 0, length) for axis, length in enumerate(entries.shape)]
    widest = entries.shape.index(max(entries.shape))
    neighbour = index_at[:widest] + [(index_at[widest] + 1) % entries.shape[widest]] + index_at[widest + 1:]
    return entries.at[tuple(index_at)].set(low).at[tuple(neighbour)].set(high)


def block_levels(key, dims, shards, low, largest):
    factor_of, own = 1.0, jax.random.fold_in(key, 6)
    for axis_at, shards_of in shards:
        draws = jnp.exp(jax.random.uniform(jax.random.fold_in(own, axis_at), (shards_of,), jnp.float32, low / len(shards), largest / len(shards)))
        factor_of = factor_of * jnp.repeat(draws, dims[axis_at] // shards_of).reshape([-1 if axis == axis_at else 1 for axis in range(len(dims))])
    return factor_of


def scatter_about(stream_key, extent, deviation, limit, cuts=(), kind=jnp.bfloat16):
    values = jax.random.normal(stream_key, extent, jnp.float32) * deviation
    if len(cuts) > 0:
        values = block_levels(stream_key, extent, cuts, -0.22, 0.18) * values
    return jnp.clip(values, min=-limit, max=limit).astype(kind)


def setup_inputs(seed: int = 0) -> dict:
    keys = jax.random.split(jax.random.key(seed), 15)
    return {
        "cell_inputs": scatter_about(keys[0], (CELLS, CELL, D), 1.0, 6.0, ((0, 8), (1, 4))),
        "out_grad": scatter_about(keys[1], (CELLS, CELL, D), 1.0, 6.0, ((0, 8), (1, 4))),
        "lengths": draw_lengths(jax.random.fold_in(keys[14], 71), 0),
        "datasets": touch_ends(jax.random.randint(keys[3], (CELLS,), 0, NDATA), jax.random.fold_in(keys[3], 1), 0, NDATA - 1).astype(jnp.int32),
        "norm_gain": jnp.clip(1.0 + 0.1 * jax.random.normal(keys[4], (2, D), jnp.float32), 0.5, 1.5).astype(jnp.bfloat16),
        "norm_bias": scatter_about(keys[5], (2, D), 0.3, 1.5),
        "qkv_weight": scatter_about(keys[6], (D, 3, D), D ** -0.5, 0.1875, ((2, 4),)),
        "qv_bias": scatter_about(keys[7], (2, D), 0.5, 3.0, ((1, 4),)),
        "out_weight": scatter_about(keys[8], (D, D), (D // 16) ** -0.5, 0.75, ((0, 4),)),
        "out_bias": scatter_about(keys[9], (2, D), 0.3, 1.5),
        "up_weight": scatter_about(keys[10], (D, FF), D ** -0.5, 0.1875, ((1, 4),)),
        "up_bias": scatter_about(keys[11], (FF,), 0.5, 3.0, ((0, 4),)),
        "down_weight": scatter_about(keys[12], (FF, D), FF ** -0.5, 0.09375, ((0, 4),)),
        "dataset_table": scatter_about(keys[13], (NDATA, D), 0.5, 3.0),
    }


@jax.custom_vjp
def low(v):
    return lax.optimization_barrier(v.astype(jnp.bfloat16)).astype(jnp.float32)

@jax.custom_vjp
def low_back(v):
    return v

def low_keep(v):
    return (low(v), None)

def low_pass(kept, grad):
    return (grad,)

def back_keep(v):
    return (v, None)

def back_low(kept, grad):
    return (low(grad),)
low.defvjp(low_keep, low_pass)
low_back.defvjp(back_keep, back_low)
EPSILON = 1e-05
HIGHEST_PRECISION = lax.Precision.HIGHEST

def rounded_pair(value):
    return low(low_back(value))

def layer_norm(inputs, scale_row, shift_row):
    center = inputs - lax.optimization_barrier(jnp.mean(inputs, axis=-1, keepdims=True))
    spread = lax.optimization_barrier(jnp.mean(center * center, axis=-1, keepdims=True))
    return center * lax.rsqrt(spread + EPSILON) * scale_row + shift_row

def block_forward(weight_set, cell_rows, valid_rows, onehot):
    norm_gain, norm_bias, qkv_weight, qv_bias, out_weight, out_bias, up_weight, up_bias, down_weight, dataset_table = weight_set
    cell_count = cell_rows.shape[0]
    embedded = jnp.dot(onehot, dataset_table, precision=HIGHEST_PRECISION)
    start_rows = cell_rows + embedded[:, None, :]
    normed = low(layer_norm(start_rows, norm_gain[0], norm_bias[0]))
    shift_rows = jnp.stack([qv_bias[0], jnp.zeros_like(qv_bias[0]), qv_bias[1]])
    projected = rounded_pair(jnp.einsum('bcd,dke->bcke', normed, qkv_weight, precision=HIGHEST_PRECISION) + shift_rows)
    head_shape = (cell_count, CELL, HEADS, HEAD_DIM)
    queries = projected[:, :, 0].reshape(head_shape)
    key_rows = projected[:, :, 1].reshape(head_shape)
    value_rows = projected[:, :, 2].reshape(head_shape)
    score_scale = 1.0 / math.sqrt(HEAD_DIM)
    raw_scores = low_back(jnp.einsum('bqhe,bkhe->bhqk', queries, key_rows, precision=HIGHEST_PRECISION) * score_scale)
    causal = lax.broadcasted_iota(jnp.int32, (CELL, CELL), 0) >= lax.broadcasted_iota(jnp.int32, (CELL, CELL), 1)
    masked = jnp.where(causal, raw_scores, -1e+30)
    attend = low(jax.nn.softmax(masked, axis=-1))
    context = rounded_pair(jnp.einsum('bhqk,bkhe->bqhe', attend, value_rows, precision=HIGHEST_PRECISION))
    context = context.reshape(cell_count, CELL, D)
    middle = start_rows + low_back(jnp.einsum('bce,ed->bcd', context, out_weight, precision=HIGHEST_PRECISION)) + out_bias[0]
    normed_second = low(layer_norm(middle, norm_gain[1], norm_bias[1]))
    hidden = low_back(jnp.einsum('bcd,df->bcf', normed_second, up_weight, precision=HIGHEST_PRECISION) + up_bias)
    active = low(jax.nn.gelu(hidden, approximate=False))
    branch = low_back(jnp.einsum('bcf,fd->bcd', active, down_weight, precision=HIGHEST_PRECISION))
    return (middle + branch + out_bias[1]) * valid_rows[:, :, None]

def reference(cell_inputs, out_grad, lengths, datasets, norm_gain, norm_bias, qkv_weight, qv_bias, out_weight, out_bias, up_weight, up_bias, down_weight, dataset_table):
    weight_set = tuple((item.astype(jnp.float32) for item in (norm_gain, norm_bias, qkv_weight, qv_bias, out_weight, out_bias, up_weight, up_bias, down_weight, dataset_table)))
    groups = CELLS // SLOTS
    cell_rows = cell_inputs.astype(jnp.float32).reshape(groups, SLOTS, CELL, D)
    cot_rows = out_grad.astype(jnp.float32).reshape(groups, SLOTS, CELL, D)
    positions = jnp.arange(CELL, dtype=jnp.int32)
    valid_rows = (positions[None, :] < lengths[:, None]).astype(jnp.float32).reshape(groups, SLOTS, CELL)
    table_ids = jnp.arange(NDATA, dtype=jnp.int32)
    onehot = (datasets[:, None] == table_ids[None, :]).astype(jnp.float32).reshape(groups, SLOTS, NDATA)

    def group_step(totals, pieces):
        rows_now, cot_now, valid_now, onehot_now = pieces

        def forward(weights_now, input_rows):
            return block_forward(weights_now, input_rows, valid_now, onehot_now)
        outputs, pullback = jax.vjp(forward, weight_set, rows_now)
        weight_grads, input_grads = pullback(cot_now)
        totals = jax.tree.map(lambda total, extra: total + extra, totals, weight_grads)
        return (totals, (outputs.astype(jnp.bfloat16), input_grads.astype(jnp.bfloat16)))
    zero_grads = jax.tree.map(jnp.zeros_like, weight_set)
    totals, (outputs, input_grads) = lax.scan(group_step, zero_grads, (cell_rows, cot_rows, valid_rows, onehot))
    return (outputs.reshape(CELLS, CELL, D), input_grads.reshape(CELLS, CELL, D), totals[0], totals[1], totals[2], totals[3], totals[4], totals[5], totals[6], totals[7], totals[8], totals[9])
```

```python
import functools
import math

import jax
import jax.numpy as jnp
from jax import lax
from jax.experimental import pallas as pl
from jax.experimental.pallas import tpu as pltpu
from jax.sharding import PartitionSpec as P

HEAD_DIM = 56
EPSILON = 1e-05
BLOCK = 256
META_BLOCKS = 8
TILE = 16
F32 = jnp.float32
LOW = jnp.bfloat16
VMEM_BYTES = 56 * 1024 * 1024
BYTES_PER_US = 3_690_000

NBLK, NCELL, HALF, QUARTER, TILE_SRC, TILE_SET, TILE_LEN, TILE_DST, CELL_OFF, CELL_ROWS, META = 0, 1, 2, 3, 8, 136, 264, 392, 520, 552, 584


def swap(value, axis, bit):
    count = lax.axis_size(axis)
    if value.ndim == 2 and value.shape[0] % TILE == 0:
        chunk = TILE if value.shape[0] // TILE % 128 else 2 * TILE
        tiled = value.reshape(value.shape[0] // chunk, chunk, value.shape[1])
        return swap(tiled, axis, bit).reshape(value.shape)
    return lax.ppermute(value, axis, [(i, i ^ bit) for i in range(count)])


CHUNKS = 4


def swap_cores(parts):
    return tuple(swap(part, "tp", 1) for part in parts)


class Sequence:
    def __init__(self):
        self.last = ()

    def then(self, *values):
        if not self.last:
            return values
        return lax.optimization_barrier((*values, *self.last))[: len(values)]

    def done(self, *values):
        self.last = (values[-1],)

    def step(self, *values):
        values = self.then(*values)
        self.last = (values[-1],)
        return values


def dot(a, b):
    return jnp.dot(a, b, preferred_element_type=F32)


def dot_nt(a, b):
    return lax.dot_general(a, b, (((1,), (1,)), ((), ())), preferred_element_type=F32)


def dot_tn(a, b):
    return lax.dot_general(a, b, (((0,), (0,)), ((), ())), preferred_element_type=F32)


def row_norm(rows):
    center = rows - jnp.mean(rows, axis=-1, keepdims=True)
    spread = jnp.mean(center * center, axis=-1, keepdims=True)
    scale = lax.rsqrt(spread + EPSILON)
    return center * scale, scale


def norm_back(grad, unit, scale, gain):
    scaled = grad * gain
    first = jnp.mean(scaled, axis=-1, keepdims=True)
    second = jnp.mean(scaled * unit, axis=-1, keepdims=True)
    return scale * (scaled - first - unit * second)


def whole(shape):
    zeros = (0,) * len(shape)
    return pl.BlockSpec(shape, lambda i, meta: zeros, pipeline_mode=pl.Buffered(1))


def rows_spec(width):
    return pl.BlockSpec((BLOCK, width), lambda i, meta: (jnp.minimum(i, meta[NBLK] - 1), 0))


PART_BLOCKS = META_BLOCKS // CHUNKS


def part_specs(width):
    def index(at, i, meta):
        return jnp.clip(jnp.minimum(i, meta[NBLK] - 1) - at * PART_BLOCKS, 0, PART_BLOCKS - 1), 0

    return [pl.BlockSpec((BLOCK, width), functools.partial(index, at)) for at in range(CHUNKS)]


def part_outs(width):
    def index(at, i, meta):
        return jnp.clip(i - at * PART_BLOCKS, 0, PART_BLOCKS - 1), 0

    return tuple(pl.BlockSpec((BLOCK, width), functools.partial(index, at)) for at in range(CHUNKS))


def part_shapes(rows, width):
    return (jax.ShapeDtypeStruct((rows // CHUNKS, width), LOW),) * CHUNKS


def add_parts(step, mine, far, rows):
    for at, (a, b) in enumerate(zip(mine, far)):

        @pl.when(step // PART_BLOCKS == at)
        def _():
            rows[...] = a[...].astype(F32) + b[...].astype(F32)


def put_part(step, value, parts):
    for at, part in enumerate(parts):

        @pl.when(step // PART_BLOCKS == at)
        def _():
            part[...] = value


def rows_out(width):
    return pl.BlockSpec((BLOCK, width), lambda i, meta: (i, 0))


ANYWHERE = pl.BlockSpec(memory_space=pl.ANY)


def call(kernel, meta, operands, in_specs, out_shape, out_specs, grid, scratch=(), cost=5, name=None):
    return pl.pallas_call(
        kernel,
        grid_spec=pltpu.PrefetchScalarGridSpec(
            num_scalar_prefetch=1,
            grid=grid,
            in_specs=in_specs,
            out_specs=out_specs,
            scratch_shapes=list(scratch),
        ),
        out_shape=out_shape,
        compiler_params=pltpu.CompilerParams(
            dimension_semantics=("arbitrary",) * len(grid), vmem_limit_bytes=VMEM_BYTES
        ),
        cost_estimate=pl.CostEstimate(flops=0, bytes_accessed=cost * BYTES_PER_US, transcendentals=0),
        name=name,
    )(meta, *operands)


def load_tiles(sources, tiles, sems, count):
    copies = [
        pltpu.make_async_copy(source, tiles.at[pl.ds(at * count, count)], sems.at[at])
        for at, source in enumerate(sources)
    ]
    for copy in copies:
        copy.start()
    for copy in copies:
        copy.wait()


def begin_kernel(count, meta, a0, a1, a2, a3, table, gain, shift, weight, bias, start, normed, projected, tiles, sems):
    step = pl.program_id(0)

    @pl.when(step == 0)
    def _():
        load_tiles((a0, a1, a2, a3), tiles, sems, count)

    @pl.when(step < meta[NBLK])
    def _():
        for j in range(BLOCK // TILE):
            at = step * (BLOCK // TILE) + j
            tile = tiles[meta[TILE_SRC + at]].astype(F32)
            start[j * TILE : (j + 1) * TILE, :] = tile + table[pl.ds(meta[TILE_SET + at], 1), :]
        unit, _ = row_norm(start[...])
        low = (unit * gain[...] + shift[...]).astype(LOW)
        normed[...] = low
        projected[...] = (dot(low, weight[...]) + bias[...]).astype(LOW)

    @pl.when(step >= meta[NBLK])
    def _():
        projected[...] = jnp.zeros_like(projected)


def project_kernel(meta, normed, eighths, bias, projected, weight, sems):
    step = pl.program_id(0)

    @pl.when(step == 0)
    def _():
        load_eighths(eighths, [weight], sems)

    @pl.when(step < meta[NBLK])
    def _():
        projected[...] = (dot(normed[...], weight[...]) + bias[...]).astype(LOW)

    @pl.when(step >= meta[NBLK])
    def _():
        projected[...] = jnp.zeros_like(projected)


def head_masks(cell, heads, shard):
    lane = lax.broadcasted_iota(jnp.int32, (cell, shard), 1)
    return [(lane >= h * HEAD_DIM) & (lane < (h + 1) * HEAD_DIM) for h in range(heads)]


def spread_heads(rows, masks, heads, low, high):
    part = rows[:, low:high]
    zero = jnp.zeros_like(part)
    return jnp.concatenate([jnp.where(masks[h][:, low:high], part, zero) for h in heads], axis=0)


def head_groups(heads, shard):
    groups = []
    at = 0
    while at < heads:
        end = min(at + 4, heads)
        low = at * HEAD_DIM // 128 * 128
        high = min(-(-end * HEAD_DIM // 128) * 128, shard)
        groups.append((tuple(range(at, end)), low, high))
        at = end
    return groups


def attention_kernel(heads, shard, cell, meta, projected, context, attend):
    context[...] = jnp.zeros_like(context)
    masks = head_masks(cell, heads, shard)
    scale = 1.0 / math.sqrt(HEAD_DIM)
    row = lax.broadcasted_iota(jnp.int32, (cell, 2 * cell), 0)
    lane = lax.broadcasted_iota(jnp.int32, (cell, 2 * cell), 1)
    left = lane < cell
    causal = row >= jnp.where(left, lane, lane - cell)

    def one(index):
        at = pl.multiple_of(meta[CELL_OFF + index] * TILE, TILE)
        queries = projected[pl.ds(at, cell), 0:shard]
        keys = projected[pl.ds(at, cell), shard : 2 * shard]
        values = projected[pl.ds(at, cell), 2 * shard : 3 * shard]
        total = None
        for group, low, high in head_groups(heads, shard):
            spread = spread_heads(keys, masks, group, low, high)
            scores = dot_nt(queries[:, low:high], spread) * scale
            parts = []
            for pair in range(0, len(group), 2):
                if pair + 1 < len(group):
                    both = jnp.where(causal, scores[:, pair * cell : (pair + 2) * cell], -1e30)
                    top_left = jnp.max(jnp.where(left, both, -1e30), axis=1, keepdims=True)
                    top_right = jnp.max(jnp.where(left, -1e30, both), axis=1, keepdims=True)
                    weights = jnp.exp(both - jnp.where(left, top_left, top_right))
                    sum_left = jnp.sum(jnp.where(left, weights, 0.0), axis=1, keepdims=True)
                    sum_right = jnp.sum(jnp.where(left, 0.0, weights), axis=1, keepdims=True)
                    parts.append((weights * jnp.where(left, 1.0 / sum_left, 1.0 / sum_right)).astype(LOW))
                else:
                    single = jnp.where(causal[:, :cell], scores[:, pair * cell :], -1e30)
                    weights = jnp.exp(single - jnp.max(single, axis=1, keepdims=True))
                    parts.append((weights * (1.0 / jnp.sum(weights, axis=1, keepdims=True))).astype(LOW))
            probs = jnp.concatenate(parts, axis=1) if len(parts) > 1 else parts[0]
            first = group[0] * cell
            attend[index, :, first : first + len(group) * cell] = probs
            part = dot(probs, spread_heads(values, masks, group, low, high))
            if total is None:
                total = jnp.pad(part, ((0, 0), (low, shard - high))) if high - low < shard else part
            else:
                total = total + jnp.pad(part, ((0, 0), (low, shard - high)))
        context[pl.ds(at, cell), :] = total.astype(LOW)

    def body(step, carry):
        one(2 * step)
        one(2 * step + 1)
        return carry

    lax.fori_loop(0, (meta[NCELL] + 1) // 2, body, 0)


def attention_back_kernel(heads, shard, cell, meta, projected, attend, context_grad, result, sums):
    result[...] = jnp.zeros_like(result)
    sums[...] = jnp.zeros_like(sums)
    masks = head_masks(cell, heads, shard)
    scale = 1.0 / math.sqrt(HEAD_DIM)
    row = lax.broadcasted_iota(jnp.int32, (cell, shard), 0)
    left = lax.broadcasted_iota(jnp.int32, (cell, 2 * cell), 1) < cell

    def fold(stacked, group, low, high):
        total = None
        for place, h in enumerate(group):
            part = jnp.where(masks[h][:, low:high], stacked[place * cell : (place + 1) * cell, :], 0.0)
            total = part if total is None else total + part
        return total

    def widen(part, low, high):
        return jnp.pad(part, ((0, 0), (low, shard - high))) if high - low < shard else part

    def one(index):
        at = pl.multiple_of(meta[CELL_OFF + index] * TILE, TILE)
        queries = projected[pl.ds(at, cell), 0:shard]
        keys = projected[pl.ds(at, cell), shard : 2 * shard]
        values = projected[pl.ds(at, cell), 2 * shard : 3 * shard]
        grads = context_grad[pl.ds(at, cell), :]
        grads = jnp.where(row < meta[CELL_ROWS + index], grads, jnp.zeros_like(grads))
        query_total = key_total = value_total = None
        for group, low, high in head_groups(heads, shard):
            first = group[0] * cell
            probs = attend[index, :, first : first + len(group) * cell]
            attend_grad = dot_nt(grads[:, low:high], spread_heads(values, masks, group, low, high))
            parts = []
            for pair in range(0, len(group), 2):
                if pair + 1 < len(group):
                    span = slice(pair * cell, (pair + 2) * cell)
                    weights = probs[:, span].astype(F32)
                    both = attend_grad[:, span]
                    product = weights * both
                    sum_left = jnp.sum(jnp.where(left, product, 0.0), axis=1, keepdims=True)
                    sum_right = jnp.sum(jnp.where(left, 0.0, product), axis=1, keepdims=True)
                    parts.append((product - weights * jnp.where(left, sum_left, sum_right)).astype(LOW))
                else:
                    span = slice(pair * cell, (pair + 1) * cell)
                    weights = probs[:, span].astype(F32)
                    product = weights * attend_grad[:, span]
                    total = jnp.sum(product, axis=1, keepdims=True)
                    parts.append((product - weights * total).astype(LOW))
            score_grad = jnp.concatenate(parts, axis=1) if len(parts) > 1 else parts[0]
            query_part = dot(score_grad, spread_heads(keys, masks, group, low, high)) * scale
            key_part = fold(dot_tn(score_grad, queries[:, low:high]), group, low, high) * scale
            value_part = fold(dot_tn(probs, grads[:, low:high]), group, low, high)
            query_part, key_part, value_part = (widen(p, low, high) for p in (query_part, key_part, value_part))
            if query_total is None:
                query_total, key_total, value_total = query_part, key_part, value_part
            else:
                query_total, key_total, value_total = (
                    query_total + query_part,
                    key_total + key_part,
                    value_total + value_part,
                )
        for place, part in enumerate((query_total, key_total, value_total)):
            low_part = part.astype(LOW)
            result[pl.ds(at, cell), place * shard : (place + 1) * shard] = low_part
            sums[place : place + 1, :] += jnp.sum(low_part.astype(F32), axis=0, keepdims=True)

    def body(step, carry):
        one(2 * step)
        one(2 * step + 1)
        return carry

    lax.fori_loop(0, (meta[NCELL] + 1) // 2, body, 0)


def out_project_kernel(meta, a, b, weight_a, weight_b, *parts):
    step = pl.program_id(0)

    @pl.when(step < meta[NBLK])
    def _():
        put_part(step, (dot(a[...], weight_a[...]) + dot(b[...], weight_b[...])).astype(LOW), parts)


def first_part_kernel(meta, a, b, weight_a, eighths, *refs):
    step = pl.program_id(0)
    *parts, weight_b, sems = refs

    @pl.when(step == 0)
    def _():
        load_eighths(eighths, [weight_b], sems)

    @pl.when(step < meta[NBLK])
    def _():
        put_part(step, (dot_nt(a[...], weight_a[...]) + dot_nt(b[...], weight_b[...])).astype(LOW), parts)


def gelu_pair(hidden):
    chance = 0.5 * (1.0 + lax.erf(hidden * (1.0 / math.sqrt(2.0))))
    slope = chance + hidden * (jnp.exp(-0.5 * hidden * hidden) * (1.0 / math.sqrt(2.0 * math.pi)))
    return hidden * chance, slope


def mlp_block(second, grad, up, bias, down, active, hidden_grad, bias_grad):
    hidden = dot(second, up[...]) + bias[...]
    value, slope = gelu_pair(hidden)
    low = value.astype(LOW)
    active[...] = low
    back = (slope * dot_nt(grad, down[...])).astype(LOW)
    hidden_grad[...] = back
    bias_grad[0:1, :] += jnp.sum(back.astype(F32), axis=0, keepdims=True)
    return dot(low, down[...]), dot_nt(back, up[...])


def mlp_first_kernel(
    count, meta, start, p0, p1, p2, p3, f0, f1, f2, f3, bias_row, gain, shift, a0, a1, a2, a3, up, up_bias, down,
    middle, second, grad, active, hidden_grad, branch, second_grad, bias_grad, tiles, sems, sums,
):
    step = pl.program_id(0)

    @pl.when(step == 0)
    def _():
        load_tiles((a0, a1, a2, a3), tiles, sems, count)
        bias_grad[...] = jnp.zeros_like(bias_grad)

    @pl.when(step < meta[NBLK])
    def _():
        add_parts(step, (p0, p1, p2, p3), (f0, f1, f2, f3), sums)
        inner = lax.broadcasted_iota(jnp.int32, (TILE, 1), 0)
        for j in range(BLOCK // TILE):
            at = step * (BLOCK // TILE) + j
            tile = tiles[meta[TILE_SRC + at]]
            grad[j * TILE : (j + 1) * TILE, :] = jnp.where(
                inner < meta[TILE_LEN + at], tile, jnp.zeros_like(tile)
            )
        rows = start[...] + sums[...] + bias_row[...]
        middle[...] = rows
        unit, _ = row_norm(rows)
        low = (unit * gain[...] + shift[...]).astype(LOW)
        second[...] = low
        out, back = mlp_block(low, grad[...], up, up_bias, down, active, hidden_grad, bias_grad)
        branch[...] = out.astype(LOW)
        second_grad[...] = back.astype(LOW)


def mlp_second_kernel(
    meta, second, grad, branch_in, second_grad_in, eighths, up_bias,
    active, hidden_grad, b0, b1, b2, b3, g0, g1, g2, g3, bias_grad, up, down, sems,
):
    step = pl.program_id(0)

    @pl.when(step == 0)
    def _():
        load_eighths(eighths, [up, down], sems)
        bias_grad[...] = jnp.zeros_like(bias_grad)

    @pl.when(step < meta[NBLK])
    def _():
        out, back = mlp_block(second[...], grad[...], up, up_bias, down, active, hidden_grad, bias_grad)
        put_part(step, (out + branch_in[...].astype(F32)).astype(LOW), (b0, b1, b2, b3))
        put_part(step, (back + second_grad_in[...].astype(F32)).astype(LOW), (g0, g1, g2, g3))


def weight_grad_kernel(pairs, meta, *refs):
    step = pl.program_id(0)
    result, total = refs[2 * pairs :]

    @pl.when(step == 0)
    def _():
        total[...] = jnp.zeros_like(total)

    @pl.when(step < meta[NBLK])
    def _():
        base = 0
        for a, b in zip(refs[: 2 * pairs : 2], refs[1 : 2 * pairs : 2]):
            count = a.shape[1]
            total[base : base + count, :] += dot_tn(a[...], b[...])
            base += count

    @pl.when(step == pl.num_programs(0) - 1)
    def _():
        result[...] = total[...].astype(LOW)


def middle_back_kernel(
    meta, p0, p1, p2, p3, f0, f1, f2, f3, middle, grad, gain, out_a, out_b,
    middle_grad, attn_grad, context_a, context_b, sums, added,
):
    step = pl.program_id(0)

    @pl.when(step == 0)
    def _():
        sums[...] = jnp.zeros_like(sums)

    @pl.when(step < meta[NBLK])
    def _():
        add_parts(step, (p0, p1, p2, p3), (f0, f1, f2, f3), added)
        unit, scale = row_norm(middle[...])
        second_grad = added[...]
        grad_rows = grad[...].astype(F32)
        total = grad_rows + norm_back(second_grad, unit, scale, gain[...])
        middle_grad[...] = total
        low = total.astype(LOW)
        attn_grad[...] = low
        context_a[...] = dot_nt(low, out_a[...]).astype(LOW)
        context_b[...] = dot_nt(low, out_b[...]).astype(LOW)
        for at, rows in enumerate((second_grad * unit, second_grad, total, grad_rows)):
            sums[at : at + 1, :] += jnp.sum(rows, axis=0, keepdims=True)


def scatter_tiles(meta, step, rows, out):
    for j in range(BLOCK // TILE):
        place = meta[TILE_DST + step * (BLOCK // TILE) + j]

        @pl.when(place >= 0)
        def _():
            out[place] = rows[j * TILE : (j + 1) * TILE, :].astype(LOW)


def start_back_kernel(
    meta, p0, p1, p2, p3, f0, f1, f2, f3, start, middle_grad, gain, out, sums, table, rows, added,
):
    step = pl.program_id(0)

    @pl.when(step == 0)
    def _():
        out[...] = jnp.zeros_like(out)
        sums[...] = jnp.zeros_like(sums)
        table[...] = jnp.zeros_like(table)

    @pl.when(step < meta[NBLK])
    def _():
        add_parts(step, (p0, p1, p2, p3), (f0, f1, f2, f3), added)
        unit, scale = row_norm(start[...])
        first_grad = added[...]
        rows[...] = middle_grad[...] + norm_back(first_grad, unit, scale, gain[...])
        for at, value in enumerate((first_grad * unit, first_grad)):
            sums[at : at + 1, :] += jnp.sum(value, axis=0, keepdims=True)
        for j in range(BLOCK // TILE):
            at = meta[TILE_SET + step * (BLOCK // TILE) + j]
            table[pl.ds(at, 1), :] += jnp.sum(rows[j * TILE : (j + 1) * TILE, :], axis=0, keepdims=True)
        scatter_tiles(meta, step, rows, out)


def finish_kernel(meta, middle, p0, p1, p2, p3, f0, f1, f2, f3, bias_row, out, rows):
    step = pl.program_id(0)

    @pl.when(step == 0)
    def _():
        out[...] = jnp.zeros_like(out)

    @pl.when(step < meta[NBLK])
    def _():
        add_parts(step, (p0, p1, p2, p3), (f0, f1, f2, f3), rows)
        rows[...] += middle[...] + bias_row[...]
        inner = lax.broadcasted_iota(jnp.int32, (TILE, 1), 0)
        for j in range(BLOCK // TILE):
            at = step * (BLOCK // TILE) + j
            place = meta[TILE_DST + at]

            @pl.when(place >= 0)
            def _():
                out[place] = jnp.where(
                    inner < meta[TILE_LEN + at], rows[j * TILE : (j + 1) * TILE, :], 0.0
                ).astype(LOW)


def window_size(half):
    return -(-half // (4 * TILE)) * TILE


def window_at(quarter, half):
    size = window_size(half)
    return pl.multiple_of(jnp.minimum(quarter * size, half - size), TILE)


def assemble_kernel(half, meta, p0, p1, p2, p3, out, sems):
    size = window_size(half)
    extra = 4 * size - half

    def each(act):
        for other, piece in enumerate((p0, p1, p2, p3)):
            quarter = meta[QUARTER] ^ other

            @pl.when(quarter < 3)
            def _():
                at = window_at(jnp.minimum(quarter, 2), half)
                act(pltpu.make_async_copy(piece, out.at[pl.ds(at, size)], sems.at[other]))

            @pl.when(quarter == 3)
            def _():
                rest = size - extra
                act(pltpu.make_async_copy(piece.at[pl.ds(extra, rest)], out.at[pl.ds(half - rest, rest)], sems.at[other]))

    each(lambda copy: copy.start())
    each(lambda copy: copy.wait())


def assemble(meta, pieces, half):
    width = pieces[0].shape[1]
    (result,) = call(
        functools.partial(assemble_kernel, half), meta, pieces, [ANYWHERE] * 4,
        (jax.ShapeDtypeStruct((half, width), LOW),), (whole((half, width)),),
        (1,), [pltpu.SemaphoreType.DMA((4,))], 3, "assemble",
    )
    return result


def gather_eighths(piece):
    groups = lax.axis_size("dp")
    spans = [list(range(at, at + 8)) for at in range(0, groups, 8)] if groups > 8 else None
    tiled = piece.reshape(piece.shape[0] // TILE, TILE, piece.shape[1])
    whole_block = lax.all_gather(tiled, "dp", axis=0, tiled=True, axis_index_groups=spans)
    return whole_block.reshape(8 * piece.shape[0], piece.shape[1])


def load_eighths(gathered, scratches, sems):
    copies = []
    for at, scratch in enumerate(scratches):
        half = scratch.shape[0] // 2
        size = window_size(half)
        extra = 4 * size - half
        for group in range(8):
            quarter = (group >> 1) & 3
            skip = extra if quarter == 3 else 0
            begin = (group & 1) * half + min(quarter * size, half - size) + skip
            copies.append(
                pltpu.make_async_copy(
                    gathered.at[pl.ds((group * len(scratches) + at) * size + skip, size - skip)],
                    scratch.at[pl.ds(begin, size - skip)],
                    sems.at[8 * at + group],
                )
            )
    for copy in copies:
        copy.start()
    for copy in copies:
        copy.wait()


def first_sum_kernel(meta, own, far, sent):
    sent[...] = (own[...].astype(F32) + far[...].astype(F32)).astype(LOW)


def first_sum(meta, own, far):
    rows, width = own.shape
    half = rows // 2
    steps = 5 if half % (5 * TILE) == 0 else 4
    block = half // steps
    source = pl.BlockSpec((block, width), lambda i, meta: ((1 - meta[HALF]) * steps + i, 0))
    (sent,) = call(
        first_sum_kernel, meta, (own, far), [source, source], (jax.ShapeDtypeStruct((half, width), LOW),),
        (pl.BlockSpec((block, width), lambda i, meta: (i, 0)),), (steps,), cost=5, name="first_sum",
    )
    return sent


def second_sum_kernel(half, meta, mine, far, arrived, own, s1, s2, s3):
    size = window_size(half)
    for other, out in enumerate((own, s1, s2, s3)):
        at = window_at(meta[QUARTER] ^ other, half)
        rows = pl.ds(at, size)
        total = mine[rows, :].astype(F32) + far[rows, :].astype(F32) + arrived[rows, :].astype(F32)
        out[...] = total.astype(out.dtype)


def second_sum(meta, own, far, arrived):
    half, width = arrived.shape
    size = window_size(half)
    outs = tuple(jax.ShapeDtypeStruct((size, width), kind) for kind in (F32, LOW, LOW, LOW))
    kept = pl.BlockSpec((half, width), lambda i, meta: (meta[HALF], 0), pipeline_mode=pl.Buffered(1))
    return call(
        functools.partial(second_sum_kernel, half), meta, (own, far, arrived), [kept, kept, whole((half, width))],
        outs, (whole((size, width)),) * 4, (1,), cost=4, name="second_sum",
    )


def third_sum_kernel(meta, own, r1, r2, r3, out):
    out[...] = (own[...] + r1[...].astype(F32) + r2[...].astype(F32) + r3[...].astype(F32)).astype(LOW)


def third_sum(meta, own, arrived):
    shape = own.shape
    (result,) = call(
        third_sum_kernel, meta, (own, *arrived), [whole(shape)] * 4,
        (jax.ShapeDtypeStruct(shape, LOW),), (whole(shape),), (1,), (), 3, "third_sum",
    )
    return result


def widen_kernel(parts, meta, mine, far, out):
    share = mine.shape[1] // parts
    for at in range(parts):
        lanes = slice(at * share, (at + 1) * share)
        out[at, meta[HALF]] = mine[:, lanes].astype(F32)
        out[at, 1 - meta[HALF]] = far[:, lanes].astype(F32)


def widen_halves(meta, mine, far, parts):
    half, width = mine.shape
    steps = 5
    block = half // steps
    share = width // parts
    spec = pl.BlockSpec((block, width), lambda i, meta: (i, 0))
    (result,) = call(
        functools.partial(widen_kernel, parts), meta, (mine, far), [spec, spec],
        (jax.ShapeDtypeStruct((parts, 2, half, share), F32),),
        (pl.BlockSpec((parts, 2, block, share), lambda i, meta: (0, 0, i, 0)),),
        (steps,), cost=6, name="widen",
    )
    return result.reshape(parts, 2 * half, share)


def widen_eighths_kernel(meta, gathered, *outs):
    size = gathered.shape[0] // 8
    half = -(-sum(out.shape[0] for out in outs) // (2 * TILE)) * TILE
    for group in range(8):
        quarter = group >> 1
        skip = 4 * size - half if quarter == 3 else 0
        begin = (group & 1) * half + min(quarter * size, half - size) + skip
        base = 0
        for out in outs:
            low, high = max(begin, base), min(begin + size - skip, base + out.shape[0])
            if low < high:
                at = group * size + skip + low - begin
                out[low - base : high - base, :] = gathered[at : at + high - low, :].astype(F32)
            base += out.shape[0]


def widen_eighths(meta, gathered, rows):
    width = gathered.shape[1]
    return call(
        widen_eighths_kernel, meta, (gathered,), [whole(gathered.shape)],
        tuple(jax.ShapeDtypeStruct((count, width), F32) for count in rows),
        tuple(whole((count, width)) for count in rows), (1,), cost=5, name="widen_eighths",
    )


class Reduction:
    def __init__(self, meta, other):
        self.meta = meta
        self.far = swap(other, "tp", 2)

    def arrive(self, order):
        (self.far,) = order.step(self.far)

    def first(self, order, own):
        self.own, self.far = order.then(own, self.far)
        sent = first_sum(self.meta, self.own, self.far)
        order.done(sent)
        self.arrived = swap(sent, "dp", 1)

    def second(self, order):
        (arrived,) = order.then(self.arrived)
        self.half = arrived.shape[0]
        self.own, *sent = second_sum(self.meta, self.own, self.far, arrived)
        order.done(self.own)
        self.parts = [swap(part, "dp", 2 * (at + 1)) for at, part in enumerate(sent)]

    def third(self, order, spread):
        own, *parts = order.then(self.own, *self.parts)
        piece = third_sum(self.meta, own, parts)
        level = 3
        while (1 << level) < lax.axis_size("dp"):
            piece = (piece.astype(F32) + swap(piece, "dp", 1 << level).astype(F32)).astype(LOW)
            level += 1
        order.done(piece)
        if spread:
            self.spread = Spread(self.meta, piece, self.half)
        else:
            self.gathered = gather_eighths(piece)

    def fourth(self, order):
        self.spread.join(order)

    def last_halves(self, order, parts):
        mine, far = order.then(*self.spread.halves())
        result = widen_halves(self.meta, mine, far, parts)
        order.done(result)
        return result

    def last_eighths(self, order, rows):
        (gathered,) = order.then(self.gathered)
        results = widen_eighths(self.meta, gathered, rows)
        order.done(results[0])
        return results


class Spread:
    def __init__(self, meta, piece, half):
        self.meta, self.half = meta, half
        self.pieces = [piece] + [swap(piece, "dp", 2 * other) for other in (1, 2, 3)]

    def join(self, order):
        pieces = order.then(*self.pieces)
        self.mine = assemble(self.meta, pieces, self.half)
        order.done(self.mine)
        self.far = swap(self.mine, "dp", 1)

    def halves(self):
        return self.mine, self.far


def eighth(block):
    half = block.shape[0] // 2
    index = lax.axis_index("dp")
    size = window_size(half)
    at = (index & 1) * half + jnp.minimum(((index >> 1) & 3) * size, half - size)
    return lax.dynamic_slice_in_dim(block, at, size, 0)


def on_device(
    cell_inputs,
    out_grad,
    lengths,
    datasets,
    norm_gain,
    norm_bias,
    qkv_weight,
    qv_bias,
    out_weight,
    out_bias,
    up_weight,
    up_bias,
    down_weight,
    dataset_table,
):
    slots, quarter, width = cell_inputs.shape
    tensor = lax.axis_index("tp")
    chip = tensor // 2
    core = tensor % 2
    blocks_per_cell = lax.axis_size("tp")
    cell = quarter * blocks_per_cell
    shard = qkv_weight.shape[2]
    ff = up_weight.shape[1]
    heads = shard // HEAD_DIM
    kept = (slots - slots // 16) // 2
    tile_cap = 128
    cap = tile_cap * TILE
    grid = (cap // BLOCK,)

    def mine_of(rows):
        pairs = rows.reshape(slots // 2, 2, *rows.shape[1:])[:kept]
        mine = lax.dynamic_index_in_dim(pairs, chip, 1, keepdims=False)
        theirs = lax.dynamic_index_in_dim(pairs, 1 - chip, 1, keepdims=False)
        return mine, theirs

    def send_cells(pair):
        pair = pair.reshape(2, kept, quarter, width)
        mine = lax.dynamic_index_in_dim(pair, chip, 0, keepdims=False)
        theirs = lax.dynamic_index_in_dim(pair, 1 - chip, 0, keepdims=False)
        return mine, swap(theirs, "tp", 2)

    def place_cells(mine, other):
        even = jnp.where(chip == 0, mine, other)
        odd = jnp.where(chip == 0, other, mine)
        both = jnp.stack([even, odd], axis=1).reshape(2 * kept, quarter, width)
        return jnp.pad(both, ((0, slots - 2 * kept), (0, 0), (0, 0)))

    cell_lengths, _ = mine_of(lengths)
    cell_sets, _ = mine_of(datasets)
    cell_tiles = (cell_lengths + TILE - 1) // TILE
    index = jnp.arange(kept, dtype=jnp.int32)
    ends = jnp.sum(jnp.where(index[None, :] <= index[:, None], cell_tiles[None, :], 0), axis=1)
    begins = ends - cell_tiles
    tile_count = ends[-1]
    tile = jnp.arange(tile_cap, dtype=jnp.int32)
    owner = jnp.sum((ends[None, :] <= tile[:, None]).astype(jnp.int32), axis=1)
    live = tile < tile_count
    owned = (owner[:, None] == index[None, :]) & live[:, None]

    def of_owner(values):
        return jnp.sum(jnp.where(owned, values[None, :], 0), axis=1)

    block = tile - of_owner(begins)
    tile_src = jnp.where(live, (block ^ tensor) * kept + owner, 0)
    tile_set = of_owner(cell_sets)
    tile_len = jnp.clip(of_owner(cell_lengths) - block * TILE, 0, TILE) * live
    tile_dst = jnp.where(live & (block % 2 == core), block // 2 * kept + owner, -1)
    cell_count = jnp.sum((cell_lengths > 0).astype(jnp.int32))
    block_count = (tile_count + BLOCK // TILE - 1) // (BLOCK // TILE)
    group = lax.axis_index("dp")
    head = jnp.stack([block_count, cell_count, group & 1, (group >> 1) & 3])

    def widen(values):
        return jnp.pad(values, (0, 32 - kept))

    meta = jnp.concatenate(
        [head, jnp.zeros((4,), jnp.int32), tile_src, tile_set, tile_len, tile_dst, widen(begins), widen(cell_tiles * TILE)]
    ).astype(jnp.int32)

    order = Sequence()
    qkv_own = qkv_weight.reshape(width, 3 * shard)
    vectors = jnp.concatenate([qv_bias.reshape(-1), up_bias])
    in_mine, in_theirs = mine_of(cell_inputs)
    in_other = swap(in_theirs, "tp", 2)
    in_far = swap(in_mine, "tp", 1)
    qkv_piece, mlp_piece, _ = lax.optimization_barrier(
        (eighth(qkv_own), jnp.concatenate([eighth(up_weight), eighth(down_weight)], axis=0), in_theirs)
    )
    qkv_piece = swap(qkv_piece, "tp", 2)
    mlp_piece = swap(mlp_piece, "tp", 2)
    order.step(qkv_own, meta)
    in_far, in_other = order.step(in_far, in_other)
    in_tiles = (in_mine, in_far, in_other, swap(in_other, "tp", 1))
    (qkv_piece,) = order.step(qkv_piece)
    qkv_other = gather_eighths(qkv_piece)

    def biases(vector):
        zeros = jnp.zeros((shard,), LOW)
        qkv_row = jnp.concatenate([vector[:shard], zeros, vector[shard : 2 * shard]])
        return qkv_row.astype(F32)[None], vector[2 * shard :].astype(F32)[None]

    qkv_bias_own, up_bias_own = biases(vectors)
    gains = norm_gain.astype(F32)
    shifts = norm_bias.astype(F32)
    out_rows = out_bias.astype(F32)
    table = dataset_table.astype(F32)

    def shape(rows, cols, kind=LOW):
        return jax.ShapeDtypeStruct((rows, cols), kind)

    row_f32, row_low = shape(cap, width, F32), shape(cap, width)
    row_scratch = pltpu.VMEM((BLOCK, width), F32)
    tile_scratch = [pltpu.VMEM((4 * kept, TILE, width), LOW), pltpu.SemaphoreType.DMA((4,))]

    in_tiles = order.then(*in_tiles)
    start, normed, proj_own = call(
        functools.partial(begin_kernel, kept), meta,
        (*in_tiles, table, gains[0:1], shifts[0:1], qkv_own, qkv_bias_own),
        [ANYWHERE] * 4 + [whole(table.shape), whole((1, width)), whole((1, width)), whole((width, 3 * shard)), whole((1, 3 * shard))],
        (row_f32, row_low, shape(cap, 3 * shard)),
        (rows_out(width), rows_out(width), rows_out(3 * shard)),
        grid, tile_scratch, 15, "begin",
    )
    order.done(proj_own)

    def attend_shard(projected):
        (projected,) = order.then(projected)
        context, attend = call(
            functools.partial(attention_kernel, heads, shard, cell), meta, (projected,),
            [whole((cap, 3 * shard))],
            (shape(cap, shard), jax.ShapeDtypeStruct((kept, cell, heads * cell), LOW)),
            (whole((cap, shard)), whole((kept, cell, heads * cell))),
            (1,), (), 24, "attend",
        )
        order.done(context)
        return context, attend

    (mlp_piece,) = order.step(mlp_piece)
    mlp_other = gather_eighths(mlp_piece)
    head_rows = jnp.pad(vectors, (0, 2 * width - vectors.shape[0])).reshape(2, width)
    out_and_vectors = jnp.concatenate([out_weight, head_rows, jnp.zeros((6, width), LOW)], axis=0)
    out_and_vectors = swap(order.then(out_and_vectors)[0], "tp", 2)
    context_own, attend_own = attend_shard(proj_own)
    (out_and_vectors,) = order.step(out_and_vectors)
    out_other = out_and_vectors[:shard]
    vectors_other = out_and_vectors[shard : shard + 2].reshape(-1)[: vectors.shape[0]]
    grad_mine, grad_theirs = mine_of(order.then(out_grad)[0])
    grad_other = swap(grad_theirs, "tp", 2)
    grad_far = swap(grad_mine, "tp", 1)
    normed_now, qkv_now = order.then(normed, qkv_other)
    qkv_bias_other, up_bias_other = biases(vectors_other)
    (proj_other,) = call(
        project_kernel, meta, (normed_now, qkv_now, qkv_bias_other),
        [rows_spec(width), ANYWHERE, whole((1, 3 * shard))],
        (shape(cap, 3 * shard),), (rows_out(3 * shard),),
        grid, [pltpu.VMEM((width, 3 * shard), LOW), pltpu.SemaphoreType.DMA((8,))],
        11, "project",
    )
    order.done(proj_other)
    context_other, attend_other = attend_shard(proj_other)
    (grad_other,) = order.step(grad_other)
    grad_tiles = (grad_mine, grad_far, grad_other, swap(grad_other, "tp", 1))
    (context_now,) = order.then(context_other)
    attn_part = call(
        out_project_kernel, meta, (context_own, context_now, out_weight, out_other),
        [rows_spec(shard), rows_spec(shard), whole((shard, width)), whole((shard, width))],
        part_shapes(cap, width), part_outs(width),
        grid, (), 10, "out_project",
    )
    order.done(*attn_part)
    attn_far = swap_cores(attn_part)

    mlp_outs = (shape(cap, ff), shape(cap, ff), row_low, row_low, shape(8, ff, F32))
    mlp_out_specs = (rows_out(ff), rows_out(ff), rows_out(width), rows_out(width), whole((8, ff)))
    start_now, *attn_far = order.then(start, *attn_far)
    middle, second, grad_low, active_own, hidden_own, branch_own, second_grad_own, up_vec_own = call(
        functools.partial(mlp_first_kernel, kept), meta,
        (start_now, *attn_part, *attn_far, out_rows[0:1], gains[1:2], shifts[1:2], *grad_tiles, up_weight, up_bias_own, down_weight),
        [rows_spec(width)] + part_specs(width) * 2 + [whole((1, width))] * 3 + [ANYWHERE] * 4 + [whole((width, ff)), whole((1, ff)), whole((ff, width))],
        (row_f32, row_low, row_low, *mlp_outs),
        (rows_out(width), rows_out(width), rows_out(width), *mlp_out_specs),
        grid, tile_scratch + [row_scratch], 36, "mlp_first",
    )
    order.done(branch_own)
    second_now, mlp_now = order.then(second, mlp_other)
    active_other, hidden_other, *parts, up_vec_other = call(
        mlp_second_kernel, meta,
        (second_now, grad_low, branch_own, second_grad_own, mlp_now, up_bias_other),
        [rows_spec(width)] * 4 + [ANYWHERE, whole((1, ff))],
        (*mlp_outs[:2], *part_shapes(cap, width), *part_shapes(cap, width), mlp_outs[-1]),
        (*mlp_out_specs[:2], *part_outs(width), *part_outs(width), mlp_out_specs[-1]),
        grid, [pltpu.VMEM((width, ff), LOW), pltpu.VMEM((ff, width), LOW), pltpu.SemaphoreType.DMA((16,))],
        30, "mlp_second",
    )
    branch, second_grad = parts[:CHUNKS], parts[CHUNKS:]
    order.done(*second_grad)
    second_grad_far = swap_cores(second_grad)

    def weight_grad(*operands, rows=None):
        operands = order.then(*operands)
        pairs = len(operands) // 2
        cols = operands[1].shape[1]
        rows = rows or operands[0].shape[1]
        (result,) = call(
            functools.partial(weight_grad_kernel, pairs), meta, operands,
            [rows_spec(operand.shape[1]) for operand in operands],
            (shape(rows, cols),), (whole((rows, cols)),),
            grid, [pltpu.VMEM((rows, cols), F32)], cost=11, name="weight_grad",
        )
        order.done(result)
        return result

    down_sum = Reduction(meta, weight_grad(active_other, grad_low))

    pair_shape = jax.ShapeDtypeStruct((2 * kept, TILE, width), LOW)
    pair_spec = whole((2 * kept, TILE, width))

    second_grad_far = order.then(*second_grad_far)
    middle_grad, attn_grad, context_grad_own, context_grad_other, second_sums = call(
        middle_back_kernel, meta,
        (*second_grad, *second_grad_far, middle, grad_low, gains[1:2], out_weight, out_other),
        part_specs(width) * 2 + [rows_spec(width)] * 2 + [whole((1, width)), whole((shard, width)), whole((shard, width))],
        (row_f32, row_low, shape(cap, shard), shape(cap, shard), shape(8, width, F32)),
        (rows_out(width), rows_out(width), rows_out(shard), rows_out(shard), whole((8, width))),
        grid, [row_scratch], 18, "middle_back",
    )
    order.done(context_grad_other)

    def attend_back(projected, attend, context_grad):
        projected, attend, context_grad = order.then(projected, attend, context_grad)
        grads, sums = call(
            functools.partial(attention_back_kernel, heads, shard, cell), meta,
            (projected, attend, context_grad),
            [whole((cap, 3 * shard)), whole((kept, cell, heads * cell)), whole((cap, shard))],
            (shape(cap, 3 * shard), shape(8, shard, F32)), (whole((cap, 3 * shard)), whole((8, shard))),
            (1,), (), 30, "attend_back",
        )
        order.done(grads)
        return grads, sums

    rows_both = -(-(width + shard) // (2 * TILE)) * 2 * TILE

    def up_and_out(hidden, context):
        return weight_grad(second, hidden, context, attn_grad, rows=rows_both)

    both_sum = Reduction(meta, up_and_out(hidden_other, context_other))
    down_sum.first(order, weight_grad(active_own, grad_low))
    proj_grad_other, qkv_vec_other = attend_back(proj_other, attend_other, context_grad_other)
    down_sum.second(order)
    qkv_sum = Reduction(meta, weight_grad(normed, proj_grad_other))
    both_own = up_and_out(hidden_own, context_own)
    down_sum.third(order, False)
    both_sum.first(order, both_own)
    proj_grad_own, qkv_vec_own = attend_back(proj_own, attend_own, context_grad_own)
    (first_grads,) = order.then(proj_grad_own)
    first_part = call(
        first_part_kernel, meta,
        (first_grads, proj_grad_other, qkv_own, qkv_other),
        [rows_spec(3 * shard)] * 2 + [whole((width, 3 * shard)), ANYWHERE],
        part_shapes(cap, width), part_outs(width),
        grid, [pltpu.VMEM((width, 3 * shard), LOW), pltpu.SemaphoreType.DMA((8,))],
        15, "first_part",
    )
    order.done(*first_part)
    first_far = swap_cores(first_part)
    both_sum.second(order)
    qkv_own_grad = weight_grad(normed, proj_grad_own)
    qkv_sum.first(order, qkv_own_grad)
    first_far = order.then(*first_far)
    input_pair, first_sums, table_grad = call(
        start_back_kernel, meta, (*first_part, *first_far, start, middle_grad, gains[0:1]),
        part_specs(width) * 2 + [rows_spec(width)] * 2 + [whole((1, width))],
        (pair_shape, shape(8, width, F32), shape(table.shape[0], width, F32)),
        (pair_spec, whole((8, width)), whole(table.shape)),
        grid, [row_scratch, row_scratch], 14, "start_back",
    )
    order.done(input_pair)
    input_keep, input_far = send_cells(input_pair)
    branch_far = swap_cores(order.then(*branch))
    shared = jnp.concatenate(
        [first_sums[0:1], second_sums[0:1], first_sums[1:2], second_sums[1:4], table_grad]
    )

    def vector_rows(qkv_vec, up_vec):
        row = jnp.concatenate([qkv_vec[0], qkv_vec[2], jnp.zeros((width - 2 * shard,), F32)])
        return jnp.stack([row, up_vec[0]])

    small = jnp.concatenate([shared, vector_rows(qkv_vec_own, up_vec_own)])
    small_other = jnp.concatenate([shared, vector_rows(qkv_vec_other, up_vec_other)])
    small_far = swap(small_other, "tp", 2)
    middle_now, *branch_far = order.then(middle, *branch_far)
    (output_pair,) = call(
        finish_kernel, meta, (middle_now, *branch, *branch_far, out_rows[1:2]),
        [rows_spec(width)] + part_specs(width) * 2 + [whole((1, width))],
        (pair_shape,), (pair_spec,),
        grid, [row_scratch], 9, "finish",
    )
    order.done(output_pair)
    (small_far,) = order.step(small_far)
    small = small + small_far
    small_far = swap(small, "dp", 1)
    qkv_sum.second(order)
    both_sum.third(order, False)
    output_keep, output_far = send_cells(output_pair)
    (down_total,) = down_sum.last_eighths(order, (width,))
    (small_far,) = order.step(small_far)
    small = small + small_far
    small_far = swap(small, "dp", 2)
    qkv_sum.third(order, True)
    (small_far,) = order.step(small_far)
    small = small + small_far
    small_far = swap(small, "dp", 4)
    input_far, output_far = order.step(input_far, output_far)
    input_grad = place_cells(input_keep, input_far)
    cell_outputs = place_cells(output_keep, output_far)
    qkv_sum.fourth(order)
    small = small + small_far
    level = 3
    while (1 << level) < lax.axis_size("dp"):
        small = small + swap(small, "dp", 1 << level)
        level += 1
    up_total, out_total = both_sum.last_eighths(order, (width, shard))
    qkv_total = qkv_sum.last_halves(order, 3)

    return (
        cell_outputs,
        input_grad,
        small[0:2],
        small[2:4],
        qkv_total.transpose(1, 0, 2),
        small[-2, : 2 * shard].reshape(2, shard),
        out_total,
        small[4:6],
        up_total,
        small[-1],
        down_total,
        small[6:-2],
    )


def solution(mesh):
    in_specs = (
        P("dp", "tp", None),
        P("dp", "tp", None),
        P("dp"),
        P("dp"),
        P(),
        P(),
        P(None, None, "tp"),
        P(None, "tp"),
        P("tp", None),
        P(),
        P(None, "tp"),
        P("tp"),
        P("tp", None),
        P(),
    )
    out_specs = (
        P("dp", "tp", None),
        P("dp", "tp", None),
        P(),
        P(),
        P(None, None, "tp"),
        P(None, "tp"),
        P("tp", None),
        P(),
        P(None, "tp"),
        P("tp"),
        P("tp", None),
        P(),
    )
    return jax.shard_map(
        on_device, mesh=mesh, in_specs=in_specs, out_specs=out_specs, check_vma=False
    )
```

```python
import functools
import math

import jax
import jax.numpy as jnp
from jax import lax
from jax.experimental import pallas as pl
from jax.experimental.pallas import tpu as pltpu
from jax.sharding import PartitionSpec as P

HEAD_DIM = 56
EPSILON = 1e-05
BLOCK = 256
META_BLOCKS = 8
TILE = 16
F32 = jnp.float32
LOW = jnp.bfloat16
VMEM_BYTES = 56 * 1024 * 1024
FLOPS_PER_US = 450000000

NBLK, NCELL, BITS, TILE_SRC, TILE_SET, TILE_LEN, TILE_DST, CELL_OFF, CELL_ROWS = 0, 1, 2, 8, 136, 264, 392, 520, 552


def swap(value, axis, bit):
    count = lax.axis_size(axis)
    if value.ndim == 2 and value.shape[0] % TILE == 0:
        chunk = TILE if value.shape[0] // TILE % 128 else 2 * TILE
        tiled = value.reshape(value.shape[0] // chunk, chunk, value.shape[1])
        return swap(tiled, axis, bit).reshape(value.shape)
    return lax.ppermute(value, axis, [(i, i ^ bit) for i in range(count)])


CHUNKS = 2


def swap_cores(parts):
    return tuple(swap(part, "tp", 1) for part in parts)


class Sequence:
    def __init__(self):
        self.last = ()

    def then(self, *values):
        if not self.last:
            return values
        return lax.optimization_barrier((*values, *self.last))[: len(values)]

    def done(self, *values):
        self.last = (values[-1],)

    def step(self, *values):
        values = self.then(*values)
        self.last = (values[-1],)
        return values


def dot(a, b):
    return jnp.dot(a, b, preferred_element_type=F32)


def dot_nt(a, b):
    return lax.dot_general(a, b, (((1,), (1,)), ((), ())), preferred_element_type=F32)


def dot_tn(a, b):
    return lax.dot_general(a, b, (((0,), (0,)), ((), ())), preferred_element_type=F32)


def row_norm(rows):
    center = rows - jnp.mean(rows, axis=-1, keepdims=True)
    spread = jnp.mean(center * center, axis=-1, keepdims=True)
    scale = lax.rsqrt(spread + EPSILON)
    return center * scale, scale


def norm_back(grad, unit, scale, gain):
    scaled = grad * gain
    first = jnp.mean(scaled, axis=-1, keepdims=True)
    second = jnp.mean(scaled * unit, axis=-1, keepdims=True)
    return scale * (scaled - first - unit * second)


def whole(shape):
    zeros = (0,) * len(shape)
    return pl.BlockSpec(shape, lambda i, meta: zeros, pipeline_mode=pl.Buffered(1))


def rows_spec(width):
    return pl.BlockSpec((BLOCK, width), lambda i, meta: (jnp.minimum(i, meta[NBLK] - 1), 0))


PART_BLOCKS = META_BLOCKS // CHUNKS
PART_ROWS = PART_BLOCKS * BLOCK


def part_shapes(rows, width):
    return (jax.ShapeDtypeStruct((rows // CHUNKS, width), LOW),) * CHUNKS


def parts_scratch(width):
    return [pltpu.VMEM((META_BLOCKS * BLOCK, width), LOW), pltpu.SemaphoreType.DMA((CHUNKS,))]


def out_scratch(width):
    return [pltpu.VMEM((2, BLOCK, width), LOW), pltpu.SemaphoreType.DMA((2,))]


def each_part(parts, rows, sems):
    return [
        pltpu.make_async_copy(part, rows.at[pl.ds(at * PART_ROWS, PART_ROWS)], sems.at[at])
        for at, part in enumerate(parts)
    ]


def fetch_parts(step, blocks, *groups):
    for parts, rows, sems in groups:
        for at, copy in enumerate(each_part(parts, rows, sems)):

            @pl.when((step == 0) & (at * PART_BLOCKS < blocks))
            def _():
                copy.start()

    for parts, rows, sems in groups:
        for at, copy in enumerate(each_part(parts, rows, sems)):

            @pl.when(step == at * PART_BLOCKS)
            def _():
                copy.wait()


def block_of(step, rows):
    return rows[pl.ds(pl.multiple_of(step * BLOCK, BLOCK), BLOCK), :].astype(F32)


def put_part(step, last, value, parts, slots, sems):
    slot = lax.rem(step, 2)

    def copy_to(part, slot):
        begin = pl.multiple_of(lax.rem(step, PART_BLOCKS) * BLOCK, BLOCK)
        return pltpu.make_async_copy(slots.at[slot], part.at[pl.ds(begin, BLOCK)], sems.at[slot])

    @pl.when(step >= 2)
    def _():
        copy_to(parts[0], slot).wait()

    slots[slot] = value
    for at, part in enumerate(parts):

        @pl.when(step // PART_BLOCKS == at)
        def _():
            copy_to(part, slot).start()

    @pl.when(last)
    def _():
        copy_to(parts[0], slot).wait()

        @pl.when(step >= 1)
        def _():
            copy_to(parts[0], 1 - slot).wait()


def rows_out(width):
    return rows_spec(width)


def rows_more(width):
    return pl.BlockSpec((BLOCK, width), lambda i, meta: (jnp.minimum(i, meta[NBLK]), 0))


def live_step(meta):
    return pl.when(pl.program_id(0) < meta[NBLK])


ANYWHERE = pl.BlockSpec(memory_space=pl.ANY)


def call(kernel, meta, operands, in_specs, out_shape, out_specs, grid, scratch=(), cost=5, name=None):
    return pl.pallas_call(
        kernel,
        grid_spec=pltpu.PrefetchScalarGridSpec(
            num_scalar_prefetch=1,
            grid=grid,
            in_specs=in_specs,
            out_specs=out_specs,
            scratch_shapes=list(scratch),
        ),
        out_shape=out_shape,
        compiler_params=pltpu.CompilerParams(
            dimension_semantics=("arbitrary",) * len(grid), vmem_limit_bytes=VMEM_BYTES
        ),
        cost_estimate=pl.CostEstimate(flops=cost * FLOPS_PER_US, bytes_accessed=0, transcendentals=0),
        name=name,
    )(meta, *operands)


def load_tiles(sources, tiles, sems, count):
    copies = [
        pltpu.make_async_copy(source, tiles.at[pl.ds(at * count, count)], sems.at[at])
        for at, source in enumerate(sources)
    ]
    for copy in copies:
        copy.start()
    for copy in copies:
        copy.wait()


def begin_kernel(count, meta, a0, a1, a2, a3, table, gain, shift, weight, bias, start, normed, projected, tiles, sems):
    step = pl.program_id(0)

    @pl.when(step == 0)
    def _():
        load_tiles((a0, a1, a2, a3), tiles, sems, count)

    @pl.when(step < meta[NBLK])
    def _():
        for j in range(BLOCK // TILE):
            at = step * (BLOCK // TILE) + j
            tile = tiles[meta[TILE_SRC + at]].astype(F32)
            start[j * TILE : (j + 1) * TILE, :] = tile + table[pl.ds(meta[TILE_SET + at], 1), :]
        unit, _ = row_norm(start[...])
        low = (unit * gain[...] + shift[...]).astype(LOW)
        normed[...] = low
        projected[...] = (dot_nt(low, weight[...]) + bias[...]).astype(LOW)

    @pl.when(step == meta[NBLK])
    def _():
        projected[...] = jnp.zeros_like(projected)


def project_kernel(meta, normed, eighths, bias, projected, weight, sems):
    step = pl.program_id(0)

    @pl.when(step == 0)
    def _():
        load_eighths(eighths, [weight], sems)

    @pl.when(step < meta[NBLK])
    def _():
        projected[...] = (dot_nt(normed[...], weight[: bias.shape[1], :]) + bias[...]).astype(LOW)

    @pl.when(step == meta[NBLK])
    def _():
        projected[...] = jnp.zeros_like(projected)


def head_masks(cell, heads, shard):
    lane = lax.broadcasted_iota(jnp.int32, (cell, shard), 1)
    return [(lane >= h * HEAD_DIM) & (lane < (h + 1) * HEAD_DIM) for h in range(heads)]


def spread_heads(rows, masks, heads, low, high):
    part = rows[:, low:high]
    zero = jnp.zeros_like(part)
    return jnp.concatenate([jnp.where(masks[h][:, low:high], part, zero) for h in heads], axis=0)


def head_groups(heads, shard):
    groups = []
    at = 0
    while at < heads:
        end = min(at + 4, heads)
        low = at * HEAD_DIM // 128 * 128
        high = min(-(-end * HEAD_DIM // 128) * 128, shard)
        groups.append((tuple(range(at, end)), low, high))
        at = end
    return groups


def attention_kernel(heads, shard, cell, meta, projected, context, attend):
    context[...] = jnp.zeros_like(context)
    masks = head_masks(cell, heads, shard)
    scale = 1.0 / math.sqrt(HEAD_DIM)
    row = lax.broadcasted_iota(jnp.int32, (cell, 2 * cell), 0)
    lane = lax.broadcasted_iota(jnp.int32, (cell, 2 * cell), 1)
    left = lane < cell
    causal = row >= jnp.where(left, lane, lane - cell)

    def one(index):
        at = pl.multiple_of(meta[CELL_OFF + index] * TILE, TILE)
        queries = projected[pl.ds(at, cell), 0:shard]
        keys = projected[pl.ds(at, cell), shard : 2 * shard]
        values = projected[pl.ds(at, cell), 2 * shard : 3 * shard]
        total = None
        for group, low, high in head_groups(heads, shard):
            spread = spread_heads(keys, masks, group, low, high)
            scores = dot_nt(queries[:, low:high], spread) * scale
            parts = []
            for pair in range(0, len(group), 2):
                if pair + 1 < len(group):
                    both = jnp.where(causal, scores[:, pair * cell : (pair + 2) * cell], -1e30)
                    top_left = jnp.max(jnp.where(left, both, -1e30), axis=1, keepdims=True)
                    top_right = jnp.max(jnp.where(left, -1e30, both), axis=1, keepdims=True)
                    weights = jnp.exp(both - jnp.where(left, top_left, top_right))
                    sum_left = jnp.sum(jnp.where(left, weights, 0.0), axis=1, keepdims=True)
                    sum_right = jnp.sum(jnp.where(left, 0.0, weights), axis=1, keepdims=True)
                    parts.append((weights * jnp.where(left, 1.0 / sum_left, 1.0 / sum_right)).astype(LOW))
                else:
                    single = jnp.where(causal[:, :cell], scores[:, pair * cell :], -1e30)
                    weights = jnp.exp(single - jnp.max(single, axis=1, keepdims=True))
                    parts.append((weights * (1.0 / jnp.sum(weights, axis=1, keepdims=True))).astype(LOW))
            probs = jnp.concatenate(parts, axis=1) if len(parts) > 1 else parts[0]
            first = group[0] * cell
            attend[index, :, first : first + len(group) * cell] = probs
            part = dot(probs, spread_heads(values, masks, group, low, high))
            if total is None:
                total = jnp.pad(part, ((0, 0), (low, shard - high))) if high - low < shard else part
            else:
                total = total + jnp.pad(part, ((0, 0), (low, shard - high)))
        context[pl.ds(at, cell), :] = total.astype(LOW)

    def body(step, carry):
        one(2 * step)
        one(2 * step + 1)
        return carry

    lax.fori_loop(0, (meta[NCELL] + 1) // 2, body, 0)


def attention_back_kernel(heads, shard, cell, meta, projected, attend, context_grad, result, sums):
    result[...] = jnp.zeros_like(result)
    sums[...] = jnp.zeros_like(sums)
    masks = head_masks(cell, heads, shard)
    scale = 1.0 / math.sqrt(HEAD_DIM)
    row = lax.broadcasted_iota(jnp.int32, (cell, shard), 0)
    left = lax.broadcasted_iota(jnp.int32, (cell, 2 * cell), 1) < cell

    def fold(stacked, group, low, high):
        total = None
        for place, h in enumerate(group):
            part = jnp.where(masks[h][:, low:high], stacked[place * cell : (place + 1) * cell, :], 0.0)
            total = part if total is None else total + part
        return total

    def widen(part, low, high):
        return jnp.pad(part, ((0, 0), (low, shard - high))) if high - low < shard else part

    def one(index):
        at = pl.multiple_of(meta[CELL_OFF + index] * TILE, TILE)
        queries = projected[pl.ds(at, cell), 0:shard]
        keys = projected[pl.ds(at, cell), shard : 2 * shard]
        values = projected[pl.ds(at, cell), 2 * shard : 3 * shard]
        grads = context_grad[pl.ds(at, cell), :]
        grads = jnp.where(row < meta[CELL_ROWS + index], grads, jnp.zeros_like(grads))
        query_total = key_total = value_total = None
        for group, low, high in head_groups(heads, shard):
            first = group[0] * cell
            probs = attend[index, :, first : first + len(group) * cell]
            attend_grad = dot_nt(grads[:, low:high], spread_heads(values, masks, group, low, high))
            parts = []
            for pair in range(0, len(group), 2):
                if pair + 1 < len(group):
                    span = slice(pair * cell, (pair + 2) * cell)
                    weights = probs[:, span].astype(F32)
                    both = attend_grad[:, span]
                    product = weights * both
                    sum_left = jnp.sum(jnp.where(left, product, 0.0), axis=1, keepdims=True)
                    sum_right = jnp.sum(jnp.where(left, 0.0, product), axis=1, keepdims=True)
                    parts.append((product - weights * jnp.where(left, sum_left, sum_right)).astype(LOW))
                else:
                    span = slice(pair * cell, (pair + 1) * cell)
                    weights = probs[:, span].astype(F32)
                    product = weights * attend_grad[:, span]
                    total = jnp.sum(product, axis=1, keepdims=True)
                    parts.append((product - weights * total).astype(LOW))
            score_grad = jnp.concatenate(parts, axis=1) if len(parts) > 1 else parts[0]
            query_part = dot(score_grad, spread_heads(keys, masks, group, low, high)) * scale
            key_part = fold(dot_tn(score_grad, queries[:, low:high]), group, low, high) * scale
            value_part = fold(dot_tn(probs, grads[:, low:high]), group, low, high)
            query_part, key_part, value_part = (widen(p, low, high) for p in (query_part, key_part, value_part))
            if query_total is None:
                query_total, key_total, value_total = query_part, key_part, value_part
            else:
                query_total, key_total, value_total = (
                    query_total + query_part,
                    key_total + key_part,
                    value_total + value_part,
                )
        for place, part in enumerate((query_total, key_total, value_total)):
            low_part = part.astype(LOW)
            result[pl.ds(at, cell), place * shard : (place + 1) * shard] = low_part
            sums[place : place + 1, :] += jnp.sum(low_part.astype(F32), axis=0, keepdims=True)

    def body(step, carry):
        one(2 * step)
        one(2 * step + 1)
        return carry

    lax.fori_loop(0, (meta[NCELL] + 1) // 2, body, 0)


def out_project_kernel(meta, a, b, weight_a, weight_b, *refs):
    *parts, slots, sems = refs
    step = pl.program_id(0)

    @live_step(meta)
    def _():
        value = (dot(a[...], weight_a[...]) + dot(b[...], weight_b[...])).astype(LOW)
        put_part(step, step == meta[NBLK] - 1, value, parts, slots, sems)


def first_part_kernel(meta, a, b, weight_a, eighths, *refs):
    step = pl.program_id(0)
    *parts, weight_b, weight_sems, slots, sems = refs

    @pl.when(step == 0)
    def _():
        load_eighths(eighths, [weight_b], weight_sems)

    @live_step(meta)
    def _():
        value = (dot(a[...], weight_a[...]) + dot(b[...], weight_b[: b.shape[1], :])).astype(LOW)
        put_part(step, step == meta[NBLK] - 1, value, parts, slots, sems)


def gelu_pair(hidden):
    chance = 0.5 * (1.0 + lax.erf(hidden * (1.0 / math.sqrt(2.0))))
    slope = chance + hidden * (jnp.exp(-0.5 * hidden * hidden) * (1.0 / math.sqrt(2.0 * math.pi)))
    return hidden * chance, slope


def mlp_block(second, grad, up, bias, down, active, hidden_grad, bias_grad):
    hidden = dot(second, up[...]) + bias[...]
    value, slope = gelu_pair(hidden)
    low = value.astype(LOW)
    active[...] = low
    back = (slope * dot_nt(grad, down[...])).astype(LOW)
    hidden_grad[...] = back
    bias_grad[...] += jnp.sum(back.astype(F32), axis=0, keepdims=True)
    return dot(low, down[...]), dot_nt(back, up[...])


def mlp_kernel(count, meta, start, *refs):
    near_parts, far_parts, refs = refs[:CHUNKS], refs[CHUNKS : 2 * CHUNKS], refs[2 * CHUNKS :]
    bias_row, gain, shift, a0, a1, a2, a3, up, up_bias, down, other_up, other_bias, eighths, *refs = refs
    middle, second, grad, active, hidden_grad, other_active, other_hidden, *refs = refs
    branch, second_grad, refs = refs[:CHUNKS], refs[CHUNKS : 2 * CHUNKS], refs[2 * CHUNKS :]
    bias_grad, tiles, sems, near_rows, near_sems, far_rows, far_sems, *refs = refs
    other_down, other_sems, branch_slots, branch_sems, grad_slots, grad_sems = refs
    step = pl.program_id(0)
    copies = eighths_copies(eighths, [other_down], other_sems)

    @pl.when(step == 0)
    def _():
        load_tiles((a0, a1, a2, a3), tiles, sems, count)
        for copy in copies:
            copy.start()
        bias_grad[...] = jnp.zeros_like(bias_grad)

    @live_step(meta)
    def _():
        last = step == meta[NBLK] - 1
        fetch_parts(step, meta[NBLK], (near_parts, near_rows, near_sems), (far_parts, far_rows, far_sems))
        inner = lax.broadcasted_iota(jnp.int32, (TILE, 1), 0)
        for j in range(BLOCK // TILE):
            at = step * (BLOCK // TILE) + j
            tile = tiles[meta[TILE_SRC + at]]
            grad[j * TILE : (j + 1) * TILE, :] = jnp.where(inner < meta[TILE_LEN + at], tile, jnp.zeros_like(tile))
        rows = start[...] + (block_of(step, near_rows) + block_of(step, far_rows)) + bias_row[...]
        middle[...] = rows
        unit, _ = row_norm(rows)
        low = (unit * gain[...] + shift[...]).astype(LOW)
        second[...] = low
        own = mlp_block(low, grad[...], up, up_bias, down, active, hidden_grad, bias_grad.at[0:1])

        @pl.when(step == 0)
        def _():
            for copy in copies:
                copy.wait()

        other = mlp_block(
            low, grad[...], other_up, other_bias, other_down, other_active, other_hidden, bias_grad.at[1:2]
        )
        put_part(step, last, (own[1] + other[1]).astype(LOW), second_grad, grad_slots, grad_sems)
        put_part(step, last, (own[0] + other[0]).astype(LOW), branch, branch_slots, branch_sems)


def weight_grad_kernel(pairs, meta, *refs):
    step = pl.program_id(0)
    result, total = refs[2 * pairs :]

    @live_step(meta)
    def _():
        base = 0
        for a, b in zip(refs[: 2 * pairs : 2], refs[1 : 2 * pairs : 2]):
            rows = slice(base, base + a.shape[1])
            part = dot_tn(a[...], b[...])
            base += a.shape[1]

            @pl.when(step == 0)
            def _():
                total[rows, :] = part

            @pl.when(step > 0)
            def _():
                total[rows, :] += part

        @pl.when(step == meta[NBLK] - 1)
        def _():
            result[...] = total[...].astype(LOW)


def middle_back_kernel(meta, *refs):
    near_parts, far_parts, refs = refs[:CHUNKS], refs[CHUNKS : 2 * CHUNKS], refs[2 * CHUNKS :]
    middle, grad, gain, out_a, out_b, middle_grad, attn_grad, context_a, context_b, sums, *refs = refs
    near_rows, near_sems, far_rows, far_sems = refs
    step = pl.program_id(0)

    @pl.when(step == 0)
    def _():
        sums[...] = jnp.zeros_like(sums)

    @live_step(meta)
    def _():
        fetch_parts(step, meta[NBLK], (near_parts, near_rows, near_sems), (far_parts, far_rows, far_sems))
        unit, scale = row_norm(middle[...])
        second_grad = block_of(step, near_rows) + block_of(step, far_rows)
        grad_rows = grad[...].astype(F32)
        total = grad_rows + norm_back(second_grad, unit, scale, gain[...])
        middle_grad[...] = total
        low = total.astype(LOW)
        attn_grad[...] = low
        context_a[...] = dot_nt(low, out_a[...]).astype(LOW)
        context_b[...] = dot_nt(low, out_b[...]).astype(LOW)
        for at, rows in enumerate((second_grad * unit, second_grad, total, grad_rows)):
            sums[at : at + 1, :] += jnp.sum(rows, axis=0, keepdims=True)


def scatter_tiles(meta, step, rows, out):
    for j in range(BLOCK // TILE):
        place = meta[TILE_DST + step * (BLOCK // TILE) + j]

        @pl.when(place >= 0)
        def _():
            out[place] = rows[j * TILE : (j + 1) * TILE, :].astype(LOW)


def start_back_kernel(meta, *refs):
    near_parts, far_parts, refs = refs[:CHUNKS], refs[CHUNKS : 2 * CHUNKS], refs[2 * CHUNKS :]
    start, middle_grad, gain, out, sums, table, rows, near_rows, near_sems, far_rows, far_sems = refs
    step = pl.program_id(0)

    @pl.when(step == 0)
    def _():
        out[...] = jnp.zeros_like(out)
        sums[...] = jnp.zeros_like(sums)
        table[...] = jnp.zeros_like(table)

    @live_step(meta)
    def _():
        fetch_parts(step, meta[NBLK], (near_parts, near_rows, near_sems), (far_parts, far_rows, far_sems))
        unit, scale = row_norm(start[...])
        first_grad = block_of(step, near_rows) + block_of(step, far_rows)
        rows[...] = middle_grad[...] + norm_back(first_grad, unit, scale, gain[...])
        for at, value in enumerate((first_grad * unit, first_grad)):
            sums[at : at + 1, :] += jnp.sum(value, axis=0, keepdims=True)
        for j in range(BLOCK // TILE):
            at = meta[TILE_SET + step * (BLOCK // TILE) + j]
            table[pl.ds(at, 1), :] += jnp.sum(rows[j * TILE : (j + 1) * TILE, :], axis=0, keepdims=True)
        scatter_tiles(meta, step, rows, out)


def finish_kernel(meta, middle, *refs):
    near_parts, far_parts, refs = refs[:CHUNKS], refs[CHUNKS : 2 * CHUNKS], refs[2 * CHUNKS :]
    bias_row, out, rows, near_rows, near_sems, far_rows, far_sems = refs
    step = pl.program_id(0)

    @pl.when(step == 0)
    def _():
        out[...] = jnp.zeros_like(out)

    @live_step(meta)
    def _():
        fetch_parts(step, meta[NBLK], (near_parts, near_rows, near_sems), (far_parts, far_rows, far_sems))
        rows[...] = middle[...] + (block_of(step, near_rows) + block_of(step, far_rows)) + bias_row[...]
        inner = lax.broadcasted_iota(jnp.int32, (TILE, 1), 0)
        for j in range(BLOCK // TILE):
            at = step * (BLOCK // TILE) + j
            place = meta[TILE_DST + at]

            @pl.when(place >= 0)
            def _():
                out[place] = jnp.where(inner < meta[TILE_LEN + at], rows[j * TILE : (j + 1) * TILE, :], 0.0).astype(LOW)


def vectors_kernel(shard, meta, first, second, table, own, other, up, small, small_other):
    for out, qkv, at in ((small, own, 0), (small_other, other, 1)):
        out[0:1, :] = first[0:1, :]
        out[1:2, :] = second[0:1, :]
        out[2:3, :] = first[1:2, :]
        out[3:6, :] = second[1:4, :]
        out[6:38, :] = table[...]
        out[38:40, :] = jnp.zeros((2, out.shape[1]), F32)
        out[38:39, :shard] = qkv[0:1, :]
        out[38:39, shard : 2 * shard] = qkv[2:3, :]
        out[39:40, :] = up[at : at + 1, :]


def window_size(half):
    return -(-half // (4 * TILE)) * TILE


def window_at(low, high, half):
    size = window_size(half)
    return low * (half - 2 * size) + high * size


def run_copies(copies):
    for copy in copies:
        copy.start()
    for copy in copies:
        copy.wait()


def join_kernel(extra, level, meta, mine, far, out, sems):
    rows = mine.shape[0]

    def put(first, second):
        run_copies(
            [
                pltpu.make_async_copy(first, out.at[pl.ds(0, rows)], sems.at[0]),
                pltpu.make_async_copy(second.at[pl.ds(extra, rows - extra)], out.at[pl.ds(rows, rows - extra)], sems.at[1]),
            ]
        )

    @pl.when(meta[BITS + level] == 0)
    def _():
        put(mine, far)

    @pl.when(meta[BITS + level] == 1)
    def _():
        put(far, mine)


def join(meta, mine, far, level, total):
    rows, width = mine.shape
    (result,) = call(
        functools.partial(join_kernel, 2 * rows - total, level), meta, (mine, far), [ANYWHERE] * 2,
        (jax.ShapeDtypeStruct((total, width), LOW),), (whole((total, width)),),
        (1,), [pltpu.SemaphoreType.DMA((2,))], cost=3, name="join",
    )
    return result


def gather_eighths(piece):
    groups = lax.axis_size("dp")
    spans = [list(range(at, at + 8)) for at in range(0, groups, 8)] if groups > 8 else None
    tiled = piece.reshape(piece.shape[0] // TILE, TILE, piece.shape[1])
    whole_block = lax.all_gather(tiled, "dp", axis=0, tiled=True, axis_index_groups=spans)
    return whole_block.reshape(8 * piece.shape[0], piece.shape[1])


def eighths_copies(gathered, scratches, sems):
    copies = []
    for at, scratch in enumerate(scratches):
        half = scratch.shape[0] // 2
        size = window_size(half)
        for group in range(8):
            low, high = (group >> 1) & 1, group >> 2
            skip = 4 * size - half if (low, high) == (1, 0) else 0
            begin = (group & 1) * half + window_at(low, high, half) + skip
            copies.append(
                pltpu.make_async_copy(
                    gathered.at[pl.ds((group * len(scratches) + at) * size + skip, size - skip)],
                    scratch.at[pl.ds(begin, size - skip)],
                    sems.at[8 * at + group],
                )
            )
    return copies


def load_eighths(gathered, scratches, sems):
    copies = eighths_copies(gathered, scratches, sems)
    for copy in copies:
        copy.start()
    for copy in copies:
        copy.wait()


def first_sum_kernel(meta, own, far, sent):
    sent[...] = (own[...].astype(F32) + far[...].astype(F32)).astype(LOW)


def first_sum(meta, own, far):
    rows, width = own.shape
    half = rows // 2
    steps = next(count for count in (5, 4, 3, 1) if half % (count * TILE) == 0)
    block = half // steps
    source = pl.BlockSpec((block, width), lambda i, meta: ((1 - meta[BITS]) * steps + i, 0))
    (sent,) = call(
        first_sum_kernel, meta, (own, far), [source, source], (jax.ShapeDtypeStruct((half, width), LOW),),
        (pl.BlockSpec((block, width), lambda i, meta: (i, 0)),), (steps,), cost=5, name="first_sum",
    )
    return sent


def second_sum_kernel(half, meta, mine, far, arrived, kept, sent):
    size = 2 * window_size(half)
    bit = meta[BITS + 1]
    for out, place in ((kept, bit), (sent, 1 - bit)):
        rows = pl.ds(pl.multiple_of(place * (half - size), TILE), size)
        total = mine[rows, :].astype(F32) + far[rows, :].astype(F32) + arrived[rows, :].astype(F32)
        out[...] = total.astype(out.dtype)


def second_sum(meta, own, far, arrived, cost):
    half, width = arrived.shape
    size = 2 * window_size(half)
    kept = pl.BlockSpec((half, width), lambda i, meta: (meta[BITS], 0), pipeline_mode=pl.Buffered(1))
    return call(
        functools.partial(second_sum_kernel, half), meta, (own, far, arrived), [kept, kept, whole((half, width))],
        (jax.ShapeDtypeStruct((size, width), F32), jax.ShapeDtypeStruct((size, width), LOW)),
        (whole((size, width)),) * 2, (1,), cost=cost, name="second_sum",
    )


def third_sum_kernel(count, meta, *refs):
    kept, arrived, own, sent = refs[:count], refs[count], refs[count + 1 : 2 * count + 1], refs[-1]
    size = own[0].shape[0]
    bit = meta[BITS + 2]
    for at in range(count):
        for place in (bit, 1 - bit):
            begin = pl.multiple_of(place * size, TILE)
            far = arrived[pl.ds(pl.multiple_of(2 * at * size + begin, TILE), size), :].astype(F32)
            total = kept[at][pl.ds(begin, size), :] + far
            if place is bit:
                own[at][...] = total
            else:
                sent[at * size : (at + 1) * size, :] = total.astype(LOW)


def third_sum(meta, kept, arrived, cost=3):
    count = len(kept)
    size, width = kept[0].shape[0] // 2, kept[0].shape[1]
    *own, sent = call(
        functools.partial(third_sum_kernel, count), meta, (*kept, arrived),
        [whole(each.shape) for each in (*kept, arrived)],
        (jax.ShapeDtypeStruct((size, width), F32),) * count + (jax.ShapeDtypeStruct((count * size, width), LOW),),
        (whole((size, width)),) * count + (whole((count * size, width)),), (1,), cost=cost, name="third_sum",
    )
    return own, sent


def fourth_sum_kernel(count, meta, *refs):
    own, arrived, outs = refs[:count], refs[count], refs[count + 1 :]
    size = own[0].shape[0]
    for at, out in enumerate(outs):
        out[...] = (own[at][...] + arrived[at * size : (at + 1) * size, :].astype(F32)).astype(out.dtype)


def fourth_sum(meta, own, arrived, kinds):
    shape = own[0].shape
    return call(
        functools.partial(fourth_sum_kernel, len(own)), meta, (*own, arrived),
        [whole(each.shape) for each in (*own, arrived)],
        tuple(jax.ShapeDtypeStruct(shape, kind) for kind in kinds), (whole(shape),) * len(own),
        (1,), cost=3, name="fourth_sum",
    )


def widen_rows_kernel(meta, mine, far, *outs):
    half = mine.shape[0]

    def put(lower, upper):
        base = 0
        for out in outs:
            count = out.shape[0]
            split = min(max(half - base, 0), count)
            if split:
                out[:split, :] = lower[base : base + split, :].astype(F32)
            if split < count:
                begin = base + split - half
                out[split:, :] = upper[begin : begin + count - split, :].astype(F32)
            base += count

    @pl.when(meta[BITS] == 0)
    def _():
        put(mine, far)

    @pl.when(meta[BITS] == 1)
    def _():
        put(far, mine)


def widen_rows(meta, mine, far, rows):
    half, width = mine.shape
    return call(
        widen_rows_kernel, meta, (mine, far), [whole((half, width))] * 2,
        tuple(jax.ShapeDtypeStruct((count, width), F32) for count in rows),
        tuple(whole((count, width)) for count in rows), (1,), name="widen_rows",
    )


def later_groups(value):
    level = 3
    while (1 << level) < lax.axis_size("dp"):
        value = (value.astype(F32) + swap(value, "dp", 1 << level).astype(F32)).astype(value.dtype)
        level += 1
    return value


class Reduction:
    def __init__(self, meta, other):
        self.meta = meta
        self.far = swap(other, "tp", 2)

    def arrive(self, order):
        (self.far,) = order.step(self.far)

    def first(self, order, own):
        self.own, self.far = order.then(own, self.far)
        sent = first_sum(self.meta, self.own, self.far)
        order.done(sent)
        self.arrived = swap(sent, "dp", 1)

    def wait_second(self, order):
        (self.arrived,) = order.step(self.arrived)

    def second(self, order, cost=4):
        (arrived,) = order.then(self.arrived)
        self.half = arrived.shape[0]
        self.kept, sent = second_sum(self.meta, self.own, self.far, arrived, cost)
        order.done(sent)
        self.arrived = swap(sent, "dp", 2)

    def third(self, order, cost=3):
        (arrived,) = order.then(self.arrived)
        self.kept, sent = third_sum(self.meta, [self.kept], arrived, cost)
        order.done(sent)
        self.arrived = swap(sent, "dp", 4)

    def fourth(self, order):
        (arrived,) = order.then(self.arrived)
        (piece,) = fourth_sum(self.meta, self.kept, arrived, (LOW,))
        order.done(piece)
        piece = later_groups(piece)
        self.mine, self.far = piece, swap(piece, "dp", 4)

    def spread(self, order, level):
        mine, far = order.then(self.mine, self.far)
        rows = 2 * mine.shape[0] if level == 2 else self.half
        self.mine = join(self.meta, mine, far, level, rows)
        order.done(self.mine)
        self.far = swap(self.mine, "dp", 1 << (level - 1))

    def last_halves(self, order, rows):
        mine, far = order.then(self.mine, self.far)
        results = widen_rows(self.meta, mine, far, rows)
        order.done(results[0])
        return results


def eighth(block):
    half = block.shape[0] // 2
    index = lax.axis_index("dp")
    at = (index & 1) * half + window_at((index >> 1) & 1, (index >> 2) & 1, half)
    return lax.dynamic_slice_in_dim(block, at, window_size(half), 0)


def on_device(
    cell_inputs,
    out_grad,
    lengths,
    datasets,
    norm_gain,
    norm_bias,
    qkv_weight,
    qv_bias,
    out_weight,
    out_bias,
    up_weight,
    up_bias,
    down_weight,
    dataset_table,
):
    slots, quarter, width = cell_inputs.shape
    tensor = lax.axis_index("tp")
    chip = tensor // 2
    core = tensor % 2
    blocks_per_cell = lax.axis_size("tp")
    cell = quarter * blocks_per_cell
    shard = qkv_weight.shape[2]
    ff = up_weight.shape[1]
    heads = shard // HEAD_DIM
    kept = slots // 2
    tile_cap = META_BLOCKS * BLOCK // TILE
    cap = META_BLOCKS * BLOCK
    grid = (META_BLOCKS,)
    group = lax.axis_index("dp")
    index = jnp.arange(kept, dtype=jnp.int32)

    def mine_of(rows):
        pairs = rows.reshape(kept, 2, *rows.shape[1:])
        mine = lax.dynamic_index_in_dim(pairs, chip, 1, keepdims=False)
        theirs = lax.dynamic_index_in_dim(pairs, 1 - chip, 1, keepdims=False)
        return mine, theirs

    def place_cells(mine, other):
        even = jnp.where(chip == 0, mine, other)
        odd = jnp.where(chip == 0, other, mine)
        return jnp.stack([even, odd], axis=1).reshape(slots, quarter, width)

    cell_lengths, _ = mine_of(lengths)
    cell_sets, _ = mine_of(datasets)
    cell_tiles = (cell_lengths + TILE - 1) // TILE
    ends = jnp.sum(jnp.where(index[None, :] <= index[:, None], cell_tiles[None, :], 0), axis=1)
    begins = ends - cell_tiles
    tile_count = ends[-1]
    tile = jnp.arange(tile_cap, dtype=jnp.int32)
    owner = jnp.sum((ends[None, :] <= tile[:, None]).astype(jnp.int32), axis=1)
    live = tile < tile_count
    owned = (owner[:, None] == index[None, :]) & live[:, None]

    def of_owner(values):
        return jnp.sum(jnp.where(owned, values[None, :], 0), axis=1)

    block = tile - of_owner(begins)
    shelf = jnp.where(block // 2 == chip, 0, kept) + owner
    tile_src = jnp.where(live, jnp.where(block % 2 == core, 0, slots) + shelf, 0)
    tile_set = of_owner(cell_sets)
    tile_len = jnp.clip(of_owner(cell_lengths) - block * TILE, 0, TILE) * live
    tile_dst = jnp.where(live & (block % 2 == core), shelf, -1)
    cell_count = jnp.sum((cell_lengths > 0).astype(jnp.int32))
    block_count = (tile_count + BLOCK // TILE - 1) // (BLOCK // TILE)
    grid = (META_BLOCKS,)
    head = jnp.stack([block_count, cell_count, group & 1, (group >> 1) & 1, (group >> 2) & 1])

    meta = jnp.concatenate(
        [head, jnp.zeros((3,), jnp.int32), tile_src, tile_set, tile_len, tile_dst, begins, cell_tiles * TILE]
    ).astype(jnp.int32)

    order = Sequence()
    qkv_own = qkv_weight.transpose(1, 2, 0).reshape(3 * shard, width)
    qkv_rows = -(-3 * shard // (2 * TILE)) * 2 * TILE
    vectors = jnp.concatenate([qv_bias.reshape(-1), up_bias])
    piece_source, cells_now = lax.optimization_barrier(
        (eighth(jnp.pad(qkv_own, ((0, qkv_rows - 3 * shard), (0, 0)))), cell_inputs)
    )
    qkv_piece = swap(piece_source, "tp", 2)
    in_mine, in_theirs = mine_of(cells_now)
    in_other = swap(in_theirs, "tp", 2)
    in_far = swap(in_mine, "tp", 1)
    head_rows = jnp.pad(vectors, (0, 2 * width - vectors.shape[0])).reshape(2, width)
    out_and_vectors = jnp.concatenate([out_weight, head_rows, jnp.zeros((6, width), LOW)], axis=0)
    meta, qkv_own, out_and_vectors, down_piece = order.step(meta, qkv_own, out_and_vectors, eighth(down_weight))
    (qkv_piece,) = order.step(qkv_piece)
    qkv_other = gather_eighths(qkv_piece)
    in_far, in_other = order.step(in_far, in_other)
    in_other_far = swap(in_other, "tp", 1)
    down_piece, out_and_vectors = order.then(down_piece, out_and_vectors)
    down_piece = swap(down_piece, "tp", 2)
    out_and_vectors = swap(out_and_vectors, "tp", 2)
    (in_other_far,) = order.step(in_other_far)

    def biases(vector):
        zeros = jnp.zeros((shard,), LOW)
        qkv_row = jnp.concatenate([vector[:shard], zeros, vector[shard : 2 * shard]])
        return qkv_row.astype(F32)[None], vector[2 * shard :].astype(F32)[None]

    qkv_bias_own, up_bias_own = biases(vectors)
    gains = norm_gain.astype(F32)
    shifts = norm_bias.astype(F32)
    out_rows = out_bias.astype(F32)
    table = dataset_table.astype(F32)

    def shape(rows, cols, kind=LOW):
        return jax.ShapeDtypeStruct((rows, cols), kind)

    row_f32, row_low = shape(cap, width, F32), shape(cap, width)
    row_scratch = pltpu.VMEM((BLOCK, width), F32)
    tile_scratch = [pltpu.VMEM((2 * slots, TILE, width), LOW), pltpu.SemaphoreType.DMA((4,))]

    start, normed, proj_own = call(
        functools.partial(begin_kernel, kept), meta,
        (in_mine, in_other, in_far, in_other_far, table, gains[0:1], shifts[0:1], qkv_own, qkv_bias_own),
        [ANYWHERE] * 4 + [whole(table.shape), whole((1, width)), whole((1, width)), whole((3 * shard, width)), whole((1, 3 * shard))],
        (row_f32, row_low, shape(cap, 3 * shard)),
        (rows_out(width), rows_out(width), rows_more(3 * shard)),
        grid, tile_scratch, 15, "begin",
    )
    order.done(proj_own)

    def attend_shard(projected):
        (projected,) = order.then(projected)
        context, attend = call(
            functools.partial(attention_kernel, heads, shard, cell), meta, (projected,),
            [whole((cap, 3 * shard))],
            (shape(cap, shard), jax.ShapeDtypeStruct((kept, cell, heads * cell), LOW)),
            (whole((cap, shard)), whole((kept, cell, heads * cell))),
            (1,), (), 4, "attend",
        )
        order.done(context)
        return context, attend

    down_piece, out_and_vectors = order.step(down_piece, out_and_vectors)
    down_other = gather_eighths(down_piece)
    grad_mine, grad_theirs = mine_of(order.then(out_grad)[0])
    grad_other = swap(grad_theirs, "tp", 2)
    grad_far = swap(grad_mine, "tp", 1)
    context_own, attend_own = attend_shard(proj_own)
    (grad_far,) = order.step(grad_far)
    up_other = swap(order.then(up_weight)[0], "tp", 2)
    out_other = out_and_vectors[:shard]
    vectors_other = out_and_vectors[shard : shard + 2].reshape(-1)[: vectors.shape[0]]
    normed_now, qkv_now = order.then(normed, qkv_other)
    qkv_bias_other, up_bias_other = biases(vectors_other)
    (proj_other,) = call(
        project_kernel, meta, (normed_now, qkv_now, qkv_bias_other),
        [rows_spec(width), ANYWHERE, whole((1, 3 * shard))],
        (shape(cap, 3 * shard),), (rows_more(3 * shard),),
        grid, [pltpu.VMEM((qkv_rows, width), LOW), pltpu.SemaphoreType.DMA((8,))],
        6, "project",
    )
    order.done(proj_other)
    context_other, attend_other = attend_shard(proj_other)
    (grad_other,) = order.step(grad_other)
    grad_other_far = swap(grad_other, "tp", 1)
    (context_now,) = order.then(context_other)
    attn_part = call(
        out_project_kernel, meta, (context_own, context_now, out_weight, out_other),
        [rows_spec(shard), rows_spec(shard), whole((shard, width)), whole((shard, width))],
        part_shapes(cap, width), (ANYWHERE,) * CHUNKS,
        grid, out_scratch(width), 10, "out_project",
    )
    order.done(*attn_part)
    attn_far = swap_cores(attn_part)
    (grad_other_far,) = order.step(grad_other_far)

    start_now, grad_far, grad_other_far, up_other, down_other, *attn_far = order.then(
        start, grad_far, grad_other_far, up_other, down_other, *attn_far
    )
    middle, second, grad_low, active_own, hidden_own, active_other, hidden_other, *parts, up_vecs = call(
        functools.partial(mlp_kernel, kept), meta,
        (start_now, *attn_part, *attn_far, out_rows[0:1], gains[1:2], shifts[1:2], grad_mine, grad_other, grad_far, grad_other_far,
         up_weight, up_bias_own, down_weight, up_other, up_bias_other, down_other),
        [rows_spec(width)] + [ANYWHERE] * (2 * CHUNKS) + [whole((1, width))] * 3 + [ANYWHERE] * 4
        + [whole((width, ff)), whole((1, ff)), whole((ff, width)), whole((width, ff)), whole((1, ff)), ANYWHERE],
        (row_f32, row_low, row_low, *(shape(cap, ff),) * 4, *part_shapes(cap, width), *part_shapes(cap, width), shape(8, ff, F32)),
        (rows_out(width),) * 3 + (rows_out(ff),) * 4 + (ANYWHERE,) * (2 * CHUNKS) + (whole((8, ff)),),
        grid,
        tile_scratch + parts_scratch(width) * 2
        + [pltpu.VMEM((ff, width), LOW), pltpu.SemaphoreType.DMA((8,))]
        + out_scratch(width) * 2,
        65, "mlp",
    )
    branch, second_grad = parts[:CHUNKS], parts[CHUNKS:]
    order.done(*second_grad)
    second_grad_far = swap_cores(second_grad)
    branch_far = swap_cores(branch)

    def weight_grad(*operands, rows=None):
        operands = order.then(*operands)
        pairs = len(operands) // 2
        cols = operands[1].shape[1]
        rows = rows or operands[0].shape[1]
        (result,) = call(
            functools.partial(weight_grad_kernel, pairs), meta, operands,
            [rows_spec(operand.shape[1]) for operand in operands],
            (shape(rows, cols),), (whole((rows, cols)),),
            grid, [pltpu.VMEM((rows, cols), F32)], cost=13, name="weight_grad",
        )
        order.done(result)
        return result

    up_sum = Reduction(meta, weight_grad(second, hidden_other))
    down_sum = Reduction(meta, weight_grad(active_other, grad_low))

    pair_shape = jax.ShapeDtypeStruct((slots, TILE, width), LOW)
    pair_spec = whole((slots, TILE, width))

    second_grad_far = order.then(*second_grad_far)
    middle_grad, attn_grad, context_grad_own, context_grad_other, second_sums = call(
        middle_back_kernel, meta,
        (*second_grad, *second_grad_far, middle, grad_low, gains[1:2], out_weight, out_other),
        [ANYWHERE] * (2 * CHUNKS) + [rows_spec(width)] * 2 + [whole((1, width)), whole((shard, width)), whole((shard, width))],
        (row_f32, row_low, shape(cap, shard), shape(cap, shard), shape(8, width, F32)),
        (rows_out(width), rows_out(width), rows_out(shard), rows_out(shard), whole((8, width))),
        grid, parts_scratch(width) * 2, 18, "middle_back",
    )
    order.done(context_grad_other)


    branch_far = order.step(*branch_far)

    def attend_back(projected, attend, context_grad):
        projected, attend, context_grad = order.then(projected, attend, context_grad)
        grads, sums = call(
            functools.partial(attention_back_kernel, heads, shard, cell), meta,
            (projected, attend, context_grad),
            [whole((cap, 3 * shard)), whole((kept, cell, heads * cell)), whole((cap, shard))],
            (shape(cap, 3 * shard), shape(8, shard, F32)), (whole((cap, 3 * shard)), whole((8, shard))),
            (1,), (), 30, "attend_back",
        )
        order.done(grads)
        return grads, sums

    up_own = weight_grad(second, hidden_own)
    proj_grad_other, qkv_vec_other = attend_back(proj_other, attend_other, context_grad_other)
    up_sum.first(order, up_own)
    down_own = weight_grad(active_own, grad_low)

    def attn_grads(proj_grad, context):
        return weight_grad(proj_grad, normed, context, attn_grad, rows=width)

    attn_sum = Reduction(meta, attn_grads(proj_grad_other, context_other))
    down_sum.first(order, down_own)
    up_sum.second(order)
    proj_grad_own, qkv_vec_own = attend_back(proj_own, attend_own, context_grad_own)
    up_sum.third(order)
    down_sum.second(order)
    attn_own = attn_grads(proj_grad_own, context_own)
    attn_sum.first(order, attn_own)
    up_sum.fourth(order)
    down_sum.third(order)
    (first_grads,) = order.then(proj_grad_own)
    first_part = call(
        first_part_kernel, meta,
        (first_grads, proj_grad_other, qkv_own, qkv_other),
        [rows_spec(3 * shard)] * 2 + [whole((3 * shard, width)), ANYWHERE],
        part_shapes(cap, width), (ANYWHERE,) * CHUNKS,
        grid, [pltpu.VMEM((qkv_rows, width), LOW), pltpu.SemaphoreType.DMA((8,)), *out_scratch(width)],
        15, "first_part",
    )
    order.done(*first_part)
    first_far = swap_cores(first_part)
    up_sum.spread(order, 2)
    down_sum.fourth(order)
    attn_sum.second(order, 60)
    first_far = order.then(*first_far)
    input_pair, first_sums, table_grad = call(
        start_back_kernel, meta, (*first_part, *first_far, start, middle_grad, gains[0:1]),
        [ANYWHERE] * (2 * CHUNKS) + [rows_spec(width)] * 2 + [whole((1, width))],
        (pair_shape, shape(8, width, F32), shape(table.shape[0], width, F32)),
        (pair_spec, whole((8, width)), whole(table.shape)),
        grid, [row_scratch] + parts_scratch(width) * 2, 15, "start_back",
    )
    order.done(input_pair)
    up_sum.spread(order, 1)
    attn_sum.third(order)
    down_sum.spread(order, 2)
    rows_small = 8 + table.shape[0]
    vector_inputs = (first_sums, second_sums, table_grad, qkv_vec_own, qkv_vec_other, up_vecs)
    small, small_other = call(
        functools.partial(vectors_kernel, shard), meta, vector_inputs,
        [whole(value.shape) for value in vector_inputs],
        (shape(rows_small, width, F32),) * 2, (whole((rows_small, width)),) * 2, (1,), (), 2, "vectors",
    )
    small_far = swap(small_other, "tp", 2)
    input_far = swap(input_pair[kept:], "tp", 2)
    attn_sum.fourth(order)
    (small_far,) = order.step(small_far)
    small = small + small_far
    small_far = swap(small, "dp", 1)
    down_sum.spread(order, 1)
    middle_now, *branch_far = order.then(middle, *branch_far)
    (output_pair,) = call(
        finish_kernel, meta, (middle_now, *branch, *branch_far, out_rows[1:2]),
        [rows_spec(width)] + [ANYWHERE] * (2 * CHUNKS) + [whole((1, width))],
        (pair_shape,), (pair_spec,),
        grid, [row_scratch] + parts_scratch(width) * 2, 10, "finish",
    )
    order.done(output_pair)
    output_far = swap(output_pair[kept:], "tp", 2)
    attn_sum.spread(order, 2)
    (input_far,) = order.step(input_far)
    (up_total,) = up_sum.last_halves(order, (width,))
    (down_total,) = down_sum.last_halves(order, (width,))
    attn_sum.spread(order, 1)
    (small_far,) = order.step(small_far)
    small = small + small_far
    small_far = swap(small, "dp", 2)
    input_grad = place_cells(input_pair[:kept], order.then(input_far)[0])
    order.done(input_grad)
    (small_far,) = order.step(small_far)
    small = small + small_far
    small_far = swap(small, "dp", 4)
    cell_outputs = place_cells(output_pair[:kept], order.then(output_far)[0])
    order.done(cell_outputs)
    (small_far,) = order.step(small_far)
    small = later_groups(small + small_far)
    qkv_total, out_total = attn_sum.last_halves(order, (3 * shard, shard))

    return (
        cell_outputs,
        input_grad,
        small[0:2],
        small[2:4],
        qkv_total.reshape(3, shard, width).transpose(2, 0, 1),
        small[-2, : 2 * shard].reshape(2, shard),
        out_total,
        small[4:6],
        up_total,
        small[-1],
        down_total,
        small[6:-2],
    )


def solution(mesh):
    in_specs = (
        P("dp", "tp", None),
        P("dp", "tp", None),
        P("dp"),
        P("dp"),
        P(),
        P(),
        P(None, None, "tp"),
        P(None, "tp"),
        P("tp", None),
        P(),
        P(None, "tp"),
        P("tp"),
        P("tp", None),
        P(),
    )
    out_specs = (
        P("dp", "tp", None),
        P("dp", "tp", None),
        P(),
        P(),
        P(None, None, "tp"),
        P(None, "tp"),
        P("tp", None),
        P(),
        P(None, "tp"),
        P("tp"),
        P("tp", None),
        P(),
    )
    return jax.shard_map(
        on_device, mesh=mesh, in_specs=in_specs, out_specs=out_specs, check_vma=False
    )
```

```python
import functools
import math

import jax
import jax.numpy as jnp
from jax import lax
from jax.experimental import pallas as pl
from jax.experimental.pallas import tpu as pltpu
from jax.sharding import PartitionSpec as P

HEAD_DIM = 56
EPSILON = 1e-05
BLOCK = 256
META_BLOCKS = 8
TILE = 16
UNROLL = 4
F32 = jnp.float32
LOW = jnp.bfloat16
VMEM_BYTES = 56 * 1024 * 1024
FLOPS_PER_US = 450000000

NBLK, NCELL, BITS, TILE_SRC, TILE_SET, TILE_LEN, TILE_DST, CELL_OFF, CELL_ROWS = 0, 1, 2, 8, 136, 264, 392, 520, 552


def swap(value, axis, bit):
    count = lax.axis_size(axis)
    if value.ndim == 2 and value.shape[0] % TILE == 0:
        chunk = TILE if value.shape[0] // TILE % 128 else 2 * TILE
        tiled = value.reshape(value.shape[0] // chunk, chunk, value.shape[1])
        return swap(tiled, axis, bit).reshape(value.shape)
    return lax.ppermute(value, axis, [(i, i ^ bit) for i in range(count)])


CHUNKS = 2


def swap_cores(parts):
    return tuple(swap(part, "tp", 1) for part in parts)


class Sequence:
    def __init__(self):
        self.last = ()

    def then(self, *values):
        if not self.last:
            return values
        return lax.optimization_barrier((*values, *self.last))[: len(values)]

    def done(self, *values):
        self.last = (values[-1],)

    def step(self, *values):
        values = self.then(*values)
        self.last = (values[-1],)
        return values


def dot(a, b):
    return jnp.dot(a, b, preferred_element_type=F32)


def dot_nt(a, b):
    return lax.dot_general(a, b, (((1,), (1,)), ((), ())), preferred_element_type=F32)


def dot_tn(a, b):
    return lax.dot_general(a, b, (((0,), (0,)), ((), ())), preferred_element_type=F32)


def row_norm(rows):
    center = rows - jnp.mean(rows, axis=-1, keepdims=True)
    spread = jnp.mean(center * center, axis=-1, keepdims=True)
    scale = lax.rsqrt(spread + EPSILON)
    return center * scale, scale


def norm_back(grad, unit, scale, gain):
    scaled = grad * gain
    first = jnp.mean(scaled, axis=-1, keepdims=True)
    second = jnp.mean(scaled * unit, axis=-1, keepdims=True)
    return scale * (scaled - first - unit * second)


def whole(shape):
    zeros = (0,) * len(shape)
    return pl.BlockSpec(shape, lambda i, meta: zeros, pipeline_mode=pl.Buffered(1))


def rows_spec(width):
    return pl.BlockSpec((BLOCK, width), lambda i, meta: (jnp.minimum(i, meta[NBLK] - 1), 0))


PART_BLOCKS = META_BLOCKS // CHUNKS
PART_ROWS = PART_BLOCKS * BLOCK


def part_shapes(rows, width):
    return (jax.ShapeDtypeStruct((rows // CHUNKS, width), LOW),) * CHUNKS


def parts_scratch(width):
    return [pltpu.VMEM((META_BLOCKS * BLOCK, width), LOW), pltpu.SemaphoreType.DMA((CHUNKS,))]


def out_scratch(width):
    return [pltpu.VMEM((2, BLOCK, width), LOW), pltpu.SemaphoreType.DMA((2,))]


def each_part(parts, rows, sems):
    return [
        pltpu.make_async_copy(part, rows.at[pl.ds(at * PART_ROWS, PART_ROWS)], sems.at[at])
        for at, part in enumerate(parts)
    ]


def fetch_parts(step, blocks, *groups):
    for parts, rows, sems in groups:
        for at, copy in enumerate(each_part(parts, rows, sems)):

            @pl.when((step == 0) & (at * PART_BLOCKS < blocks))
            def _():
                copy.start()

    for parts, rows, sems in groups:
        for at, copy in enumerate(each_part(parts, rows, sems)):

            @pl.when(step == at * PART_BLOCKS)
            def _():
                copy.wait()


def block_of(step, rows):
    return rows[pl.ds(pl.multiple_of(step * BLOCK, BLOCK), BLOCK), :].astype(F32)


def put_part(step, last, value, parts, slots, sems):
    slot = lax.rem(step, 2)

    def copy_to(part, slot):
        begin = pl.multiple_of(lax.rem(step, PART_BLOCKS) * BLOCK, BLOCK)
        return pltpu.make_async_copy(slots.at[slot], part.at[pl.ds(begin, BLOCK)], sems.at[slot])

    @pl.when(step >= 2)
    def _():
        copy_to(parts[0], slot).wait()

    slots[slot] = value
    for at, part in enumerate(parts):

        @pl.when(step // PART_BLOCKS == at)
        def _():
            copy_to(part, slot).start()

    @pl.when(last)
    def _():
        copy_to(parts[0], slot).wait()

        @pl.when(step >= 1)
        def _():
            copy_to(parts[0], 1 - slot).wait()


def rows_out(width):
    return rows_spec(width)


def rows_more(width):
    return pl.BlockSpec((BLOCK, width), lambda i, meta: (jnp.minimum(i, meta[NBLK]), 0))


def live_step(meta):
    return pl.when(pl.program_id(0) < meta[NBLK])


ANYWHERE = pl.BlockSpec(memory_space=pl.ANY)


def call(kernel, meta, operands, in_specs, out_shape, out_specs, grid, scratch=(), cost=5, name=None):
    return pl.pallas_call(
        kernel,
        grid_spec=pltpu.PrefetchScalarGridSpec(
            num_scalar_prefetch=1,
            grid=grid,
            in_specs=in_specs,
            out_specs=out_specs,
            scratch_shapes=list(scratch),
        ),
        out_shape=out_shape,
        compiler_params=pltpu.CompilerParams(
            dimension_semantics=("arbitrary",) * len(grid), vmem_limit_bytes=VMEM_BYTES
        ),
        cost_estimate=pl.CostEstimate(flops=cost * FLOPS_PER_US, bytes_accessed=0, transcendentals=0),
        name=name,
    )(meta, *operands)


def load_tiles(sources, tiles, sems, count):
    copies = [
        pltpu.make_async_copy(source, tiles.at[pl.ds(at * count, count)], sems.at[at])
        for at, source in enumerate(sources)
    ]
    for copy in copies:
        copy.start()
    for copy in copies:
        copy.wait()


def begin_kernel(count, meta, a0, a1, a2, a3, table, gain, shift, weight, bias, start, normed, projected, tiles, sems):
    step = pl.program_id(0)

    @pl.when(step == 0)
    def _():
        load_tiles((a0, a1, a2, a3), tiles, sems, count)

    @pl.when(step < meta[NBLK])
    def _():
        for j in range(BLOCK // TILE):
            at = step * (BLOCK // TILE) + j
            tile = tiles[meta[TILE_SRC + at]].astype(F32)
            start[j * TILE : (j + 1) * TILE, :] = tile + table[pl.ds(meta[TILE_SET + at], 1), :]
        unit, _ = row_norm(start[...])
        low = (unit * gain[...] + shift[...]).astype(LOW)
        normed[...] = low
        projected[...] = (dot_nt(low, weight[...]) + bias[...]).astype(LOW)

    @pl.when(step == meta[NBLK])
    def _():
        projected[...] = jnp.zeros_like(projected)


def project_kernel(meta, normed, eighths, bias, projected, weight, sems):
    step = pl.program_id(0)

    @pl.when(step == 0)
    def _():
        load_eighths(eighths, [weight], sems)

    @pl.when(step < meta[NBLK])
    def _():
        projected[...] = (dot_nt(normed[...], weight[: bias.shape[1], :]) + bias[...]).astype(LOW)

    @pl.when(step == meta[NBLK])
    def _():
        projected[...] = jnp.zeros_like(projected)


def head_masks(cell, heads, shard):
    lane = lax.broadcasted_iota(jnp.int32, (cell, shard), 1)
    return [(lane >= h * HEAD_DIM) & (lane < (h + 1) * HEAD_DIM) for h in range(heads)]


def spread_heads(rows, masks, heads, low, high):
    part = rows[:, low:high]
    zero = jnp.zeros_like(part)
    return jnp.concatenate([jnp.where(masks[h][:, low:high], part, zero) for h in heads], axis=0)


def head_groups(heads, shard):
    groups = []
    at = 0
    while at < heads:
        end = min(at + 4, heads)
        low = at * HEAD_DIM // 128 * 128
        high = min(-(-end * HEAD_DIM // 128) * 128, shard)
        groups.append((tuple(range(at, end)), low, high))
        at = end
    return groups


def attention_kernel(heads, shard, cell, meta, projected, context, attend, same_head):
    context[...] = jnp.zeros_like(context)
    masks = head_masks(cell, heads, shard)
    scale = 1.0 / math.sqrt(HEAD_DIM)
    span = same_head.shape[0]
    head_of = [lax.broadcasted_iota(jnp.int32, (span, span), axis) // cell for axis in (0, 1)]
    same_head[...] = jnp.where(head_of[0] == head_of[1], 1.0, 0.0).astype(LOW)

    def one(index):
        at = pl.multiple_of(meta[CELL_OFF + index] * TILE, TILE)
        queries = projected[pl.ds(at, cell), 0:shard]
        keys = projected[pl.ds(at, cell), shard : 2 * shard]
        values = projected[pl.ds(at, cell), 2 * shard : 3 * shard]
        total = None
        for group, low, high in head_groups(heads, shard):
            count = len(group) * cell
            scores = dot_nt(queries[:, low:high], spread_heads(keys, masks, group, low, high)) * scale
            row = lax.broadcasted_iota(jnp.int32, (cell, count), 0)
            lane = lax.broadcasted_iota(jnp.int32, (cell, count), 1)
            scores = jnp.where(row >= lax.rem(lane, cell), scores, -1e30)
            shifted = []
            for pair in range(0, len(group), 2):
                both = scores[:, pair * cell : min(pair + 2, len(group)) * cell]
                if pair + 1 < len(group):
                    left = lax.broadcasted_iota(jnp.int32, both.shape, 1) < cell
                    top_left = jnp.max(jnp.where(left, both, -1e30), axis=1, keepdims=True)
                    top_right = jnp.max(jnp.where(left, -1e30, both), axis=1, keepdims=True)
                    shifted.append(both - jnp.where(left, top_left, top_right))
                else:
                    shifted.append(both - jnp.max(both, axis=1, keepdims=True))
            weights = jnp.exp(jnp.concatenate(shifted, axis=1) if len(shifted) > 1 else shifted[0])
            if len(group) > 1:
                sums = dot(weights.astype(LOW), same_head[:count, :count])
            else:
                sums = jnp.sum(weights, axis=1, keepdims=True)
            probs = (weights * (1.0 / sums)).astype(LOW)
            first = group[0] * cell
            attend[index, :, first : first + count] = probs
            part = dot(probs, spread_heads(values, masks, group, low, high))
            if high - low < shard:
                part = jnp.pad(part, ((0, 0), (low, shard - high)))
            total = part if total is None else total + part
        context[pl.ds(at, cell), :] = total.astype(LOW)

    def body(step, carry):
        for place in range(UNROLL):
            one(UNROLL * step + place)
        return carry

    lax.fori_loop(0, (meta[NCELL] + UNROLL - 1) // UNROLL, body, 0)


def attention_back_kernel(heads, shard, cell, meta, projected, attend, context_grad, result, sums):
    result[...] = jnp.zeros_like(result)
    sums[...] = jnp.zeros_like(sums)
    masks = head_masks(cell, heads, shard)
    scale = 1.0 / math.sqrt(HEAD_DIM)
    row = lax.broadcasted_iota(jnp.int32, (cell, shard), 0)
    left = lax.broadcasted_iota(jnp.int32, (cell, 2 * cell), 1) < cell

    def fold(stacked, group, low, high):
        total = None
        for place, h in enumerate(group):
            part = jnp.where(masks[h][:, low:high], stacked[place * cell : (place + 1) * cell, :], 0.0)
            total = part if total is None else total + part
        return total

    def widen(part, low, high):
        return jnp.pad(part, ((0, 0), (low, shard - high))) if high - low < shard else part

    def one(index):
        at = pl.multiple_of(meta[CELL_OFF + index] * TILE, TILE)
        queries = projected[pl.ds(at, cell), 0:shard]
        keys = projected[pl.ds(at, cell), shard : 2 * shard]
        values = projected[pl.ds(at, cell), 2 * shard : 3 * shard]
        grads = context_grad[pl.ds(at, cell), :]
        grads = jnp.where(row < meta[CELL_ROWS + index], grads, jnp.zeros_like(grads))
        query_total = key_total = value_total = None
        for group, low, high in head_groups(heads, shard):
            first = group[0] * cell
            probs = attend[index, :, first : first + len(group) * cell]
            attend_grad = dot_nt(grads[:, low:high], spread_heads(values, masks, group, low, high))
            parts = []
            for pair in range(0, len(group), 2):
                if pair + 1 < len(group):
                    span = slice(pair * cell, (pair + 2) * cell)
                    weights = probs[:, span].astype(F32)
                    both = attend_grad[:, span]
                    product = weights * both
                    sum_left = jnp.sum(jnp.where(left, product, 0.0), axis=1, keepdims=True)
                    sum_right = jnp.sum(jnp.where(left, 0.0, product), axis=1, keepdims=True)
                    parts.append((product - weights * jnp.where(left, sum_left, sum_right)).astype(LOW))
                else:
                    span = slice(pair * cell, (pair + 1) * cell)
                    weights = probs[:, span].astype(F32)
                    product = weights * attend_grad[:, span]
                    total = jnp.sum(product, axis=1, keepdims=True)
                    parts.append((product - weights * total).astype(LOW))
            score_grad = jnp.concatenate(parts, axis=1) if len(parts) > 1 else parts[0]
            query_part = dot(score_grad, spread_heads(keys, masks, group, low, high)) * scale
            key_part = fold(dot_tn(score_grad, queries[:, low:high]), group, low, high) * scale
            value_part = fold(dot_tn(probs, grads[:, low:high]), group, low, high)
            query_part, key_part, value_part = (widen(p, low, high) for p in (query_part, key_part, value_part))
            if query_total is None:
                query_total, key_total, value_total = query_part, key_part, value_part
            else:
                query_total, key_total, value_total = (
                    query_total + query_part,
                    key_total + key_part,
                    value_total + value_part,
                )
        for place, part in enumerate((query_total, key_total, value_total)):
            low_part = part.astype(LOW)
            result[pl.ds(at, cell), place * shard : (place + 1) * shard] = low_part
            sums[place : place + 1, :] += jnp.sum(low_part.astype(F32), axis=0, keepdims=True)

    def body(step, carry):
        one(2 * step)
        one(2 * step + 1)
        return carry

    lax.fori_loop(0, (meta[NCELL] + 1) // 2, body, 0)


def out_project_kernel(meta, a, b, weight_a, weight_b, *refs):
    *parts, slots, sems = refs
    step = pl.program_id(0)

    @live_step(meta)
    def _():
        value = (dot(a[...], weight_a[...]) + dot(b[...], weight_b[...])).astype(LOW)
        put_part(step, step == meta[NBLK] - 1, value, parts, slots, sems)


def first_part_kernel(meta, a, b, weight_a, eighths, *refs):
    step = pl.program_id(0)
    *parts, weight_b, weight_sems, slots, sems = refs

    @pl.when(step == 0)
    def _():
        load_eighths(eighths, [weight_b], weight_sems)

    @live_step(meta)
    def _():
        value = (dot(a[...], weight_a[...]) + dot(b[...], weight_b[: b.shape[1], :])).astype(LOW)
        put_part(step, step == meta[NBLK] - 1, value, parts, slots, sems)


def gelu_pair(hidden):
    chance = 0.5 * (1.0 + lax.erf(hidden * (1.0 / math.sqrt(2.0))))
    slope = chance + hidden * (jnp.exp(-0.5 * hidden * hidden) * (1.0 / math.sqrt(2.0 * math.pi)))
    return hidden * chance, slope


def mlp_block(second, product, up, bias, down, active, hidden_grad, bias_grad):
    hidden = dot(second, up[...]) + bias[...]
    value, slope = gelu_pair(hidden)
    low = value.astype(LOW)
    active[...] = low
    back = (slope * product).astype(LOW)
    hidden_grad[...] = back
    bias_grad[...] += jnp.sum(back.astype(F32), axis=0, keepdims=True)
    return dot(low, down[...]), dot_nt(back, up[...])


def mlp_kernel(count, meta, start, *refs):
    near_parts, far_parts, refs = refs[:CHUNKS], refs[CHUNKS : 2 * CHUNKS], refs[2 * CHUNKS :]
    bias_row, gain, shift, a0, a1, a2, a3, up, up_bias, down, other_up, other_bias, eighths, *refs = refs
    middle, second, grad, active, hidden_grad, other_active, other_hidden, *refs = refs
    branch, second_grad, refs = refs[:CHUNKS], refs[CHUNKS : 2 * CHUNKS], refs[2 * CHUNKS :]
    bias_grad, tiles, sems, near_rows, near_sems, far_rows, far_sems, *refs = refs
    other_down, other_sems, branch_slots, branch_sems, grad_slots, grad_sems = refs
    step = pl.program_id(0)
    copies = eighths_copies(eighths, [other_down], other_sems)

    @pl.when(step == 0)
    def _():
        load_tiles((a0, a1, a2, a3), tiles, sems, count)
        for copy in copies:
            copy.start()
        bias_grad[...] = jnp.zeros_like(bias_grad)

    @live_step(meta)
    def _():
        last = step == meta[NBLK] - 1
        fetch_parts(step, meta[NBLK], (near_parts, near_rows, near_sems), (far_parts, far_rows, far_sems))
        inner = lax.broadcasted_iota(jnp.int32, (TILE, 1), 0)
        for j in range(BLOCK // TILE):
            at = step * (BLOCK // TILE) + j
            tile = tiles[meta[TILE_SRC + at]]
            grad[j * TILE : (j + 1) * TILE, :] = jnp.where(inner < meta[TILE_LEN + at], tile, jnp.zeros_like(tile))

        @pl.when(step == 0)
        def _():
            for copy in copies:
                copy.wait()

        own_product = dot_nt(grad[...], down[...])
        other_product = dot_nt(grad[...], other_down[...])
        rows = start[...] + (block_of(step, near_rows) + block_of(step, far_rows)) + bias_row[...]
        middle[...] = rows
        unit, _ = row_norm(rows)
        low = (unit * gain[...] + shift[...]).astype(LOW)
        second[...] = low
        own = mlp_block(low, own_product, up, up_bias, down, active, hidden_grad, bias_grad.at[0:1])
        other = mlp_block(
            low, other_product, other_up, other_bias, other_down, other_active, other_hidden, bias_grad.at[1:2]
        )
        put_part(step, last, (own[1] + other[1]).astype(LOW), second_grad, grad_slots, grad_sems)
        put_part(step, last, (own[0] + other[0]).astype(LOW), branch, branch_slots, branch_sems)


def weight_grad_kernel(pairs, meta, *refs):
    step = pl.program_id(0)
    result, total = refs[2 * pairs :]

    @live_step(meta)
    def _():
        base = 0
        for a, b in zip(refs[: 2 * pairs : 2], refs[1 : 2 * pairs : 2]):
            rows = slice(base, base + a.shape[1])
            part = dot_tn(a[...], b[...])
            base += a.shape[1]

            @pl.when(step == 0)
            def _():
                total[rows, :] = part

            @pl.when(step > 0)
            def _():
                total[rows, :] += part

        @pl.when(step == meta[NBLK] - 1)
        def _():
            result[...] = total[...].astype(LOW)


def middle_back_kernel(meta, *refs):
    near_parts, far_parts, refs = refs[:CHUNKS], refs[CHUNKS : 2 * CHUNKS], refs[2 * CHUNKS :]
    middle, grad, gain, out_a, out_b, middle_grad, attn_grad, context_a, context_b, sums, *refs = refs
    near_rows, near_sems, far_rows, far_sems = refs
    step = pl.program_id(0)

    @pl.when(step == 0)
    def _():
        sums[...] = jnp.zeros_like(sums)

    @live_step(meta)
    def _():
        fetch_parts(step, meta[NBLK], (near_parts, near_rows, near_sems), (far_parts, far_rows, far_sems))
        unit, scale = row_norm(middle[...])
        second_grad = block_of(step, near_rows) + block_of(step, far_rows)
        grad_rows = grad[...].astype(F32)
        total = grad_rows + norm_back(second_grad, unit, scale, gain[...])
        middle_grad[...] = total
        low = total.astype(LOW)
        attn_grad[...] = low
        context_a[...] = dot_nt(low, out_a[...]).astype(LOW)
        context_b[...] = dot_nt(low, out_b[...]).astype(LOW)
        for at, rows in enumerate((second_grad * unit, second_grad, total, grad_rows)):
            sums[at : at + 1, :] += jnp.sum(rows, axis=0, keepdims=True)


def scatter_tiles(meta, step, rows, out):
    for j in range(BLOCK // TILE):
        place = meta[TILE_DST + step * (BLOCK // TILE) + j]

        @pl.when(place >= 0)
        def _():
            out[place] = rows[j * TILE : (j + 1) * TILE, :].astype(LOW)


def start_back_kernel(meta, *refs):
    near_parts, far_parts, refs = refs[:CHUNKS], refs[CHUNKS : 2 * CHUNKS], refs[2 * CHUNKS :]
    start, middle_grad, gain, out, sums, table, rows, near_rows, near_sems, far_rows, far_sems = refs
    step = pl.program_id(0)

    @pl.when(step == 0)
    def _():
        out[...] = jnp.zeros_like(out)
        sums[...] = jnp.zeros_like(sums)
        table[...] = jnp.zeros_like(table)

    @live_step(meta)
    def _():
        fetch_parts(step, meta[NBLK], (near_parts, near_rows, near_sems), (far_parts, far_rows, far_sems))
        unit, scale = row_norm(start[...])
        first_grad = block_of(step, near_rows) + block_of(step, far_rows)
        rows[...] = middle_grad[...] + norm_back(first_grad, unit, scale, gain[...])
        for at, value in enumerate((first_grad * unit, first_grad)):
            sums[at : at + 1, :] += jnp.sum(value, axis=0, keepdims=True)
        for j in range(BLOCK // TILE):
            at = meta[TILE_SET + step * (BLOCK // TILE) + j]
            table[pl.ds(at, 1), :] += jnp.sum(rows[j * TILE : (j + 1) * TILE, :], axis=0, keepdims=True)
        scatter_tiles(meta, step, rows, out)


def finish_kernel(meta, middle, *refs):
    near_parts, far_parts, refs = refs[:CHUNKS], refs[CHUNKS : 2 * CHUNKS], refs[2 * CHUNKS :]
    bias_row, out, rows, near_rows, near_sems, far_rows, far_sems = refs
    step = pl.program_id(0)

    @pl.when(step == 0)
    def _():
        out[...] = jnp.zeros_like(out)

    @live_step(meta)
    def _():
        fetch_parts(step, meta[NBLK], (near_parts, near_rows, near_sems), (far_parts, far_rows, far_sems))
        rows[...] = middle[...] + (block_of(step, near_rows) + block_of(step, far_rows)) + bias_row[...]
        inner = lax.broadcasted_iota(jnp.int32, (TILE, 1), 0)
        for j in range(BLOCK // TILE):
            at = step * (BLOCK // TILE) + j
            place = meta[TILE_DST + at]

            @pl.when(place >= 0)
            def _():
                out[place] = jnp.where(inner < meta[TILE_LEN + at], rows[j * TILE : (j + 1) * TILE, :], 0.0).astype(LOW)


def vectors_kernel(shard, meta, first, second, table, own, other, up, small, small_other):
    for out, qkv, at in ((small, own, 0), (small_other, other, 1)):
        out[0:1, :] = first[0:1, :]
        out[1:2, :] = second[0:1, :]
        out[2:3, :] = first[1:2, :]
        out[3:6, :] = second[1:4, :]
        out[6:38, :] = table[...]
        out[38:40, :] = jnp.zeros((2, out.shape[1]), F32)
        out[38:39, :shard] = qkv[0:1, :]
        out[38:39, shard : 2 * shard] = qkv[2:3, :]
        out[39:40, :] = up[at : at + 1, :]


def window_size(half):
    return -(-half // (4 * TILE)) * TILE


def window_at(low, high, half):
    size = window_size(half)
    return low * (half - 2 * size) + high * size


def run_copies(copies):
    for copy in copies:
        copy.start()
    for copy in copies:
        copy.wait()


def join_kernel(extra, level, meta, mine, far, out, sems):
    rows = mine.shape[0]

    def put(first, second):
        run_copies(
            [
                pltpu.make_async_copy(first, out.at[pl.ds(0, rows)], sems.at[0]),
                pltpu.make_async_copy(second.at[pl.ds(extra, rows - extra)], out.at[pl.ds(rows, rows - extra)], sems.at[1]),
            ]
        )

    @pl.when(meta[BITS + level] == 0)
    def _():
        put(mine, far)

    @pl.when(meta[BITS + level] == 1)
    def _():
        put(far, mine)


def join(meta, mine, far, level, total):
    rows, width = mine.shape
    (result,) = call(
        functools.partial(join_kernel, 2 * rows - total, level), meta, (mine, far), [ANYWHERE] * 2,
        (jax.ShapeDtypeStruct((total, width), LOW),), (whole((total, width)),),
        (1,), [pltpu.SemaphoreType.DMA((2,))], cost=3, name="join",
    )
    return result


def gather_eighths(piece):
    groups = lax.axis_size("dp")
    spans = [list(range(at, at + 8)) for at in range(0, groups, 8)] if groups > 8 else None
    tiled = piece.reshape(piece.shape[0] // TILE, TILE, piece.shape[1])
    whole_block = lax.all_gather(tiled, "dp", axis=0, tiled=True, axis_index_groups=spans)
    return whole_block.reshape(8 * piece.shape[0], piece.shape[1])


def eighths_copies(gathered, scratches, sems):
    copies = []
    for at, scratch in enumerate(scratches):
        half = scratch.shape[0] // 2
        size = window_size(half)
        for group in range(8):
            low, high = (group >> 1) & 1, group >> 2
            skip = 4 * size - half if (low, high) == (1, 0) else 0
            begin = (group & 1) * half + window_at(low, high, half) + skip
            copies.append(
                pltpu.make_async_copy(
                    gathered.at[pl.ds((group * len(scratches) + at) * size + skip, size - skip)],
                    scratch.at[pl.ds(begin, size - skip)],
                    sems.at[8 * at + group],
                )
            )
    return copies


def load_eighths(gathered, scratches, sems):
    copies = eighths_copies(gathered, scratches, sems)
    for copy in copies:
        copy.start()
    for copy in copies:
        copy.wait()


def first_sum_kernel(meta, own, far, sent):
    sent[...] = (own[...].astype(F32) + far[...].astype(F32)).astype(LOW)


def first_sum(meta, own, far):
    rows, width = own.shape
    half = rows // 2
    steps = next(count for count in (5, 4, 3, 1) if half % (count * TILE) == 0)
    block = half // steps
    source = pl.BlockSpec((block, width), lambda i, meta: ((1 - meta[BITS]) * steps + i, 0))
    (sent,) = call(
        first_sum_kernel, meta, (own, far), [source, source], (jax.ShapeDtypeStruct((half, width), LOW),),
        (pl.BlockSpec((block, width), lambda i, meta: (i, 0)),), (steps,), cost=5, name="first_sum",
    )
    return sent


def second_sum_kernel(half, meta, mine, far, arrived, kept, sent):
    size = 2 * window_size(half)
    bit = meta[BITS + 1]
    for out, place in ((kept, bit), (sent, 1 - bit)):
        rows = pl.ds(pl.multiple_of(place * (half - size), TILE), size)
        total = mine[rows, :].astype(F32) + far[rows, :].astype(F32) + arrived[rows, :].astype(F32)
        out[...] = total.astype(out.dtype)


def second_sum(meta, own, far, arrived, cost):
    half, width = arrived.shape
    size = 2 * window_size(half)
    kept = pl.BlockSpec((half, width), lambda i, meta: (meta[BITS], 0), pipeline_mode=pl.Buffered(1))
    return call(
        functools.partial(second_sum_kernel, half), meta, (own, far, arrived), [kept, kept, whole((half, width))],
        (jax.ShapeDtypeStruct((size, width), F32), jax.ShapeDtypeStruct((size, width), LOW)),
        (whole((size, width)),) * 2, (1,), cost=cost, name="second_sum",
    )


def third_sum_kernel(count, meta, *refs):
    kept, arrived, own, sent = refs[:count], refs[count], refs[count + 1 : 2 * count + 1], refs[-1]
    size = own[0].shape[0]
    bit = meta[BITS + 2]
    for at in range(count):
        for place in (bit, 1 - bit):
            begin = pl.multiple_of(place * size, TILE)
            far = arrived[pl.ds(pl.multiple_of(2 * at * size + begin, TILE), size), :].astype(F32)
            total = kept[at][pl.ds(begin, size), :] + far
            if place is bit:
                own[at][...] = total
            else:
                sent[at * size : (at + 1) * size, :] = total.astype(LOW)


def third_sum(meta, kept, arrived, cost=3):
    count = len(kept)
    size, width = kept[0].shape[0] // 2, kept[0].shape[1]
    *own, sent = call(
        functools.partial(third_sum_kernel, count), meta, (*kept, arrived),
        [whole(each.shape) for each in (*kept, arrived)],
        (jax.ShapeDtypeStruct((size, width), F32),) * count + (jax.ShapeDtypeStruct((count * size, width), LOW),),
        (whole((size, width)),) * count + (whole((count * size, width)),), (1,), cost=cost, name="third_sum",
    )
    return own, sent


def fourth_sum_kernel(count, meta, *refs):
    own, arrived, outs = refs[:count], refs[count], refs[count + 1 :]
    size = own[0].shape[0]
    for at, out in enumerate(outs):
        out[...] = (own[at][...] + arrived[at * size : (at + 1) * size, :].astype(F32)).astype(out.dtype)


def fourth_sum(meta, own, arrived, kinds):
    shape = own[0].shape
    return call(
        functools.partial(fourth_sum_kernel, len(own)), meta, (*own, arrived),
        [whole(each.shape) for each in (*own, arrived)],
        tuple(jax.ShapeDtypeStruct(shape, kind) for kind in kinds), (whole(shape),) * len(own),
        (1,), cost=3, name="fourth_sum",
    )


def widen_rows_kernel(meta, mine, far, *outs):
    half = mine.shape[0]

    def put(lower, upper):
        base = 0
        for out in outs:
            count = out.shape[0]
            split = min(max(half - base, 0), count)
            if split:
                out[:split, :] = lower[base : base + split, :].astype(F32)
            if split < count:
                begin = base + split - half
                out[split:, :] = upper[begin : begin + count - split, :].astype(F32)
            base += count

    @pl.when(meta[BITS] == 0)
    def _():
        put(mine, far)

    @pl.when(meta[BITS] == 1)
    def _():
        put(far, mine)


def widen_rows(meta, mine, far, rows):
    half, width = mine.shape
    return call(
        widen_rows_kernel, meta, (mine, far), [whole((half, width))] * 2,
        tuple(jax.ShapeDtypeStruct((count, width), F32) for count in rows),
        tuple(whole((count, width)) for count in rows), (1,), name="widen_rows",
    )


def later_groups(value):
    level = 3
    while (1 << level) < lax.axis_size("dp"):
        value = (value.astype(F32) + swap(value, "dp", 1 << level).astype(F32)).astype(value.dtype)
        level += 1
    return value


class Reduction:
    def __init__(self, meta, other):
        self.meta = meta
        self.far = swap(other, "tp", 2)

    def arrive(self, order):
        (self.far,) = order.step(self.far)

    def first(self, order, own):
        self.own, self.far = order.then(own, self.far)
        sent = first_sum(self.meta, self.own, self.far)
        order.done(sent)
        self.arrived = swap(sent, "dp", 1)

    def wait_second(self, order):
        (self.arrived,) = order.step(self.arrived)

    def second(self, order, cost=4):
        (arrived,) = order.then(self.arrived)
        self.half = arrived.shape[0]
        self.kept, sent = second_sum(self.meta, self.own, self.far, arrived, cost)
        order.done(sent)
        self.arrived = swap(sent, "dp", 2)

    def third(self, order, cost=3):
        (arrived,) = order.then(self.arrived)
        self.kept, sent = third_sum(self.meta, [self.kept], arrived, cost)
        order.done(sent)
        self.arrived = swap(sent, "dp", 4)

    def fourth(self, order):
        (arrived,) = order.then(self.arrived)
        (piece,) = fourth_sum(self.meta, self.kept, arrived, (LOW,))
        order.done(piece)
        piece = later_groups(piece)
        self.mine, self.far = piece, swap(piece, "dp", 4)

    def spread(self, order, level):
        mine, far = order.then(self.mine, self.far)
        rows = 2 * mine.shape[0] if level == 2 else self.half
        self.mine = join(self.meta, mine, far, level, rows)
        order.done(self.mine)
        self.far = swap(self.mine, "dp", 1 << (level - 1))

    def last_halves(self, order, rows):
        mine, far = order.then(self.mine, self.far)
        results = widen_rows(self.meta, mine, far, rows)
        order.done(results[0])
        return results


def eighth(block):
    half = block.shape[0] // 2
    index = lax.axis_index("dp")
    at = (index & 1) * half + window_at((index >> 1) & 1, (index >> 2) & 1, half)
    return lax.dynamic_slice_in_dim(block, at, window_size(half), 0)


def on_device(
    cell_inputs,
    out_grad,
    lengths,
    datasets,
    norm_gain,
    norm_bias,
    qkv_weight,
    qv_bias,
    out_weight,
    out_bias,
    up_weight,
    up_bias,
    down_weight,
    dataset_table,
):
    slots, quarter, width = cell_inputs.shape
    tensor = lax.axis_index("tp")
    chip = tensor // 2
    core = tensor % 2
    blocks_per_cell = lax.axis_size("tp")
    cell = quarter * blocks_per_cell
    shard = qkv_weight.shape[2]
    ff = up_weight.shape[1]
    heads = shard // HEAD_DIM
    kept = slots // 2
    tile_cap = META_BLOCKS * BLOCK // TILE
    cap = META_BLOCKS * BLOCK
    grid = (META_BLOCKS,)
    group = lax.axis_index("dp")
    index = jnp.arange(kept, dtype=jnp.int32)

    def mine_of(rows):
        pairs = rows.reshape(kept, 2, *rows.shape[1:])
        mine = lax.dynamic_index_in_dim(pairs, chip, 1, keepdims=False)
        theirs = lax.dynamic_index_in_dim(pairs, 1 - chip, 1, keepdims=False)
        return mine, theirs

    def place_cells(mine, other):
        even = jnp.where(chip == 0, mine, other)
        odd = jnp.where(chip == 0, other, mine)
        return jnp.stack([even, odd], axis=1).reshape(slots, quarter, width)

    cell_lengths, _ = mine_of(lengths)
    cell_sets, _ = mine_of(datasets)
    cell_tiles = (cell_lengths + TILE - 1) // TILE
    ends = jnp.sum(jnp.where(index[None, :] <= index[:, None], cell_tiles[None, :], 0), axis=1)
    begins = ends - cell_tiles
    tile_count = ends[-1]
    tile = jnp.arange(tile_cap, dtype=jnp.int32)
    owner = jnp.sum((ends[None, :] <= tile[:, None]).astype(jnp.int32), axis=1)
    live = tile < tile_count
    owned = (owner[:, None] == index[None, :]) & live[:, None]

    def of_owner(values):
        return jnp.sum(jnp.where(owned, values[None, :], 0), axis=1)

    block = tile - of_owner(begins)
    shelf = jnp.where(block // 2 == chip, 0, kept) + owner
    tile_src = jnp.where(live, jnp.where(block % 2 == core, 0, slots) + shelf, 0)
    tile_set = of_owner(cell_sets)
    tile_len = jnp.clip(of_owner(cell_lengths) - block * TILE, 0, TILE) * live
    tile_dst = jnp.where(live & (block % 2 == core), shelf, -1)
    cell_count = jnp.sum((cell_lengths > 0).astype(jnp.int32))
    block_count = (tile_count + BLOCK // TILE - 1) // (BLOCK // TILE)
    grid = (META_BLOCKS,)
    head = jnp.stack([block_count, cell_count, group & 1, (group >> 1) & 1, (group >> 2) & 1])

    meta = jnp.concatenate(
        [head, jnp.zeros((3,), jnp.int32), tile_src, tile_set, tile_len, tile_dst, begins, cell_tiles * TILE]
    ).astype(jnp.int32)

    order = Sequence()
    qkv_own = qkv_weight.transpose(1, 2, 0).reshape(3 * shard, width)
    qkv_rows = -(-3 * shard // (2 * TILE)) * 2 * TILE
    vectors = jnp.concatenate([qv_bias.reshape(-1), up_bias])
    piece_source, cells_now = lax.optimization_barrier(
        (eighth(jnp.pad(qkv_own, ((0, qkv_rows - 3 * shard), (0, 0)))), cell_inputs)
    )
    qkv_piece = swap(piece_source, "tp", 2)
    in_mine, in_theirs = mine_of(cells_now)
    in_other = swap(in_theirs, "tp", 2)
    in_far = swap(in_mine, "tp", 1)
    head_rows = jnp.pad(vectors, (0, 2 * width - vectors.shape[0])).reshape(2, width)
    out_and_vectors = jnp.concatenate([out_weight, head_rows, jnp.zeros((6, width), LOW)], axis=0)
    down_piece, out_and_vectors, grad_now, _ = lax.optimization_barrier(
        (eighth(down_weight), out_and_vectors, out_grad, in_theirs)
    )
    down_piece = swap(down_piece, "tp", 2)
    out_and_vectors = swap(out_and_vectors, "tp", 2)
    grad_mine, grad_theirs = mine_of(grad_now)
    meta, qkv_own, grad_mine, grad_theirs = order.step(meta, qkv_own, grad_mine, grad_theirs)
    (qkv_piece,) = order.step(qkv_piece)
    qkv_other = gather_eighths(qkv_piece)
    in_far, in_other = order.step(in_far, in_other)
    in_other_far = swap(in_other, "tp", 1)
    grad_other = swap(order.then(grad_theirs)[0], "tp", 2)
    (in_other_far,) = order.step(in_other_far)

    def biases(vector):
        zeros = jnp.zeros((shard,), LOW)
        qkv_row = jnp.concatenate([vector[:shard], zeros, vector[shard : 2 * shard]])
        return qkv_row.astype(F32)[None], vector[2 * shard :].astype(F32)[None]

    qkv_bias_own, up_bias_own = biases(vectors)
    gains = norm_gain.astype(F32)
    shifts = norm_bias.astype(F32)
    out_rows = out_bias.astype(F32)
    table = dataset_table.astype(F32)

    def shape(rows, cols, kind=LOW):
        return jax.ShapeDtypeStruct((rows, cols), kind)

    row_f32, row_low = shape(cap, width, F32), shape(cap, width)
    row_scratch = pltpu.VMEM((BLOCK, width), F32)
    tile_scratch = [pltpu.VMEM((2 * slots, TILE, width), LOW), pltpu.SemaphoreType.DMA((4,))]

    start, normed, proj_own = call(
        functools.partial(begin_kernel, kept), meta,
        (in_mine, in_other, in_far, in_other_far, table, gains[0:1], shifts[0:1], qkv_own, qkv_bias_own),
        [ANYWHERE] * 4 + [whole(table.shape), whole((1, width)), whole((1, width)), whole((3 * shard, width)), whole((1, 3 * shard))],
        (row_f32, row_low, shape(cap, 3 * shard)),
        (rows_out(width), rows_out(width), rows_more(3 * shard)),
        grid, tile_scratch, 15, "begin",
    )
    order.done(proj_own)

    def attend_shard(projected):
        (projected,) = order.then(projected)
        context, attend = call(
            functools.partial(attention_kernel, heads, shard, cell), meta, (projected,),
            [whole((cap, 3 * shard))],
            (shape(cap, shard), jax.ShapeDtypeStruct((kept, cell, heads * cell), LOW)),
            (whole((cap, shard)), whole((kept, cell, heads * cell))),
            (1,), [pltpu.VMEM((4 * cell, 4 * cell), LOW)], 4, "attend",
        )
        order.done(context)
        return context, attend

    down_piece, out_and_vectors = order.step(down_piece, out_and_vectors)
    down_other = gather_eighths(down_piece)
    grad_now, up_now = order.then(grad_mine, up_weight)
    up_other = swap(up_now, "tp", 2)
    grad_far = swap(grad_now, "tp", 1)
    context_own, attend_own = attend_shard(proj_own)
    grad_far, grad_other = order.step(grad_far, grad_other)
    out_other = out_and_vectors[:shard]
    vectors_other = out_and_vectors[shard : shard + 2].reshape(-1)[: vectors.shape[0]]
    normed_now, qkv_now = order.then(normed, qkv_other)
    qkv_bias_other, up_bias_other = biases(vectors_other)
    (proj_other,) = call(
        project_kernel, meta, (normed_now, qkv_now, qkv_bias_other),
        [rows_spec(width), ANYWHERE, whole((1, 3 * shard))],
        (shape(cap, 3 * shard),), (rows_more(3 * shard),),
        grid, [pltpu.VMEM((qkv_rows, width), LOW), pltpu.SemaphoreType.DMA((8,))],
        6, "project",
    )
    order.done(proj_other)
    context_other, attend_other = attend_shard(proj_other)
    grad_other_far = swap(grad_other, "tp", 1)
    (context_now,) = order.then(context_other)
    attn_part = call(
        out_project_kernel, meta, (context_own, context_now, out_weight, out_other),
        [rows_spec(shard), rows_spec(shard), whole((shard, width)), whole((shard, width))],
        part_shapes(cap, width), (ANYWHERE,) * CHUNKS,
        grid, out_scratch(width), 10, "out_project",
    )
    order.done(*attn_part)
    attn_far = swap_cores(attn_part)
    (grad_other_far,) = order.step(grad_other_far)

    start_now, grad_far, grad_other_far, up_other, down_other, *attn_far = order.then(
        start, grad_far, grad_other_far, up_other, down_other, *attn_far
    )
    middle, second, grad_low, active_own, hidden_own, active_other, hidden_other, *parts, up_vecs = call(
        functools.partial(mlp_kernel, kept), meta,
        (start_now, *attn_part, *attn_far, out_rows[0:1], gains[1:2], shifts[1:2], grad_mine, grad_other, grad_far, grad_other_far,
         up_weight, up_bias_own, down_weight, up_other, up_bias_other, down_other),
        [rows_spec(width)] + [ANYWHERE] * (2 * CHUNKS) + [whole((1, width))] * 3 + [ANYWHERE] * 4
        + [whole((width, ff)), whole((1, ff)), whole((ff, width)), whole((width, ff)), whole((1, ff)), ANYWHERE],
        (row_f32, row_low, row_low, *(shape(cap, ff),) * 4, *part_shapes(cap, width), *part_shapes(cap, width), shape(8, ff, F32)),
        (rows_out(width),) * 3 + (rows_out(ff),) * 4 + (ANYWHERE,) * (2 * CHUNKS) + (whole((8, ff)),),
        grid,
        tile_scratch + parts_scratch(width) * 2
        + [pltpu.VMEM((ff, width), LOW), pltpu.SemaphoreType.DMA((8,))]
        + out_scratch(width) * 2,
        65, "mlp",
    )
    branch, second_grad = parts[:CHUNKS], parts[CHUNKS:]
    order.done(*second_grad)
    second_grad_far = swap_cores(second_grad)
    branch_far = swap_cores(branch)

    def weight_grad(*operands, rows=None):
        operands = order.then(*operands)
        pairs = len(operands) // 2
        cols = operands[1].shape[1]
        rows = rows or operands[0].shape[1]
        (result,) = call(
            functools.partial(weight_grad_kernel, pairs), meta, operands,
            [rows_spec(operand.shape[1]) for operand in operands],
            (shape(rows, cols),), (whole((rows, cols)),),
            grid, [pltpu.VMEM((rows, cols), F32)], cost=13, name="weight_grad",
        )
        order.done(result)
        return result

    up_sum = Reduction(meta, weight_grad(second, hidden_other))
    down_sum = Reduction(meta, weight_grad(active_other, grad_low))

    pair_shape = jax.ShapeDtypeStruct((slots, TILE, width), LOW)
    pair_spec = whole((slots, TILE, width))

    second_grad_far = order.then(*second_grad_far)
    middle_grad, attn_grad, context_grad_own, context_grad_other, second_sums = call(
        middle_back_kernel, meta,
        (*second_grad, *second_grad_far, middle, grad_low, gains[1:2], out_weight, out_other),
        [ANYWHERE] * (2 * CHUNKS) + [rows_spec(width)] * 2 + [whole((1, width)), whole((shard, width)), whole((shard, width))],
        (row_f32, row_low, shape(cap, shard), shape(cap, shard), shape(8, width, F32)),
        (rows_out(width), rows_out(width), rows_out(shard), rows_out(shard), whole((8, width))),
        grid, parts_scratch(width) * 2, 18, "middle_back",
    )
    order.done(context_grad_other)


    branch_far = order.step(*branch_far)

    def attend_back(projected, attend, context_grad):
        projected, attend, context_grad = order.then(projected, attend, context_grad)
        grads, sums = call(
            functools.partial(attention_back_kernel, heads, shard, cell), meta,
            (projected, attend, context_grad),
            [whole((cap, 3 * shard)), whole((kept, cell, heads * cell)), whole((cap, shard))],
            (shape(cap, 3 * shard), shape(8, shard, F32)), (whole((cap, 3 * shard)), whole((8, shard))),
            (1,), (), 30, "attend_back",
        )
        order.done(grads)
        return grads, sums

    up_own = weight_grad(second, hidden_own)
    proj_grad_other, qkv_vec_other = attend_back(proj_other, attend_other, context_grad_other)
    up_sum.first(order, up_own)
    down_own = weight_grad(active_own, grad_low)

    def attn_grads(proj_grad, context):
        return weight_grad(proj_grad, normed, context, attn_grad, rows=width)

    attn_sum = Reduction(meta, attn_grads(proj_grad_other, context_other))
    down_sum.first(order, down_own)
    up_sum.second(order)
    proj_grad_own, qkv_vec_own = attend_back(proj_own, attend_own, context_grad_own)
    up_sum.third(order)
    down_sum.second(order)
    attn_own = attn_grads(proj_grad_own, context_own)
    attn_sum.first(order, attn_own)
    up_sum.fourth(order)
    down_sum.third(order)
    (first_grads,) = order.then(proj_grad_own)
    first_part = call(
        first_part_kernel, meta,
        (first_grads, proj_grad_other, qkv_own, qkv_other),
        [rows_spec(3 * shard)] * 2 + [whole((3 * shard, width)), ANYWHERE],
        part_shapes(cap, width), (ANYWHERE,) * CHUNKS,
        grid, [pltpu.VMEM((qkv_rows, width), LOW), pltpu.SemaphoreType.DMA((8,)), *out_scratch(width)],
        15, "first_part",
    )
    order.done(*first_part)
    first_far = swap_cores(first_part)
    up_sum.spread(order, 2)
    down_sum.fourth(order)
    attn_sum.second(order, 60)
    first_far = order.then(*first_far)
    input_pair, first_sums, table_grad = call(
        start_back_kernel, meta, (*first_part, *first_far, start, middle_grad, gains[0:1]),
        [ANYWHERE] * (2 * CHUNKS) + [rows_spec(width)] * 2 + [whole((1, width))],
        (pair_shape, shape(8, width, F32), shape(table.shape[0], width, F32)),
        (pair_spec, whole((8, width)), whole(table.shape)),
        grid, [row_scratch] + parts_scratch(width) * 2, 15, "start_back",
    )
    order.done(input_pair)
    up_sum.spread(order, 1)
    attn_sum.third(order)
    down_sum.spread(order, 2)
    rows_small = 8 + table.shape[0]
    vector_inputs = (first_sums, second_sums, table_grad, qkv_vec_own, qkv_vec_other, up_vecs)
    small, small_other = call(
        functools.partial(vectors_kernel, shard), meta, vector_inputs,
        [whole(value.shape) for value in vector_inputs],
        (shape(rows_small, width, F32),) * 2, (whole((rows_small, width)),) * 2, (1,), (), 2, "vectors",
    )
    small_far = swap(small_other, "tp", 2)
    input_far = swap(input_pair[kept:], "tp", 2)
    attn_sum.fourth(order)
    (small_far,) = order.step(small_far)
    small = small + small_far
    small_far = swap(small, "dp", 1)
    down_sum.spread(order, 1)
    middle_now, *branch_far = order.then(middle, *branch_far)
    (output_pair,) = call(
        finish_kernel, meta, (middle_now, *branch, *branch_far, out_rows[1:2]),
        [rows_spec(width)] + [ANYWHERE] * (2 * CHUNKS) + [whole((1, width))],
        (pair_shape,), (pair_spec,),
        grid, [row_scratch] + parts_scratch(width) * 2, 10, "finish",
    )
    order.done(output_pair)
    output_far = swap(output_pair[kept:], "tp", 2)
    attn_sum.spread(order, 2)
    (input_far,) = order.step(input_far)
    (up_total,) = up_sum.last_halves(order, (width,))
    (down_total,) = down_sum.last_halves(order, (width,))
    attn_sum.spread(order, 1)
    (small_far,) = order.step(small_far)
    small = small + small_far
    small_far = swap(small, "dp", 2)
    input_grad = place_cells(input_pair[:kept], order.then(input_far)[0])
    order.done(input_grad)
    (small_far,) = order.step(small_far)
    small = small + small_far
    small_far = swap(small, "dp", 4)
    cell_outputs = place_cells(output_pair[:kept], order.then(output_far)[0])
    order.done(cell_outputs)
    (small_far,) = order.step(small_far)
    small = later_groups(small + small_far)
    qkv_total, out_total = attn_sum.last_halves(order, (3 * shard, shard))

    return (
        cell_outputs,
        input_grad,
        small[0:2],
        small[2:4],
        qkv_total.reshape(3, shard, width).transpose(2, 0, 1),
        small[-2, : 2 * shard].reshape(2, shard),
        out_total,
        small[4:6],
        up_total,
        small[-1],
        down_total,
        small[6:-2],
    )


def solution(mesh):
    in_specs = (
        P("dp", "tp", None),
        P("dp", "tp", None),
        P("dp"),
        P("dp"),
        P(),
        P(),
        P(None, None, "tp"),
        P(None, "tp"),
        P("tp", None),
        P(),
        P(None, "tp"),
        P("tp"),
        P("tp", None),
        P(),
    )
    out_specs = (
        P("dp", "tp", None),
        P("dp", "tp", None),
        P(),
        P(),
        P(None, None, "tp"),
        P(None, "tp"),
        P("tp", None),
        P(),
        P(None, "tp"),
        P("tp"),
        P("tp", None),
        P(),
    )
    return jax.shard_map(
        on_device, mesh=mesh, in_specs=in_specs, out_specs=out_specs, check_vma=False
    )
```

```python
import functools
import math

import jax
import jax.numpy as jnp
from jax import lax
from jax.experimental import pallas as pl
from jax.experimental.pallas import tpu as pltpu
from jax.sharding import PartitionSpec as P

HEAD_DIM = 56
EPSILON = 1e-05
BLOCK = 256
META_BLOCKS = 8
TILE = 16
UNROLL = 4
F32 = jnp.float32
LOW = jnp.bfloat16
VMEM_BYTES = 56 * 1024 * 1024
FLOPS_PER_US = 450000000

NBLK, NCELL, BITS, TILE_SRC, TILE_SET, TILE_LEN, TILE_DST, CELL_OFF, CELL_ROWS = 0, 1, 2, 8, 136, 264, 392, 520, 552


def swap(value, axis, bit):
    count = lax.axis_size(axis)
    if value.ndim == 2 and value.shape[0] % TILE == 0:
        chunk = TILE if value.shape[0] // TILE % 128 else 2 * TILE
        tiled = value.reshape(value.shape[0] // chunk, chunk, value.shape[1])
        return swap(tiled, axis, bit).reshape(value.shape)
    return lax.ppermute(value, axis, [(i, i ^ bit) for i in range(count)])


CHUNKS = 2


def swap_cores(parts):
    return tuple(swap(part, "tp", 1) for part in parts)


class Sequence:
    def __init__(self):
        self.last = ()

    def then(self, *values):
        if not self.last:
            return values
        return lax.optimization_barrier((*values, *self.last))[: len(values)]

    def done(self, *values):
        self.last = (values[-1],)

    def step(self, *values):
        values = self.then(*values)
        self.last = (values[-1],)
        return values


def dot(a, b):
    return jnp.dot(a, b, preferred_element_type=F32)


def dot_nt(a, b):
    return lax.dot_general(a, b, (((1,), (1,)), ((), ())), preferred_element_type=F32)


def dot_tn(a, b):
    return lax.dot_general(a, b, (((0,), (0,)), ((), ())), preferred_element_type=F32)


def row_norm(rows):
    center = rows - jnp.mean(rows, axis=-1, keepdims=True)
    spread = jnp.mean(center * center, axis=-1, keepdims=True)
    scale = lax.rsqrt(spread + EPSILON)
    return center * scale, scale


def norm_back(grad, unit, scale, gain):
    scaled = grad * gain
    first = jnp.mean(scaled, axis=-1, keepdims=True)
    second = jnp.mean(scaled * unit, axis=-1, keepdims=True)
    return scale * (scaled - first - unit * second)


def whole(shape):
    zeros = (0,) * len(shape)
    return pl.BlockSpec(shape, lambda i, meta: zeros, pipeline_mode=pl.Buffered(1))


def rows_spec(width):
    return pl.BlockSpec((BLOCK, width), lambda i, meta: (jnp.minimum(i, meta[NBLK] - 1), 0))


PART_BLOCKS = META_BLOCKS // CHUNKS
PART_ROWS = PART_BLOCKS * BLOCK


def part_shapes(rows, width):
    return (jax.ShapeDtypeStruct((rows // CHUNKS, width), LOW),) * CHUNKS


def parts_scratch(width):
    return [pltpu.VMEM((META_BLOCKS * BLOCK, width), LOW), pltpu.SemaphoreType.DMA((CHUNKS,))]


def out_scratch(width):
    return [pltpu.VMEM((2, BLOCK, width), LOW), pltpu.SemaphoreType.DMA((2,))]


def each_part(parts, rows, sems):
    return [
        pltpu.make_async_copy(part, rows.at[pl.ds(at * PART_ROWS, PART_ROWS)], sems.at[at])
        for at, part in enumerate(parts)
    ]


def fetch_parts(step, blocks, *groups):
    for parts, rows, sems in groups:
        for at, copy in enumerate(each_part(parts, rows, sems)):

            @pl.when((step == 0) & (at * PART_BLOCKS < blocks))
            def _():
                copy.start()

    for parts, rows, sems in groups:
        for at, copy in enumerate(each_part(parts, rows, sems)):

            @pl.when(step == at * PART_BLOCKS)
            def _():
                copy.wait()


def block_of(step, rows):
    return rows[pl.ds(pl.multiple_of(step * BLOCK, BLOCK), BLOCK), :].astype(F32)


def put_part(step, last, value, parts, slots, sems):
    slot = lax.rem(step, 2)

    def copy_to(part, slot):
        begin = pl.multiple_of(lax.rem(step, PART_BLOCKS) * BLOCK, BLOCK)
        return pltpu.make_async_copy(slots.at[slot], part.at[pl.ds(begin, BLOCK)], sems.at[slot])

    @pl.when(step >= 2)
    def _():
        copy_to(parts[0], slot).wait()

    slots[slot] = value
    for at, part in enumerate(parts):

        @pl.when(step // PART_BLOCKS == at)
        def _():
            copy_to(part, slot).start()

    @pl.when(last)
    def _():
        copy_to(parts[0], slot).wait()

        @pl.when(step >= 1)
        def _():
            copy_to(parts[0], 1 - slot).wait()


def rows_out(width):
    return rows_spec(width)


def deep_spec(width):
    return pl.BlockSpec((2 * BLOCK, width), lambda i, meta: (jnp.minimum(i, (meta[NBLK] + 1) // 2 - 1), 0))


def rows_more(width):
    return pl.BlockSpec((BLOCK, width), lambda i, meta: (jnp.minimum(i, meta[NBLK]), 0))


def live_step(meta):
    return pl.when(pl.program_id(0) < meta[NBLK])


ANYWHERE = pl.BlockSpec(memory_space=pl.ANY)


def call(kernel, meta, operands, in_specs, out_shape, out_specs, grid, scratch=(), cost=5, name=None):
    return pl.pallas_call(
        kernel,
        grid_spec=pltpu.PrefetchScalarGridSpec(
            num_scalar_prefetch=1,
            grid=grid,
            in_specs=in_specs,
            out_specs=out_specs,
            scratch_shapes=list(scratch),
        ),
        out_shape=out_shape,
        compiler_params=pltpu.CompilerParams(
            dimension_semantics=("arbitrary",) * len(grid), vmem_limit_bytes=VMEM_BYTES
        ),
        cost_estimate=pl.CostEstimate(flops=cost * FLOPS_PER_US, bytes_accessed=0, transcendentals=0),
        name=name,
    )(meta, *operands)


def load_tiles(sources, tiles, sems, count):
    copies = [
        pltpu.make_async_copy(source, tiles.at[pl.ds(at * count, count)], sems.at[at])
        for at, source in enumerate(sources)
    ]
    for copy in copies:
        copy.start()
    for copy in copies:
        copy.wait()


def begin_kernel(count, meta, a0, a1, a2, a3, table, gain, shift, weight, bias, start, normed, projected, tiles, sems):
    step = pl.program_id(0)

    @pl.when(step == 0)
    def _():
        load_tiles((a0, a1, a2, a3), tiles, sems, count)

    @pl.when(step < meta[NBLK])
    def _():
        for j in range(BLOCK // TILE):
            at = step * (BLOCK // TILE) + j
            tile = tiles[meta[TILE_SRC + at]].astype(F32)
            start[j * TILE : (j + 1) * TILE, :] = tile + table[pl.ds(meta[TILE_SET + at], 1), :]
        unit, _ = row_norm(start[...])
        low = (unit * gain[...] + shift[...]).astype(LOW)
        normed[...] = low
        projected[...] = (dot_nt(low, weight[...]) + bias[...]).astype(LOW)

    @pl.when(step == meta[NBLK])
    def _():
        projected[...] = jnp.zeros_like(projected)


def project_kernel(meta, normed, eighths, bias, projected, weight, sems):
    step = pl.program_id(0)

    @pl.when(step == 0)
    def _():
        load_eighths(eighths, [weight], sems)

    @pl.when(step < meta[NBLK])
    def _():
        projected[...] = (dot_nt(normed[...], weight[: bias.shape[1], :]) + bias[...]).astype(LOW)

    @pl.when(step == meta[NBLK])
    def _():
        projected[...] = jnp.zeros_like(projected)


def head_masks(cell, heads, shard):
    lane = lax.broadcasted_iota(jnp.int32, (cell, shard), 1)
    return [(lane >= h * HEAD_DIM) & (lane < (h + 1) * HEAD_DIM) for h in range(heads)]


def spread_heads(rows, masks, heads, low, high):
    part = rows[:, low:high]
    zero = jnp.zeros_like(part)
    return jnp.concatenate([jnp.where(masks[h][:, low:high], part, zero) for h in heads], axis=0)


def head_groups(heads, shard):
    groups = []
    at = 0
    while at < heads:
        end = min(at + 4, heads)
        low = at * HEAD_DIM // 128 * 128
        high = min(-(-end * HEAD_DIM // 128) * 128, shard)
        groups.append((tuple(range(at, end)), low, high))
        at = end
    return groups


def attention_kernel(heads, shard, cell, meta, projected, context, attend, same_head):
    context[...] = jnp.zeros_like(context)
    masks = head_masks(cell, heads, shard)
    scale = 1.0 / math.sqrt(HEAD_DIM)
    span = same_head.shape[0]
    head_of = [lax.broadcasted_iota(jnp.int32, (span, span), axis) // cell for axis in (0, 1)]
    same_head[...] = jnp.where(head_of[0] == head_of[1], 1.0, 0.0).astype(LOW)

    def one(index):
        at = pl.multiple_of(meta[CELL_OFF + index] * TILE, TILE)
        queries = projected[pl.ds(at, cell), 0:shard]
        keys = projected[pl.ds(at, cell), shard : 2 * shard]
        values = projected[pl.ds(at, cell), 2 * shard : 3 * shard]
        total = None
        for group, low, high in head_groups(heads, shard):
            count = len(group) * cell
            scores = dot_nt(queries[:, low:high], spread_heads(keys, masks, group, low, high)) * scale
            row = lax.broadcasted_iota(jnp.int32, (cell, count), 0)
            lane = lax.broadcasted_iota(jnp.int32, (cell, count), 1)
            scores = jnp.where(row >= lax.rem(lane, cell), scores, -1e30)
            shifted = []
            for pair in range(0, len(group), 2):
                both = scores[:, pair * cell : min(pair + 2, len(group)) * cell]
                if pair + 1 < len(group):
                    left = lax.broadcasted_iota(jnp.int32, both.shape, 1) < cell
                    top_left = jnp.max(jnp.where(left, both, -1e30), axis=1, keepdims=True)
                    top_right = jnp.max(jnp.where(left, -1e30, both), axis=1, keepdims=True)
                    shifted.append(both - jnp.where(left, top_left, top_right))
                else:
                    shifted.append(both - jnp.max(both, axis=1, keepdims=True))
            weights = jnp.exp(jnp.concatenate(shifted, axis=1) if len(shifted) > 1 else shifted[0])
            if len(group) > 1:
                sums = dot(weights.astype(LOW), same_head[:count, :count])
            else:
                sums = jnp.sum(weights, axis=1, keepdims=True)
            probs = (weights * (1.0 / sums)).astype(LOW)
            first = group[0] * cell
            attend[index, :, first : first + count] = probs
            part = dot(probs, spread_heads(values, masks, group, low, high))
            if high - low < shard:
                part = jnp.pad(part, ((0, 0), (low, shard - high)))
            total = part if total is None else total + part
        context[pl.ds(at, cell), :] = total.astype(LOW)

    def body(step, carry):
        for place in range(UNROLL):
            one(UNROLL * step + place)
        return carry

    lax.fori_loop(0, (meta[NCELL] + UNROLL - 1) // UNROLL, body, 0)


def attention_back_kernel(heads, shard, cell, meta, projected, attend, context_grad, result, sums):
    result[...] = jnp.zeros_like(result)
    sums[...] = jnp.zeros_like(sums)
    masks = head_masks(cell, heads, shard)
    scale = 1.0 / math.sqrt(HEAD_DIM)
    row = lax.broadcasted_iota(jnp.int32, (cell, shard), 0)
    left = lax.broadcasted_iota(jnp.int32, (cell, 2 * cell), 1) < cell

    def fold(stacked, group, low, high):
        total = None
        for place, h in enumerate(group):
            part = jnp.where(masks[h][:, low:high], stacked[place * cell : (place + 1) * cell, :], 0.0)
            total = part if total is None else total + part
        return total

    def widen(part, low, high):
        return jnp.pad(part, ((0, 0), (low, shard - high))) if high - low < shard else part

    def one(index):
        at = pl.multiple_of(meta[CELL_OFF + index] * TILE, TILE)
        queries = projected[pl.ds(at, cell), 0:shard]
        keys = projected[pl.ds(at, cell), shard : 2 * shard]
        values = projected[pl.ds(at, cell), 2 * shard : 3 * shard]
        grads = context_grad[pl.ds(at, cell), :]
        grads = jnp.where(row < meta[CELL_ROWS + index], grads, jnp.zeros_like(grads))
        query_total = key_total = value_total = None
        for group, low, high in head_groups(heads, shard):
            first = group[0] * cell
            probs = attend[index, :, first : first + len(group) * cell]
            attend_grad = dot_nt(grads[:, low:high], spread_heads(values, masks, group, low, high))
            parts = []
            for pair in range(0, len(group), 2):
                if pair + 1 < len(group):
                    span = slice(pair * cell, (pair + 2) * cell)
                    weights = probs[:, span].astype(F32)
                    both = attend_grad[:, span]
                    product = weights * both
                    sum_left = jnp.sum(jnp.where(left, product, 0.0), axis=1, keepdims=True)
                    sum_right = jnp.sum(jnp.where(left, 0.0, product), axis=1, keepdims=True)
                    parts.append((product - weights * jnp.where(left, sum_left, sum_right)).astype(LOW))
                else:
                    span = slice(pair * cell, (pair + 1) * cell)
                    weights = probs[:, span].astype(F32)
                    product = weights * attend_grad[:, span]
                    total = jnp.sum(product, axis=1, keepdims=True)
                    parts.append((product - weights * total).astype(LOW))
            score_grad = jnp.concatenate(parts, axis=1) if len(parts) > 1 else parts[0]
            query_part = dot(score_grad, spread_heads(keys, masks, group, low, high)) * scale
            key_part = fold(dot_tn(score_grad, queries[:, low:high]), group, low, high) * scale
            value_part = fold(dot_tn(probs, grads[:, low:high]), group, low, high)
            query_part, key_part, value_part = (widen(p, low, high) for p in (query_part, key_part, value_part))
            if query_total is None:
                query_total, key_total, value_total = query_part, key_part, value_part
            else:
                query_total, key_total, value_total = (
                    query_total + query_part,
                    key_total + key_part,
                    value_total + value_part,
                )
        for place, part in enumerate((query_total, key_total, value_total)):
            low_part = part.astype(LOW)
            result[pl.ds(at, cell), place * shard : (place + 1) * shard] = low_part
            sums[place : place + 1, :] += jnp.sum(low_part.astype(F32), axis=0, keepdims=True)

    def body(step, carry):
        one(2 * step)
        one(2 * step + 1)
        return carry

    lax.fori_loop(0, (meta[NCELL] + 1) // 2, body, 0)


def out_project_kernel(meta, a, b, weight_a, weight_b, *refs):
    *parts, slots, sems = refs
    step = pl.program_id(0)

    @live_step(meta)
    def _():
        value = (dot(a[...], weight_a[...]) + dot(b[...], weight_b[...])).astype(LOW)
        put_part(step, step == meta[NBLK] - 1, value, parts, slots, sems)


def first_part_kernel(meta, a, b, weight_a, eighths, *refs):
    step = pl.program_id(0)
    *parts, weight_b, weight_sems, slots, sems = refs

    @pl.when(step == 0)
    def _():
        load_eighths(eighths, [weight_b], weight_sems)

    @live_step(meta)
    def _():
        value = (dot(a[...], weight_a[...]) + dot(b[...], weight_b[: b.shape[1], :])).astype(LOW)
        put_part(step, step == meta[NBLK] - 1, value, parts, slots, sems)


def gelu_pair(hidden):
    chance = 0.5 * (1.0 + lax.erf(hidden * (1.0 / math.sqrt(2.0))))
    slope = chance + hidden * (jnp.exp(-0.5 * hidden * hidden) * (1.0 / math.sqrt(2.0 * math.pi)))
    return hidden * chance, slope


def mlp_block(second, product, up, bias, down, active, hidden_grad, bias_grad):
    hidden = dot(second, up[...]) + bias[...]
    value, slope = gelu_pair(hidden)
    low = value.astype(LOW)
    active[...] = low
    back = (slope * product).astype(LOW)
    hidden_grad[...] = back
    bias_grad[...] += jnp.sum(back.astype(F32), axis=0, keepdims=True)
    return dot(low, down[...]), dot_nt(back, up[...])


def mlp_kernel(count, meta, start, *refs):
    near_parts, far_parts, refs = refs[:CHUNKS], refs[CHUNKS : 2 * CHUNKS], refs[2 * CHUNKS :]
    bias_row, gain, shift, a0, a1, a2, a3, up, up_bias, down, other_up, other_bias, eighths, *refs = refs
    middle, second, grad, active, hidden_grad, other_active, other_hidden, *refs = refs
    branch, second_grad, refs = refs[:CHUNKS], refs[CHUNKS : 2 * CHUNKS], refs[2 * CHUNKS :]
    bias_grad, tiles, sems, near_rows, near_sems, far_rows, far_sems, *refs = refs
    other_down, other_sems, branch_slots, branch_sems, grad_slots, grad_sems = refs
    step = pl.program_id(0)
    copies = eighths_copies(eighths, [other_down], other_sems)

    @pl.when(step == 0)
    def _():
        load_tiles((a0, a1, a2, a3), tiles, sems, count)
        for copy in copies:
            copy.start()
        bias_grad[...] = jnp.zeros_like(bias_grad)

    @live_step(meta)
    def _():
        last = step == meta[NBLK] - 1
        fetch_parts(step, meta[NBLK], (near_parts, near_rows, near_sems), (far_parts, far_rows, far_sems))
        inner = lax.broadcasted_iota(jnp.int32, (TILE, 1), 0)
        for j in range(BLOCK // TILE):
            at = step * (BLOCK // TILE) + j
            tile = tiles[meta[TILE_SRC + at]]
            grad[j * TILE : (j + 1) * TILE, :] = jnp.where(inner < meta[TILE_LEN + at], tile, jnp.zeros_like(tile))

        @pl.when(step == 0)
        def _():
            for copy in copies:
                copy.wait()

        own_product = dot_nt(grad[...], down[...])
        other_product = dot_nt(grad[...], other_down[...])
        rows = start[...] + (block_of(step, near_rows) + block_of(step, far_rows)) + bias_row[...]
        middle[...] = rows
        unit, _ = row_norm(rows)
        low = (unit * gain[...] + shift[...]).astype(LOW)
        second[...] = low
        own = mlp_block(low, own_product, up, up_bias, down, active, hidden_grad, bias_grad.at[0:1])
        other = mlp_block(
            low, other_product, other_up, other_bias, other_down, other_active, other_hidden, bias_grad.at[1:2]
        )
        put_part(step, last, (own[1] + other[1]).astype(LOW), second_grad, grad_slots, grad_sems)
        put_part(step, last, (own[0] + other[0]).astype(LOW), branch, branch_slots, branch_sems)


def weight_grad_kernel(pairs, meta, *refs):
    step = pl.program_id(0)
    result, total = refs[2 * pairs :]
    blocks = meta[NBLK] - 2 * step

    def add(count):
        base = 0
        for a, b in zip(refs[: 2 * pairs : 2], refs[1 : 2 * pairs : 2]):
            rows = slice(base, base + a.shape[1])
            part = dot_tn(a[:count, :], b[:count, :])
            base += a.shape[1]

            @pl.when(step == 0)
            def _():
                total[rows, :] = part

            @pl.when(step > 0)
            def _():
                total[rows, :] += part

    @pl.when(blocks >= 2)
    def _():
        add(2 * BLOCK)

    @pl.when(blocks == 1)
    def _():
        add(BLOCK)

    @pl.when((blocks > 0) & (blocks <= 2))
    def _():
        result[...] = total[...].astype(LOW)


def middle_back_kernel(meta, *refs):
    near_parts, far_parts, refs = refs[:CHUNKS], refs[CHUNKS : 2 * CHUNKS], refs[2 * CHUNKS :]
    middle, grad, gain, out_a, out_b, middle_grad, attn_grad, context_a, context_b, sums, *refs = refs
    near_rows, near_sems, far_rows, far_sems = refs
    step = pl.program_id(0)

    @pl.when(step == 0)
    def _():
        sums[...] = jnp.zeros_like(sums)

    @live_step(meta)
    def _():
        fetch_parts(step, meta[NBLK], (near_parts, near_rows, near_sems), (far_parts, far_rows, far_sems))
        unit, scale = row_norm(middle[...])
        second_grad = block_of(step, near_rows) + block_of(step, far_rows)
        grad_rows = grad[...].astype(F32)
        total = grad_rows + norm_back(second_grad, unit, scale, gain[...])
        middle_grad[...] = total
        low = total.astype(LOW)
        attn_grad[...] = low
        context_a[...] = dot_nt(low, out_a[...]).astype(LOW)
        context_b[...] = dot_nt(low, out_b[...]).astype(LOW)
        for at, rows in enumerate((second_grad * unit, second_grad, total, grad_rows)):
            sums[at : at + 1, :] += jnp.sum(rows, axis=0, keepdims=True)


def scatter_tiles(meta, step, rows, out):
    for j in range(BLOCK // TILE):
        place = meta[TILE_DST + step * (BLOCK // TILE) + j]

        @pl.when(place >= 0)
        def _():
            out[place] = rows[j * TILE : (j + 1) * TILE, :].astype(LOW)


def start_back_kernel(meta, *refs):
    near_parts, far_parts, refs = refs[:CHUNKS], refs[CHUNKS : 2 * CHUNKS], refs[2 * CHUNKS :]
    start, middle_grad, gain, out, sums, table, rows, near_rows, near_sems, far_rows, far_sems = refs
    step = pl.program_id(0)

    @pl.when(step == 0)
    def _():
        out[...] = jnp.zeros_like(out)
        sums[...] = jnp.zeros_like(sums)
        table[...] = jnp.zeros_like(table)

    @live_step(meta)
    def _():
        fetch_parts(step, meta[NBLK], (near_parts, near_rows, near_sems), (far_parts, far_rows, far_sems))
        unit, scale = row_norm(start[...])
        first_grad = block_of(step, near_rows) + block_of(step, far_rows)
        rows[...] = middle_grad[...] + norm_back(first_grad, unit, scale, gain[...])
        for at, value in enumerate((first_grad * unit, first_grad)):
            sums[at : at + 1, :] += jnp.sum(value, axis=0, keepdims=True)
        for j in range(BLOCK // TILE):
            at = meta[TILE_SET + step * (BLOCK // TILE) + j]
            table[pl.ds(at, 1), :] += jnp.sum(rows[j * TILE : (j + 1) * TILE, :], axis=0, keepdims=True)
        scatter_tiles(meta, step, rows, out)


def finish_kernel(meta, middle, *refs):
    near_parts, far_parts, refs = refs[:CHUNKS], refs[CHUNKS : 2 * CHUNKS], refs[2 * CHUNKS :]
    bias_row, out, rows, near_rows, near_sems, far_rows, far_sems = refs
    step = pl.program_id(0)

    @pl.when(step == 0)
    def _():
        out[...] = jnp.zeros_like(out)

    @live_step(meta)
    def _():
        fetch_parts(step, meta[NBLK], (near_parts, near_rows, near_sems), (far_parts, far_rows, far_sems))
        rows[...] = middle[...] + (block_of(step, near_rows) + block_of(step, far_rows)) + bias_row[...]
        inner = lax.broadcasted_iota(jnp.int32, (TILE, 1), 0)
        for j in range(BLOCK // TILE):
            at = step * (BLOCK // TILE) + j
            place = meta[TILE_DST + at]

            @pl.when(place >= 0)
            def _():
                out[place] = jnp.where(inner < meta[TILE_LEN + at], rows[j * TILE : (j + 1) * TILE, :], 0.0).astype(LOW)


def vectors_kernel(shard, meta, first, second, table, own, other, up, small, small_other):
    for out, qkv, at in ((small, own, 0), (small_other, other, 1)):
        out[0:1, :] = first[0:1, :]
        out[1:2, :] = second[0:1, :]
        out[2:3, :] = first[1:2, :]
        out[3:6, :] = second[1:4, :]
        out[6:38, :] = table[...]
        out[38:40, :] = jnp.zeros((2, out.shape[1]), F32)
        out[38:39, :shard] = qkv[0:1, :]
        out[38:39, shard : 2 * shard] = qkv[2:3, :]
        out[39:40, :] = up[at : at + 1, :]


def window_size(half):
    return -(-half // (4 * TILE)) * TILE


def window_at(low, high, half):
    size = window_size(half)
    return low * (half - 2 * size) + high * size


def run_copies(copies):
    for copy in copies:
        copy.start()
    for copy in copies:
        copy.wait()


def join_kernel(extra, level, meta, mine, far, out, sems):
    rows = mine.shape[0]

    def put(first, second):
        run_copies(
            [
                pltpu.make_async_copy(first, out.at[pl.ds(0, rows)], sems.at[0]),
                pltpu.make_async_copy(second.at[pl.ds(extra, rows - extra)], out.at[pl.ds(rows, rows - extra)], sems.at[1]),
            ]
        )

    @pl.when(meta[BITS + level] == 0)
    def _():
        put(mine, far)

    @pl.when(meta[BITS + level] == 1)
    def _():
        put(far, mine)


def join(meta, mine, far, level, total):
    rows, width = mine.shape
    (result,) = call(
        functools.partial(join_kernel, 2 * rows - total, level), meta, (mine, far), [ANYWHERE] * 2,
        (jax.ShapeDtypeStruct((total, width), LOW),), (whole((total, width)),),
        (1,), [pltpu.SemaphoreType.DMA((2,))], cost=3, name="join",
    )
    return result


def gather_eighths(piece):
    groups = lax.axis_size("dp")
    spans = [list(range(at, at + 8)) for at in range(0, groups, 8)] if groups > 8 else None
    tiled = piece.reshape(piece.shape[0] // TILE, TILE, piece.shape[1])
    whole_block = lax.all_gather(tiled, "dp", axis=0, tiled=True, axis_index_groups=spans)
    return whole_block.reshape(8 * piece.shape[0], piece.shape[1])


def eighths_copies(gathered, scratches, sems):
    copies = []
    for at, scratch in enumerate(scratches):
        half = scratch.shape[0] // 2
        size = window_size(half)
        for group in range(8):
            low, high = (group >> 1) & 1, group >> 2
            skip = 4 * size - half if (low, high) == (1, 0) else 0
            begin = (group & 1) * half + window_at(low, high, half) + skip
            copies.append(
                pltpu.make_async_copy(
                    gathered.at[pl.ds((group * len(scratches) + at) * size + skip, size - skip)],
                    scratch.at[pl.ds(begin, size - skip)],
                    sems.at[8 * at + group],
                )
            )
    return copies


def load_eighths(gathered, scratches, sems):
    copies = eighths_copies(gathered, scratches, sems)
    for copy in copies:
        copy.start()
    for copy in copies:
        copy.wait()


def first_sum_kernel(meta, own, far, sent):
    sent[...] = (own[...].astype(F32) + far[...].astype(F32)).astype(LOW)


def first_sum(meta, own, far):
    rows, width = own.shape
    half = rows // 2
    steps = next(count for count in (5, 4, 3, 1) if half % (count * TILE) == 0)
    block = half // steps
    source = pl.BlockSpec((block, width), lambda i, meta: ((1 - meta[BITS]) * steps + i, 0))
    (sent,) = call(
        first_sum_kernel, meta, (own, far), [source, source], (jax.ShapeDtypeStruct((half, width), LOW),),
        (pl.BlockSpec((block, width), lambda i, meta: (i, 0)),), (steps,), cost=5, name="first_sum",
    )
    return sent


def second_sum_kernel(half, meta, mine, far, arrived, kept, sent):
    size = 2 * window_size(half)
    bit = meta[BITS + 1]
    for out, place in ((kept, bit), (sent, 1 - bit)):
        rows = pl.ds(pl.multiple_of(place * (half - size), TILE), size)
        total = mine[rows, :].astype(F32) + far[rows, :].astype(F32) + arrived[rows, :].astype(F32)
        out[...] = total.astype(out.dtype)


def second_sum(meta, own, far, arrived, cost):
    half, width = arrived.shape
    size = 2 * window_size(half)
    kept = pl.BlockSpec((half, width), lambda i, meta: (meta[BITS], 0), pipeline_mode=pl.Buffered(1))
    return call(
        functools.partial(second_sum_kernel, half), meta, (own, far, arrived), [kept, kept, whole((half, width))],
        (jax.ShapeDtypeStruct((size, width), F32), jax.ShapeDtypeStruct((size, width), LOW)),
        (whole((size, width)),) * 2, (1,), cost=cost, name="second_sum",
    )


def third_sum_kernel(count, meta, *refs):
    kept, arrived, own, sent = refs[:count], refs[count], refs[count + 1 : 2 * count + 1], refs[-1]
    size = own[0].shape[0]
    bit = meta[BITS + 2]
    for at in range(count):
        for place in (bit, 1 - bit):
            begin = pl.multiple_of(place * size, TILE)
            far = arrived[pl.ds(pl.multiple_of(2 * at * size + begin, TILE), size), :].astype(F32)
            total = kept[at][pl.ds(begin, size), :] + far
            if place is bit:
                own[at][...] = total
            else:
                sent[at * size : (at + 1) * size, :] = total.astype(LOW)


def third_sum(meta, kept, arrived, cost=3):
    count = len(kept)
    size, width = kept[0].shape[0] // 2, kept[0].shape[1]
    *own, sent = call(
        functools.partial(third_sum_kernel, count), meta, (*kept, arrived),
        [whole(each.shape) for each in (*kept, arrived)],
        (jax.ShapeDtypeStruct((size, width), F32),) * count + (jax.ShapeDtypeStruct((count * size, width), LOW),),
        (whole((size, width)),) * count + (whole((count * size, width)),), (1,), cost=cost, name="third_sum",
    )
    return own, sent


def fourth_sum_kernel(count, meta, *refs):
    own, arrived, outs = refs[:count], refs[count], refs[count + 1 :]
    size = own[0].shape[0]
    for at, out in enumerate(outs):
        out[...] = (own[at][...] + arrived[at * size : (at + 1) * size, :].astype(F32)).astype(out.dtype)


def fourth_sum(meta, own, arrived, kinds):
    shape = own[0].shape
    return call(
        functools.partial(fourth_sum_kernel, len(own)), meta, (*own, arrived),
        [whole(each.shape) for each in (*own, arrived)],
        tuple(jax.ShapeDtypeStruct(shape, kind) for kind in kinds), (whole(shape),) * len(own),
        (1,), cost=3, name="fourth_sum",
    )


def widen_rows_kernel(meta, mine, far, *outs):
    half = mine.shape[0]

    def put(lower, upper):
        base = 0
        for out in outs:
            count = out.shape[0]
            split = min(max(half - base, 0), count)
            if split:
                out[:split, :] = lower[base : base + split, :].astype(F32)
            if split < count:
                begin = base + split - half
                out[split:, :] = upper[begin : begin + count - split, :].astype(F32)
            base += count

    @pl.when(meta[BITS] == 0)
    def _():
        put(mine, far)

    @pl.when(meta[BITS] == 1)
    def _():
        put(far, mine)


def widen_rows(meta, mine, far, rows):
    half, width = mine.shape
    return call(
        widen_rows_kernel, meta, (mine, far), [whole((half, width))] * 2,
        tuple(jax.ShapeDtypeStruct((count, width), F32) for count in rows),
        tuple(whole((count, width)) for count in rows), (1,), name="widen_rows",
    )


def later_groups(value):
    level = 3
    while (1 << level) < lax.axis_size("dp"):
        value = (value.astype(F32) + swap(value, "dp", 1 << level).astype(F32)).astype(value.dtype)
        level += 1
    return value


class Reduction:
    def __init__(self, meta, other):
        self.meta = meta
        self.far = swap(other, "tp", 2)

    def arrive(self, order):
        (self.far,) = order.step(self.far)

    def first(self, order, own):
        self.own, self.far = order.then(own, self.far)
        sent = first_sum(self.meta, self.own, self.far)
        order.done(sent)
        self.arrived = swap(sent, "dp", 1)

    def wait_second(self, order):
        (self.arrived,) = order.step(self.arrived)

    def second(self, order, cost=4):
        (arrived,) = order.then(self.arrived)
        self.half = arrived.shape[0]
        self.kept, sent = second_sum(self.meta, self.own, self.far, arrived, cost)
        order.done(sent)
        self.arrived = swap(sent, "dp", 2)

    def third(self, order, cost=3):
        (arrived,) = order.then(self.arrived)
        self.kept, sent = third_sum(self.meta, [self.kept], arrived, cost)
        order.done(sent)
        self.arrived = swap(sent, "dp", 4)

    def fourth(self, order):
        (arrived,) = order.then(self.arrived)
        (piece,) = fourth_sum(self.meta, self.kept, arrived, (LOW,))
        order.done(piece)
        piece = later_groups(piece)
        self.mine, self.far = piece, swap(piece, "dp", 4)

    def spread(self, order, level):
        mine, far = order.then(self.mine, self.far)
        rows = 2 * mine.shape[0] if level == 2 else self.half
        self.mine = join(self.meta, mine, far, level, rows)
        order.done(self.mine)
        self.far = swap(self.mine, "dp", 1 << (level - 1))

    def last_halves(self, order, rows):
        mine, far = order.then(self.mine, self.far)
        results = widen_rows(self.meta, mine, far, rows)
        order.done(results[0])
        return results


def eighth(block):
    half = block.shape[0] // 2
    index = lax.axis_index("dp")
    at = (index & 1) * half + window_at((index >> 1) & 1, (index >> 2) & 1, half)
    return lax.dynamic_slice_in_dim(block, at, window_size(half), 0)


def on_device(
    cell_inputs,
    out_grad,
    lengths,
    datasets,
    norm_gain,
    norm_bias,
    qkv_weight,
    qv_bias,
    out_weight,
    out_bias,
    up_weight,
    up_bias,
    down_weight,
    dataset_table,
):
    slots, quarter, width = cell_inputs.shape
    tensor = lax.axis_index("tp")
    chip = tensor // 2
    core = tensor % 2
    blocks_per_cell = lax.axis_size("tp")
    cell = quarter * blocks_per_cell
    shard = qkv_weight.shape[2]
    ff = up_weight.shape[1]
    heads = shard // HEAD_DIM
    kept = slots // 2
    tile_cap = META_BLOCKS * BLOCK // TILE
    cap = META_BLOCKS * BLOCK
    grid = (META_BLOCKS,)
    group = lax.axis_index("dp")
    index = jnp.arange(kept, dtype=jnp.int32)

    def mine_of(rows):
        pairs = rows.reshape(kept, 2, *rows.shape[1:])
        mine = lax.dynamic_index_in_dim(pairs, chip, 1, keepdims=False)
        theirs = lax.dynamic_index_in_dim(pairs, 1 - chip, 1, keepdims=False)
        return mine, theirs

    def place_cells(mine, other):
        even = jnp.where(chip == 0, mine, other)
        odd = jnp.where(chip == 0, other, mine)
        return jnp.stack([even, odd], axis=1).reshape(slots, quarter, width)

    cell_lengths, _ = mine_of(lengths)
    cell_sets, _ = mine_of(datasets)
    cell_tiles = (cell_lengths + TILE - 1) // TILE
    ends = jnp.sum(jnp.where(index[None, :] <= index[:, None], cell_tiles[None, :], 0), axis=1)
    begins = ends - cell_tiles
    tile_count = ends[-1]
    tile = jnp.arange(tile_cap, dtype=jnp.int32)
    owner = jnp.sum((ends[None, :] <= tile[:, None]).astype(jnp.int32), axis=1)
    live = tile < tile_count
    owned = (owner[:, None] == index[None, :]) & live[:, None]

    def of_owner(values):
        return jnp.sum(jnp.where(owned, values[None, :], 0), axis=1)

    block = tile - of_owner(begins)
    shelf = jnp.where(block // 2 == chip, 0, kept) + owner
    tile_src = jnp.where(live, jnp.where(block % 2 == core, 0, slots) + shelf, 0)
    tile_set = of_owner(cell_sets)
    tile_len = jnp.clip(of_owner(cell_lengths) - block * TILE, 0, TILE) * live
    tile_dst = jnp.where(live & (block % 2 == core), shelf, -1)
    cell_count = jnp.sum((cell_lengths > 0).astype(jnp.int32))
    block_count = (tile_count + BLOCK // TILE - 1) // (BLOCK // TILE)
    grid = (META_BLOCKS,)
    head = jnp.stack([block_count, cell_count, group & 1, (group >> 1) & 1, (group >> 2) & 1])

    meta = jnp.concatenate(
        [head, jnp.zeros((3,), jnp.int32), tile_src, tile_set, tile_len, tile_dst, begins, cell_tiles * TILE]
    ).astype(jnp.int32)

    order = Sequence()
    qkv_own = qkv_weight.transpose(1, 2, 0).reshape(3 * shard, width)
    qkv_rows = -(-3 * shard // (2 * TILE)) * 2 * TILE
    vectors = jnp.concatenate([qv_bias.reshape(-1), up_bias])
    piece_source, cells_now = lax.optimization_barrier(
        (eighth(jnp.pad(qkv_own, ((0, qkv_rows - 3 * shard), (0, 0)))), cell_inputs)
    )
    qkv_piece = swap(piece_source, "tp", 2)
    in_mine, in_theirs = mine_of(cells_now)
    in_other = swap(in_theirs, "tp", 2)
    in_far = swap(in_mine, "tp", 1)
    head_rows = jnp.pad(vectors, (0, 2 * width - vectors.shape[0])).reshape(2, width)
    out_and_vectors = jnp.concatenate([out_weight, head_rows, jnp.zeros((6, width), LOW)], axis=0)
    down_piece, out_and_vectors, grad_now, _ = lax.optimization_barrier(
        (eighth(down_weight), out_and_vectors, out_grad, in_theirs)
    )
    down_piece = swap(down_piece, "tp", 2)
    out_and_vectors = swap(out_and_vectors, "tp", 2)
    grad_mine, grad_theirs = mine_of(grad_now)
    meta, qkv_own, grad_mine, grad_theirs = order.step(meta, qkv_own, grad_mine, grad_theirs)
    (qkv_piece,) = order.step(qkv_piece)
    qkv_other = gather_eighths(qkv_piece)
    in_far, in_other = order.step(in_far, in_other)
    in_other_far = swap(in_other, "tp", 1)
    grad_other = swap(order.then(grad_theirs)[0], "tp", 2)
    (in_other_far,) = order.step(in_other_far)

    def biases(vector):
        zeros = jnp.zeros((shard,), LOW)
        qkv_row = jnp.concatenate([vector[:shard], zeros, vector[shard : 2 * shard]])
        return qkv_row.astype(F32)[None], vector[2 * shard :].astype(F32)[None]

    qkv_bias_own, up_bias_own = biases(vectors)
    gains = norm_gain.astype(F32)
    shifts = norm_bias.astype(F32)
    out_rows = out_bias.astype(F32)
    table = dataset_table.astype(F32)

    def shape(rows, cols, kind=LOW):
        return jax.ShapeDtypeStruct((rows, cols), kind)

    row_f32, row_low = shape(cap, width, F32), shape(cap, width)
    row_scratch = pltpu.VMEM((BLOCK, width), F32)
    tile_scratch = [pltpu.VMEM((2 * slots, TILE, width), LOW), pltpu.SemaphoreType.DMA((4,))]

    start, normed, proj_own = call(
        functools.partial(begin_kernel, kept), meta,
        (in_mine, in_other, in_far, in_other_far, table, gains[0:1], shifts[0:1], qkv_own, qkv_bias_own),
        [ANYWHERE] * 4 + [whole(table.shape), whole((1, width)), whole((1, width)), whole((3 * shard, width)), whole((1, 3 * shard))],
        (row_f32, row_low, shape(cap, 3 * shard)),
        (rows_out(width), rows_out(width), rows_more(3 * shard)),
        grid, tile_scratch, 15, "begin",
    )
    order.done(proj_own)

    def attend_shard(projected):
        (projected,) = order.then(projected)
        context, attend = call(
            functools.partial(attention_kernel, heads, shard, cell), meta, (projected,),
            [whole((cap, 3 * shard))],
            (shape(cap, shard), jax.ShapeDtypeStruct((kept, cell, heads * cell), LOW)),
            (whole((cap, shard)), whole((kept, cell, heads * cell))),
            (1,), [pltpu.VMEM((4 * cell, 4 * cell), LOW)], 4, "attend",
        )
        order.done(context)
        return context, attend

    down_piece, out_and_vectors = order.step(down_piece, out_and_vectors)
    down_other = gather_eighths(down_piece)
    grad_now, up_now = order.then(grad_mine, up_weight)
    up_other = swap(up_now, "tp", 2)
    grad_far = swap(grad_now, "tp", 1)
    context_own, attend_own = attend_shard(proj_own)
    grad_far, grad_other = order.step(grad_far, grad_other)
    out_other = out_and_vectors[:shard]
    vectors_other = out_and_vectors[shard : shard + 2].reshape(-1)[: vectors.shape[0]]
    normed_now, qkv_now = order.then(normed, qkv_other)
    qkv_bias_other, up_bias_other = biases(vectors_other)
    (proj_other,) = call(
        project_kernel, meta, (normed_now, qkv_now, qkv_bias_other),
        [rows_spec(width), ANYWHERE, whole((1, 3 * shard))],
        (shape(cap, 3 * shard),), (rows_more(3 * shard),),
        grid, [pltpu.VMEM((qkv_rows, width), LOW), pltpu.SemaphoreType.DMA((8,))],
        6, "project",
    )
    order.done(proj_other)
    context_other, attend_other = attend_shard(proj_other)
    grad_other_far = swap(grad_other, "tp", 1)
    (context_now,) = order.then(context_other)
    attn_part = call(
        out_project_kernel, meta, (context_own, context_now, out_weight, out_other),
        [rows_spec(shard), rows_spec(shard), whole((shard, width)), whole((shard, width))],
        part_shapes(cap, width), (ANYWHERE,) * CHUNKS,
        grid, out_scratch(width), 10, "out_project",
    )
    order.done(*attn_part)
    attn_far = swap_cores(attn_part)
    (grad_other_far,) = order.step(grad_other_far)

    start_now, grad_far, grad_other_far, up_other, down_other, *attn_far = order.then(
        start, grad_far, grad_other_far, up_other, down_other, *attn_far
    )
    middle, second, grad_low, active_own, hidden_own, active_other, hidden_other, *parts, up_vecs = call(
        functools.partial(mlp_kernel, kept), meta,
        (start_now, *attn_part, *attn_far, out_rows[0:1], gains[1:2], shifts[1:2], grad_mine, grad_other, grad_far, grad_other_far,
         up_weight, up_bias_own, down_weight, up_other, up_bias_other, down_other),
        [rows_spec(width)] + [ANYWHERE] * (2 * CHUNKS) + [whole((1, width))] * 3 + [ANYWHERE] * 4
        + [whole((width, ff)), whole((1, ff)), whole((ff, width)), whole((width, ff)), whole((1, ff)), ANYWHERE],
        (row_f32, row_low, row_low, *(shape(cap, ff),) * 4, *part_shapes(cap, width), *part_shapes(cap, width), shape(8, ff, F32)),
        (rows_out(width),) * 3 + (rows_out(ff),) * 4 + (ANYWHERE,) * (2 * CHUNKS) + (whole((8, ff)),),
        grid,
        tile_scratch + parts_scratch(width) * 2
        + [pltpu.VMEM((ff, width), LOW), pltpu.SemaphoreType.DMA((8,))]
        + out_scratch(width) * 2,
        65, "mlp",
    )
    branch, second_grad = parts[:CHUNKS], parts[CHUNKS:]
    order.done(*second_grad)
    second_grad_far = swap_cores(second_grad)
    branch_far = swap_cores(branch)

    def weight_grad(*operands, rows=None):
        operands = order.then(*operands)
        pairs = len(operands) // 2
        cols = operands[1].shape[1]
        rows = rows or operands[0].shape[1]
        (result,) = call(
            functools.partial(weight_grad_kernel, pairs), meta, operands,
            [deep_spec(operand.shape[1]) for operand in operands],
            (shape(rows, cols),), (whole((rows, cols)),),
            (META_BLOCKS // 2,), [pltpu.VMEM((rows, cols), F32)], cost=13, name="weight_grad",
        )
        order.done(result)
        return result

    up_sum = Reduction(meta, weight_grad(second, hidden_other))
    down_sum = Reduction(meta, weight_grad(active_other, grad_low))

    pair_shape = jax.ShapeDtypeStruct((slots, TILE, width), LOW)
    pair_spec = whole((slots, TILE, width))

    second_grad_far = order.then(*second_grad_far)
    middle_grad, attn_grad, context_grad_own, context_grad_other, second_sums = call(
        middle_back_kernel, meta,
        (*second_grad, *second_grad_far, middle, grad_low, gains[1:2], out_weight, out_other),
        [ANYWHERE] * (2 * CHUNKS) + [rows_spec(width)] * 2 + [whole((1, width)), whole((shard, width)), whole((shard, width))],
        (row_f32, row_low, shape(cap, shard), shape(cap, shard), shape(8, width, F32)),
        (rows_out(width), rows_out(width), rows_out(shard), rows_out(shard), whole((8, width))),
        grid, parts_scratch(width) * 2, 18, "middle_back",
    )
    order.done(context_grad_other)


    branch_far = order.step(*branch_far)

    def attend_back(projected, attend, context_grad):
        projected, attend, context_grad = order.then(projected, attend, context_grad)
        grads, sums = call(
            functools.partial(attention_back_kernel, heads, shard, cell), meta,
            (projected, attend, context_grad),
            [whole((cap, 3 * shard)), whole((kept, cell, heads * cell)), whole((cap, shard))],
            (shape(cap, 3 * shard), shape(8, shard, F32)), (whole((cap, 3 * shard)), whole((8, shard))),
            (1,), (), 30, "attend_back",
        )
        order.done(grads)
        return grads, sums

    up_own = weight_grad(second, hidden_own)
    proj_grad_other, qkv_vec_other = attend_back(proj_other, attend_other, context_grad_other)
    up_sum.first(order, up_own)
    down_own = weight_grad(active_own, grad_low)

    def attn_grads(proj_grad, context):
        return weight_grad(proj_grad, normed, context, attn_grad, rows=width)

    attn_sum = Reduction(meta, attn_grads(proj_grad_other, context_other))
    down_sum.first(order, down_own)
    up_sum.second(order)
    proj_grad_own, qkv_vec_own = attend_back(proj_own, attend_own, context_grad_own)
    up_sum.third(order)
    down_sum.second(order)
    attn_own = attn_grads(proj_grad_own, context_own)
    attn_sum.first(order, attn_own)
    up_sum.fourth(order)
    down_sum.third(order)
    (first_grads,) = order.then(proj_grad_own)
    first_part = call(
        first_part_kernel, meta,
        (first_grads, proj_grad_other, qkv_own, qkv_other),
        [rows_spec(3 * shard)] * 2 + [whole((3 * shard, width)), ANYWHERE],
        part_shapes(cap, width), (ANYWHERE,) * CHUNKS,
        grid, [pltpu.VMEM((qkv_rows, width), LOW), pltpu.SemaphoreType.DMA((8,)), *out_scratch(width)],
        15, "first_part",
    )
    order.done(*first_part)
    first_far = swap_cores(first_part)
    up_sum.spread(order, 2)
    down_sum.fourth(order)
    attn_sum.second(order, 60)
    first_far = order.then(*first_far)
    input_pair, first_sums, table_grad = call(
        start_back_kernel, meta, (*first_part, *first_far, start, middle_grad, gains[0:1]),
        [ANYWHERE] * (2 * CHUNKS) + [rows_spec(width)] * 2 + [whole((1, width))],
        (pair_shape, shape(8, width, F32), shape(table.shape[0], width, F32)),
        (pair_spec, whole((8, width)), whole(table.shape)),
        grid, [row_scratch] + parts_scratch(width) * 2, 15, "start_back",
    )
    order.done(input_pair)
    up_sum.spread(order, 1)
    attn_sum.third(order)
    down_sum.spread(order, 2)
    rows_small = 8 + table.shape[0]
    vector_inputs = (first_sums, second_sums, table_grad, qkv_vec_own, qkv_vec_other, up_vecs)
    small, small_other = call(
        functools.partial(vectors_kernel, shard), meta, vector_inputs,
        [whole(value.shape) for value in vector_inputs],
        (shape(rows_small, width, F32),) * 2, (whole((rows_small, width)),) * 2, (1,), (), 2, "vectors",
    )
    small_far = swap(small_other, "tp", 2)
    input_far = swap(input_pair[kept:], "tp", 2)
    attn_sum.fourth(order)
    (small_far,) = order.step(small_far)
    small = small + small_far
    small_far = swap(small, "dp", 1)
    down_sum.spread(order, 1)
    middle_now, *branch_far = order.then(middle, *branch_far)
    (output_pair,) = call(
        finish_kernel, meta, (middle_now, *branch, *branch_far, out_rows[1:2]),
        [rows_spec(width)] + [ANYWHERE] * (2 * CHUNKS) + [whole((1, width))],
        (pair_shape,), (pair_spec,),
        grid, [row_scratch] + parts_scratch(width) * 2, 10, "finish",
    )
    order.done(output_pair)
    output_far = swap(output_pair[kept:], "tp", 2)
    attn_sum.spread(order, 2)
    (input_far,) = order.step(input_far)
    (up_total,) = up_sum.last_halves(order, (width,))
    (down_total,) = down_sum.last_halves(order, (width,))
    attn_sum.spread(order, 1)
    (small_far,) = order.step(small_far)
    small = small + small_far
    small_far = swap(small, "dp", 2)
    input_grad = place_cells(input_pair[:kept], order.then(input_far)[0])
    order.done(input_grad)
    (small_far,) = order.step(small_far)
    small = small + small_far
    small_far = swap(small, "dp", 4)
    cell_outputs = place_cells(output_pair[:kept], order.then(output_far)[0])
    order.done(cell_outputs)
    (small_far,) = order.step(small_far)
    small = later_groups(small + small_far)
    qkv_total, out_total = attn_sum.last_halves(order, (3 * shard, shard))

    return (
        cell_outputs,
        input_grad,
        small[0:2],
        small[2:4],
        qkv_total.reshape(3, shard, width).transpose(2, 0, 1),
        small[-2, : 2 * shard].reshape(2, shard),
        out_total,
        small[4:6],
        up_total,
        small[-1],
        down_total,
        small[6:-2],
    )


def solution(mesh):
    in_specs = (
        P("dp", "tp", None),
        P("dp", "tp", None),
        P("dp"),
        P("dp"),
        P(),
        P(),
        P(None, None, "tp"),
        P(None, "tp"),
        P("tp", None),
        P(),
        P(None, "tp"),
        P("tp"),
        P("tp", None),
        P(),
    )
    out_specs = (
        P("dp", "tp", None),
        P("dp", "tp", None),
        P(),
        P(),
        P(None, None, "tp"),
        P(None, "tp"),
        P("tp", None),
        P(),
        P(None, "tp"),
        P("tp"),
        P("tp", None),
        P(),
    )
    return jax.shard_map(
        on_device, mesh=mesh, in_specs=in_specs, out_specs=out_specs, check_vma=False
    )
```

```python
import functools
import math

import jax
import jax.numpy as jnp
from jax import lax
from jax.experimental import pallas as pl
from jax.experimental.pallas import tpu as pltpu
from jax.sharding import PartitionSpec as P

HEAD_DIM = 56
EPSILON = 1e-05
BLOCK = 256
META_BLOCKS = 8
TILE = 16
UNROLL = 6
F32 = jnp.float32
LOW = jnp.bfloat16
VMEM_BYTES = 56 * 1024 * 1024
FLOPS_PER_US = 450000000

NBLK, NCELL, BITS, TILE_SRC, TILE_SET, TILE_LEN, TILE_DST, CELL_OFF, CELL_ROWS = 0, 1, 2, 8, 136, 264, 392, 520, 552


def swap(value, axis, bit):
    count = lax.axis_size(axis)
    if value.ndim == 2 and value.shape[0] % TILE == 0:
        chunk = TILE if value.shape[0] // TILE % 128 else 2 * TILE
        tiled = value.reshape(value.shape[0] // chunk, chunk, value.shape[1])
        return swap(tiled, axis, bit).reshape(value.shape)
    return lax.ppermute(value, axis, [(i, i ^ bit) for i in range(count)])


CHUNKS = 2


def swap_cores(parts):
    return tuple(swap(part, "tp", 1) for part in parts)


class Sequence:
    def __init__(self):
        self.last = ()

    def then(self, *values):
        if not self.last:
            return values
        return lax.optimization_barrier((*values, *self.last))[: len(values)]

    def done(self, *values):
        self.last = (values[-1],)

    def step(self, *values):
        values = self.then(*values)
        self.last = (values[-1],)
        return values


def dot(a, b):
    return jnp.dot(a, b, preferred_element_type=F32)


def dot_nt(a, b):
    return lax.dot_general(a, b, (((1,), (1,)), ((), ())), preferred_element_type=F32)


def dot_tn(a, b):
    return lax.dot_general(a, b, (((0,), (0,)), ((), ())), preferred_element_type=F32)


def row_norm(rows):
    center = rows - jnp.mean(rows, axis=-1, keepdims=True)
    spread = jnp.mean(center * center, axis=-1, keepdims=True)
    scale = lax.rsqrt(spread + EPSILON)
    return center * scale, scale


def norm_back(grad, unit, scale, gain):
    scaled = grad * gain
    first = jnp.mean(scaled, axis=-1, keepdims=True)
    second = jnp.mean(scaled * unit, axis=-1, keepdims=True)
    return scale * (scaled - first - unit * second)


def whole(shape):
    zeros = (0,) * len(shape)
    return pl.BlockSpec(shape, lambda i, meta: zeros, pipeline_mode=pl.Buffered(1))


def rows_spec(width):
    return pl.BlockSpec((BLOCK, width), lambda i, meta: (jnp.minimum(i, meta[NBLK] - 1), 0))


PART_BLOCKS = META_BLOCKS // CHUNKS
PART_ROWS = PART_BLOCKS * BLOCK


def part_shapes(rows, width):
    return (jax.ShapeDtypeStruct((rows // CHUNKS, width), LOW),) * CHUNKS


def parts_scratch(width):
    return [pltpu.VMEM((META_BLOCKS * BLOCK, width), LOW), pltpu.SemaphoreType.DMA((CHUNKS,))]


def out_scratch(width):
    return [pltpu.VMEM((2, BLOCK, width), LOW), pltpu.SemaphoreType.DMA((2,))]


def each_part(parts, rows, sems):
    return [
        pltpu.make_async_copy(part, rows.at[pl.ds(at * PART_ROWS, PART_ROWS)], sems.at[at])
        for at, part in enumerate(parts)
    ]


def fetch_parts(step, blocks, *groups):
    for parts, rows, sems in groups:
        for at, copy in enumerate(each_part(parts, rows, sems)):

            @pl.when((step == 0) & (at * PART_BLOCKS < blocks))
            def _():
                copy.start()

    for parts, rows, sems in groups:
        for at, copy in enumerate(each_part(parts, rows, sems)):

            @pl.when(step == at * PART_BLOCKS)
            def _():
                copy.wait()


def block_of(step, rows):
    return rows[pl.ds(pl.multiple_of(step * BLOCK, BLOCK), BLOCK), :].astype(F32)


def put_part(step, last, value, parts, slots, sems):
    slot = lax.rem(step, 2)

    def copy_to(part, slot):
        begin = pl.multiple_of(lax.rem(step, PART_BLOCKS) * BLOCK, BLOCK)
        return pltpu.make_async_copy(slots.at[slot], part.at[pl.ds(begin, BLOCK)], sems.at[slot])

    @pl.when(step >= 2)
    def _():
        copy_to(parts[0], slot).wait()

    slots[slot] = value
    for at, part in enumerate(parts):

        @pl.when(step // PART_BLOCKS == at)
        def _():
            copy_to(part, slot).start()

    @pl.when(last)
    def _():
        copy_to(parts[0], slot).wait()

        @pl.when(step >= 1)
        def _():
            copy_to(parts[0], 1 - slot).wait()


def rows_out(width):
    return rows_spec(width)


def deep_spec(width):
    return pl.BlockSpec((2 * BLOCK, width), lambda i, meta: (jnp.minimum(i, (meta[NBLK] + 1) // 2 - 1), 0))


def rows_more(width):
    return pl.BlockSpec((BLOCK, width), lambda i, meta: (jnp.minimum(i, meta[NBLK]), 0))


def live_step(meta):
    return pl.when(pl.program_id(0) < meta[NBLK])


ANYWHERE = pl.BlockSpec(memory_space=pl.ANY)


def call(kernel, meta, operands, in_specs, out_shape, out_specs, grid, scratch=(), cost=5, name=None):
    return pl.pallas_call(
        kernel,
        grid_spec=pltpu.PrefetchScalarGridSpec(
            num_scalar_prefetch=1,
            grid=grid,
            in_specs=in_specs,
            out_specs=out_specs,
            scratch_shapes=list(scratch),
        ),
        out_shape=out_shape,
        compiler_params=pltpu.CompilerParams(
            dimension_semantics=("arbitrary",) * len(grid), vmem_limit_bytes=VMEM_BYTES
        ),
        cost_estimate=pl.CostEstimate(flops=cost * FLOPS_PER_US, bytes_accessed=0, transcendentals=0),
        name=name,
    )(meta, *operands)


def load_tiles(sources, tiles, sems, count):
    copies = [
        pltpu.make_async_copy(source, tiles.at[pl.ds(at * count, count)], sems.at[at])
        for at, source in enumerate(sources)
    ]
    for copy in copies:
        copy.start()
    for copy in copies:
        copy.wait()


def begin_kernel(count, meta, a0, a1, a2, a3, table, gain, shift, weight, bias, start, normed, projected, tiles, sems):
    step = pl.program_id(0)

    @pl.when(step == 0)
    def _():
        load_tiles((a0, a1, a2, a3), tiles, sems, count)

    @pl.when(step < meta[NBLK])
    def _():
        for j in range(BLOCK // TILE):
            at = step * (BLOCK // TILE) + j
            tile = tiles[meta[TILE_SRC + at]].astype(F32)
            start[j * TILE : (j + 1) * TILE, :] = tile + table[pl.ds(meta[TILE_SET + at], 1), :]
        unit, _ = row_norm(start[...])
        low = (unit * gain[...] + shift[...]).astype(LOW)
        normed[...] = low
        projected[...] = (dot_nt(low, weight[...]) + bias[...]).astype(LOW)

    @pl.when(step == meta[NBLK])
    def _():
        projected[...] = jnp.zeros_like(projected)


def project_kernel(meta, normed, eighths, bias, projected, weight, sems):
    step = pl.program_id(0)

    @pl.when(step == 0)
    def _():
        load_eighths(eighths, [weight], sems)

    @pl.when(step < meta[NBLK])
    def _():
        projected[...] = (dot_nt(normed[...], weight[: bias.shape[1], :]) + bias[...]).astype(LOW)

    @pl.when(step == meta[NBLK])
    def _():
        projected[...] = jnp.zeros_like(projected)


def head_masks(cell, heads, shard):
    lane = lax.broadcasted_iota(jnp.int32, (cell, shard), 1)
    return [(lane >= h * HEAD_DIM) & (lane < (h + 1) * HEAD_DIM) for h in range(heads)]


def spread_heads(rows, masks, heads, low, high):
    part = rows[:, low:high]
    zero = jnp.zeros_like(part)
    return jnp.concatenate([jnp.where(masks[h][:, low:high], part, zero) for h in heads], axis=0)


def head_groups(heads, shard):
    groups = []
    at = 0
    while at < heads:
        end = min(at + 4, heads)
        low = at * HEAD_DIM // 128 * 128
        high = min(-(-end * HEAD_DIM // 128) * 128, shard)
        groups.append((tuple(range(at, end)), low, high))
        at = end
    return groups


def attention_kernel(heads, shard, cell, meta, projected, context, attend, same_head):
    context[...] = jnp.zeros_like(context)
    masks = head_masks(cell, heads, shard)
    scale = 1.0 / math.sqrt(HEAD_DIM)
    span = same_head.shape[0]
    head_of = [lax.broadcasted_iota(jnp.int32, (span, span), axis) // cell for axis in (0, 1)]
    same_head[...] = jnp.where(head_of[0] == head_of[1], 1.0, 0.0).astype(LOW)

    def one(index):
        at = pl.multiple_of(meta[CELL_OFF + index] * TILE, TILE)
        queries = projected[pl.ds(at, cell), 0:shard]
        keys = projected[pl.ds(at, cell), shard : 2 * shard]
        values = projected[pl.ds(at, cell), 2 * shard : 3 * shard]
        total = None
        for group, low, high in head_groups(heads, shard):
            count = len(group) * cell
            scores = dot_nt(queries[:, low:high], spread_heads(keys, masks, group, low, high)) * scale
            row = lax.broadcasted_iota(jnp.int32, (cell, count), 0)
            lane = lax.broadcasted_iota(jnp.int32, (cell, count), 1)
            scores = jnp.where(row >= lax.rem(lane, cell), scores, -1e30)
            shifted = []
            for pair in range(0, len(group), 2):
                both = scores[:, pair * cell : min(pair + 2, len(group)) * cell]
                if pair + 1 < len(group):
                    left = lax.broadcasted_iota(jnp.int32, both.shape, 1) < cell
                    top_left = jnp.max(jnp.where(left, both, -1e30), axis=1, keepdims=True)
                    top_right = jnp.max(jnp.where(left, -1e30, both), axis=1, keepdims=True)
                    shifted.append(both - jnp.where(left, top_left, top_right))
                else:
                    shifted.append(both - jnp.max(both, axis=1, keepdims=True))
            weights = jnp.exp(jnp.concatenate(shifted, axis=1) if len(shifted) > 1 else shifted[0])
            if len(group) > 1:
                sums = dot(weights.astype(LOW), same_head[:count, :count])
            else:
                sums = jnp.sum(weights, axis=1, keepdims=True)
            probs = (weights * (1.0 / sums)).astype(LOW)
            first = group[0] * cell
            attend[index, :, first : first + count] = probs
            part = dot(probs, spread_heads(values, masks, group, low, high))
            if high - low < shard:
                part = jnp.pad(part, ((0, 0), (low, shard - high)))
            total = part if total is None else total + part
        context[pl.ds(at, cell), :] = total.astype(LOW)

    def body(step, carry):
        for place in range(UNROLL):
            one(UNROLL * step + place)
        return carry

    lax.fori_loop(0, (meta[NCELL] + UNROLL - 1) // UNROLL, body, 0)


def attention_back_kernel(heads, shard, cell, meta, projected, attend, context_grad, result, sums):
    result[...] = jnp.zeros_like(result)
    sums[...] = jnp.zeros_like(sums)
    masks = head_masks(cell, heads, shard)
    scale = 1.0 / math.sqrt(HEAD_DIM)
    row = lax.broadcasted_iota(jnp.int32, (cell, shard), 0)
    left = lax.broadcasted_iota(jnp.int32, (cell, 2 * cell), 1) < cell

    def fold(stacked, group, low, high):
        total = None
        for place, h in enumerate(group):
            part = jnp.where(masks[h][:, low:high], stacked[place * cell : (place + 1) * cell, :], 0.0)
            total = part if total is None else total + part
        return total

    def widen(part, low, high):
        return jnp.pad(part, ((0, 0), (low, shard - high))) if high - low < shard else part

    def one(index):
        at = pl.multiple_of(meta[CELL_OFF + index] * TILE, TILE)
        queries = projected[pl.ds(at, cell), 0:shard]
        keys = projected[pl.ds(at, cell), shard : 2 * shard]
        values = projected[pl.ds(at, cell), 2 * shard : 3 * shard]
        grads = context_grad[pl.ds(at, cell), :]
        grads = jnp.where(row < meta[CELL_ROWS + index], grads, jnp.zeros_like(grads))
        query_total = key_total = value_total = None
        for group, low, high in head_groups(heads, shard):
            first = group[0] * cell
            probs = attend[index, :, first : first + len(group) * cell]
            attend_grad = dot_nt(grads[:, low:high], spread_heads(values, masks, group, low, high))
            parts = []
            for pair in range(0, len(group), 2):
                if pair + 1 < len(group):
                    span = slice(pair * cell, (pair + 2) * cell)
                    weights = probs[:, span].astype(F32)
                    both = attend_grad[:, span]
                    product = weights * both
                    sum_left = jnp.sum(jnp.where(left, product, 0.0), axis=1, keepdims=True)
                    sum_right = jnp.sum(jnp.where(left, 0.0, product), axis=1, keepdims=True)
                    parts.append((product - weights * jnp.where(left, sum_left, sum_right)).astype(LOW))
                else:
                    span = slice(pair * cell, (pair + 1) * cell)
                    weights = probs[:, span].astype(F32)
                    product = weights * attend_grad[:, span]
                    total = jnp.sum(product, axis=1, keepdims=True)
                    parts.append((product - weights * total).astype(LOW))
            score_grad = jnp.concatenate(parts, axis=1) if len(parts) > 1 else parts[0]
            query_part = dot(score_grad, spread_heads(keys, masks, group, low, high)) * scale
            key_part = fold(dot_tn(score_grad, queries[:, low:high]), group, low, high) * scale
            value_part = fold(dot_tn(probs, grads[:, low:high]), group, low, high)
            query_part, key_part, value_part = (widen(p, low, high) for p in (query_part, key_part, value_part))
            if query_total is None:
                query_total, key_total, value_total = query_part, key_part, value_part
            else:
                query_total, key_total, value_total = (
                    query_total + query_part,
                    key_total + key_part,
                    value_total + value_part,
                )
        for place, part in enumerate((query_total, key_total, value_total)):
            low_part = part.astype(LOW)
            result[pl.ds(at, cell), place * shard : (place + 1) * shard] = low_part
            sums[place : place + 1, :] += jnp.sum(low_part.astype(F32), axis=0, keepdims=True)

    def body(step, carry):
        one(2 * step)
        one(2 * step + 1)
        return carry

    lax.fori_loop(0, (meta[NCELL] + 1) // 2, body, 0)


def out_project_kernel(meta, a, b, weight_a, weight_b, *refs):
    *parts, slots, sems = refs
    step = pl.program_id(0)

    @live_step(meta)
    def _():
        value = (dot(a[...], weight_a[...]) + dot(b[...], weight_b[...])).astype(LOW)
        put_part(step, step == meta[NBLK] - 1, value, parts, slots, sems)


def first_part_kernel(meta, a, b, weight_a, eighths, *refs):
    step = pl.program_id(0)
    *parts, weight_b, weight_sems, slots, sems = refs

    @pl.when(step == 0)
    def _():
        load_eighths(eighths, [weight_b], weight_sems)

    @live_step(meta)
    def _():
        value = (dot(a[...], weight_a[...]) + dot(b[...], weight_b[: b.shape[1], :])).astype(LOW)
        put_part(step, step == meta[NBLK] - 1, value, parts, slots, sems)


def gelu_pair(hidden):
    chance = 0.5 * (1.0 + lax.erf(hidden * (1.0 / math.sqrt(2.0))))
    slope = chance + hidden * (jnp.exp(-0.5 * hidden * hidden) * (1.0 / math.sqrt(2.0 * math.pi)))
    return hidden * chance, slope


def mlp_block(second, product, up, bias, down, active, hidden_grad, bias_grad):
    hidden = dot(second, up[...]) + bias[...]
    value, slope = gelu_pair(hidden)
    low = value.astype(LOW)
    active[...] = low
    back = (slope * product).astype(LOW)
    hidden_grad[...] = back
    bias_grad[...] += jnp.sum(back.astype(F32), axis=0, keepdims=True)
    return dot(low, down[...]), dot_nt(back, up[...])


def mlp_kernel(count, meta, start, *refs):
    near_parts, far_parts, refs = refs[:CHUNKS], refs[CHUNKS : 2 * CHUNKS], refs[2 * CHUNKS :]
    bias_row, gain, shift, a0, a1, a2, a3, up, up_bias, down, other_up, other_bias, eighths, *refs = refs
    middle, second, grad, active, hidden_grad, other_active, other_hidden, *refs = refs
    branch, second_grad, refs = refs[:CHUNKS], refs[CHUNKS : 2 * CHUNKS], refs[2 * CHUNKS :]
    bias_grad, tiles, sems, near_rows, near_sems, far_rows, far_sems, *refs = refs
    other_down, other_sems, branch_slots, branch_sems, grad_slots, grad_sems = refs
    step = pl.program_id(0)
    copies = eighths_copies(eighths, [other_down], other_sems)

    @pl.when(step == 0)
    def _():
        load_tiles((a0, a1, a2, a3), tiles, sems, count)
        for copy in copies:
            copy.start()
        bias_grad[...] = jnp.zeros_like(bias_grad)

    @live_step(meta)
    def _():
        last = step == meta[NBLK] - 1
        fetch_parts(step, meta[NBLK], (near_parts, near_rows, near_sems), (far_parts, far_rows, far_sems))
        inner = lax.broadcasted_iota(jnp.int32, (TILE, 1), 0)
        for j in range(BLOCK // TILE):
            at = step * (BLOCK // TILE) + j
            tile = tiles[meta[TILE_SRC + at]]
            grad[j * TILE : (j + 1) * TILE, :] = jnp.where(inner < meta[TILE_LEN + at], tile, jnp.zeros_like(tile))

        @pl.when(step == 0)
        def _():
            for copy in copies:
                copy.wait()

        own_product = dot_nt(grad[...], down[...])
        other_product = dot_nt(grad[...], other_down[...])
        rows = start[...] + (block_of(step, near_rows) + block_of(step, far_rows)) + bias_row[...]
        middle[...] = rows
        unit, _ = row_norm(rows)
        low = (unit * gain[...] + shift[...]).astype(LOW)
        second[...] = low
        own = mlp_block(low, own_product, up, up_bias, down, active, hidden_grad, bias_grad.at[0:1])
        other = mlp_block(
            low, other_product, other_up, other_bias, other_down, other_active, other_hidden, bias_grad.at[1:2]
        )
        put_part(step, last, (own[1] + other[1]).astype(LOW), second_grad, grad_slots, grad_sems)
        put_part(step, last, (own[0] + other[0]).astype(LOW), branch, branch_slots, branch_sems)


def weight_grad_kernel(pairs, meta, *refs):
    step = pl.program_id(0)
    result, total = refs[2 * pairs :]
    blocks = meta[NBLK] - 2 * step

    def add(count):
        base = 0
        for a, b in zip(refs[: 2 * pairs : 2], refs[1 : 2 * pairs : 2]):
            rows = slice(base, base + a.shape[1])
            part = dot_tn(a[:count, :], b[:count, :])
            base += a.shape[1]

            @pl.when(step == 0)
            def _():
                total[rows, :] = part

            @pl.when(step > 0)
            def _():
                total[rows, :] += part

    @pl.when(blocks >= 2)
    def _():
        add(2 * BLOCK)

    @pl.when(blocks == 1)
    def _():
        add(BLOCK)

    @pl.when((blocks > 0) & (blocks <= 2))
    def _():
        result[...] = total[...].astype(LOW)


def middle_back_kernel(meta, *refs):
    near_parts, far_parts, refs = refs[:CHUNKS], refs[CHUNKS : 2 * CHUNKS], refs[2 * CHUNKS :]
    middle, grad, gain, out_a, out_b, middle_grad, attn_grad, context_a, context_b, sums, *refs = refs
    near_rows, near_sems, far_rows, far_sems = refs
    step = pl.program_id(0)

    @pl.when(step == 0)
    def _():
        sums[...] = jnp.zeros_like(sums)

    @live_step(meta)
    def _():
        fetch_parts(step, meta[NBLK], (near_parts, near_rows, near_sems), (far_parts, far_rows, far_sems))
        unit, scale = row_norm(middle[...])
        second_grad = block_of(step, near_rows) + block_of(step, far_rows)
        grad_rows = grad[...].astype(F32)
        total = grad_rows + norm_back(second_grad, unit, scale, gain[...])
        middle_grad[...] = total
        low = total.astype(LOW)
        attn_grad[...] = low
        context_a[...] = dot_nt(low, out_a[...]).astype(LOW)
        context_b[...] = dot_nt(low, out_b[...]).astype(LOW)
        for at, rows in enumerate((second_grad * unit, second_grad, total, grad_rows)):
            sums[at : at + 1, :] += jnp.sum(rows, axis=0, keepdims=True)


def scatter_tiles(meta, step, rows, out):
    for j in range(BLOCK // TILE):
        place = meta[TILE_DST + step * (BLOCK // TILE) + j]

        @pl.when(place >= 0)
        def _():
            out[place] = rows[j * TILE : (j + 1) * TILE, :].astype(LOW)


def start_back_kernel(meta, *refs):
    near_parts, far_parts, refs = refs[:CHUNKS], refs[CHUNKS : 2 * CHUNKS], refs[2 * CHUNKS :]
    start, middle_grad, gain, out, sums, table, rows, near_rows, near_sems, far_rows, far_sems = refs
    step = pl.program_id(0)

    @pl.when(step == 0)
    def _():
        out[...] = jnp.zeros_like(out)
        sums[...] = jnp.zeros_like(sums)
        table[...] = jnp.zeros_like(table)

    @live_step(meta)
    def _():
        fetch_parts(step, meta[NBLK], (near_parts, near_rows, near_sems), (far_parts, far_rows, far_sems))
        unit, scale = row_norm(start[...])
        first_grad = block_of(step, near_rows) + block_of(step, far_rows)
        rows[...] = middle_grad[...] + norm_back(first_grad, unit, scale, gain[...])
        for at, value in enumerate((first_grad * unit, first_grad)):
            sums[at : at + 1, :] += jnp.sum(value, axis=0, keepdims=True)
        for j in range(BLOCK // TILE):
            at = meta[TILE_SET + step * (BLOCK // TILE) + j]
            table[pl.ds(at, 1), :] += jnp.sum(rows[j * TILE : (j + 1) * TILE, :], axis=0, keepdims=True)
        scatter_tiles(meta, step, rows, out)


def finish_kernel(meta, middle, *refs):
    near_parts, far_parts, refs = refs[:CHUNKS], refs[CHUNKS : 2 * CHUNKS], refs[2 * CHUNKS :]
    bias_row, out, rows, near_rows, near_sems, far_rows, far_sems = refs
    step = pl.program_id(0)

    @pl.when(step == 0)
    def _():
        out[...] = jnp.zeros_like(out)

    @live_step(meta)
    def _():
        fetch_parts(step, meta[NBLK], (near_parts, near_rows, near_sems), (far_parts, far_rows, far_sems))
        rows[...] = middle[...] + (block_of(step, near_rows) + block_of(step, far_rows)) + bias_row[...]
        inner = lax.broadcasted_iota(jnp.int32, (TILE, 1), 0)
        for j in range(BLOCK // TILE):
            at = step * (BLOCK // TILE) + j
            place = meta[TILE_DST + at]

            @pl.when(place >= 0)
            def _():
                out[place] = jnp.where(inner < meta[TILE_LEN + at], rows[j * TILE : (j + 1) * TILE, :], 0.0).astype(LOW)


def vectors_kernel(shard, meta, first, second, table, own, other, up, small, small_other):
    for out, qkv, at in ((small, own, 0), (small_other, other, 1)):
        out[0:1, :] = first[0:1, :]
        out[1:2, :] = second[0:1, :]
        out[2:3, :] = first[1:2, :]
        out[3:6, :] = second[1:4, :]
        out[6:38, :] = table[...]
        out[38:40, :] = jnp.zeros((2, out.shape[1]), F32)
        out[38:39, :shard] = qkv[0:1, :]
        out[38:39, shard : 2 * shard] = qkv[2:3, :]
        out[39:40, :] = up[at : at + 1, :]


def window_size(half):
    return -(-half // (4 * TILE)) * TILE


def window_at(low, high, half):
    size = window_size(half)
    return low * (half - 2 * size) + high * size


def run_copies(copies):
    for copy in copies:
        copy.start()
    for copy in copies:
        copy.wait()


def join_kernel(extra, level, meta, mine, far, out, sems):
    rows = mine.shape[0]

    def put(first, second):
        run_copies(
            [
                pltpu.make_async_copy(first, out.at[pl.ds(0, rows)], sems.at[0]),
                pltpu.make_async_copy(second.at[pl.ds(extra, rows - extra)], out.at[pl.ds(rows, rows - extra)], sems.at[1]),
            ]
        )

    @pl.when(meta[BITS + level] == 0)
    def _():
        put(mine, far)

    @pl.when(meta[BITS + level] == 1)
    def _():
        put(far, mine)


def join(meta, mine, far, level, total):
    rows, width = mine.shape
    (result,) = call(
        functools.partial(join_kernel, 2 * rows - total, level), meta, (mine, far), [ANYWHERE] * 2,
        (jax.ShapeDtypeStruct((total, width), LOW),), (whole((total, width)),),
        (1,), [pltpu.SemaphoreType.DMA((2,))], cost=3, name="join",
    )
    return result


def gather_eighths(piece):
    groups = lax.axis_size("dp")
    spans = [list(range(at, at + 8)) for at in range(0, groups, 8)] if groups > 8 else None
    tiled = piece.reshape(piece.shape[0] // TILE, TILE, piece.shape[1])
    whole_block = lax.all_gather(tiled, "dp", axis=0, tiled=True, axis_index_groups=spans)
    return whole_block.reshape(8 * piece.shape[0], piece.shape[1])


def eighths_copies(gathered, scratches, sems):
    copies = []
    for at, scratch in enumerate(scratches):
        half = scratch.shape[0] // 2
        size = window_size(half)
        for group in range(8):
            low, high = (group >> 1) & 1, group >> 2
            skip = 4 * size - half if (low, high) == (1, 0) else 0
            begin = (group & 1) * half + window_at(low, high, half) + skip
            copies.append(
                pltpu.make_async_copy(
                    gathered.at[pl.ds((group * len(scratches) + at) * size + skip, size - skip)],
                    scratch.at[pl.ds(begin, size - skip)],
                    sems.at[8 * at + group],
                )
            )
    return copies


def load_eighths(gathered, scratches, sems):
    copies = eighths_copies(gathered, scratches, sems)
    for copy in copies:
        copy.start()
    for copy in copies:
        copy.wait()


def first_sum_kernel(meta, own, far, sent):
    sent[...] = (own[...].astype(F32) + far[...].astype(F32)).astype(LOW)


def first_sum(meta, own, far):
    rows, width = own.shape
    half = rows // 2
    steps = next(count for count in (5, 4, 3, 1) if half % (count * TILE) == 0)
    block = half // steps
    source = pl.BlockSpec((block, width), lambda i, meta: ((1 - meta[BITS]) * steps + i, 0))
    (sent,) = call(
        first_sum_kernel, meta, (own, far), [source, source], (jax.ShapeDtypeStruct((half, width), LOW),),
        (pl.BlockSpec((block, width), lambda i, meta: (i, 0)),), (steps,), cost=5, name="first_sum",
    )
    return sent


def second_sum_kernel(half, meta, mine, far, arrived, kept, sent):
    size = 2 * window_size(half)
    bit = meta[BITS + 1]
    for out, place in ((kept, bit), (sent, 1 - bit)):
        rows = pl.ds(pl.multiple_of(place * (half - size), TILE), size)
        total = mine[rows, :].astype(F32) + far[rows, :].astype(F32) + arrived[rows, :].astype(F32)
        out[...] = total.astype(out.dtype)


def second_sum(meta, own, far, arrived, cost):
    half, width = arrived.shape
    size = 2 * window_size(half)
    kept = pl.BlockSpec((half, width), lambda i, meta: (meta[BITS], 0), pipeline_mode=pl.Buffered(1))
    return call(
        functools.partial(second_sum_kernel, half), meta, (own, far, arrived), [kept, kept, whole((half, width))],
        (jax.ShapeDtypeStruct((size, width), F32), jax.ShapeDtypeStruct((size, width), LOW)),
        (whole((size, width)),) * 2, (1,), cost=cost, name="second_sum",
    )


def third_sum_kernel(count, meta, *refs):
    kept, arrived, own, sent = refs[:count], refs[count], refs[count + 1 : 2 * count + 1], refs[-1]
    size = own[0].shape[0]
    bit = meta[BITS + 2]
    for at in range(count):
        for place in (bit, 1 - bit):
            begin = pl.multiple_of(place * size, TILE)
            far = arrived[pl.ds(pl.multiple_of(2 * at * size + begin, TILE), size), :].astype(F32)
            total = kept[at][pl.ds(begin, size), :] + far
            if place is bit:
                own[at][...] = total
            else:
                sent[at * size : (at + 1) * size, :] = total.astype(LOW)


def third_sum(meta, kept, arrived, cost=3):
    count = len(kept)
    size, width = kept[0].shape[0] // 2, kept[0].shape[1]
    *own, sent = call(
        functools.partial(third_sum_kernel, count), meta, (*kept, arrived),
        [whole(each.shape) for each in (*kept, arrived)],
        (jax.ShapeDtypeStruct((size, width), F32),) * count + (jax.ShapeDtypeStruct((count * size, width), LOW),),
        (whole((size, width)),) * count + (whole((count * size, width)),), (1,), cost=cost, name="third_sum",
    )
    return own, sent


def fourth_sum_kernel(count, meta, *refs):
    own, arrived, outs = refs[:count], refs[count], refs[count + 1 :]
    size = own[0].shape[0]
    for at, out in enumerate(outs):
        out[...] = (own[at][...] + arrived[at * size : (at + 1) * size, :].astype(F32)).astype(out.dtype)


def fourth_sum(meta, own, arrived, kinds):
    shape = own[0].shape
    return call(
        functools.partial(fourth_sum_kernel, len(own)), meta, (*own, arrived),
        [whole(each.shape) for each in (*own, arrived)],
        tuple(jax.ShapeDtypeStruct(shape, kind) for kind in kinds), (whole(shape),) * len(own),
        (1,), cost=3, name="fourth_sum",
    )


def widen_rows_kernel(meta, mine, far, *outs):
    half = mine.shape[0]

    def put(lower, upper):
        base = 0
        for out in outs:
            count = out.shape[0]
            split = min(max(half - base, 0), count)
            if split:
                out[:split, :] = lower[base : base + split, :].astype(F32)
            if split < count:
                begin = base + split - half
                out[split:, :] = upper[begin : begin + count - split, :].astype(F32)
            base += count

    @pl.when(meta[BITS] == 0)
    def _():
        put(mine, far)

    @pl.when(meta[BITS] == 1)
    def _():
        put(far, mine)


def widen_rows(meta, mine, far, rows):
    half, width = mine.shape
    return call(
        widen_rows_kernel, meta, (mine, far), [whole((half, width))] * 2,
        tuple(jax.ShapeDtypeStruct((count, width), F32) for count in rows),
        tuple(whole((count, width)) for count in rows), (1,), name="widen_rows",
    )


def later_groups(value):
    level = 3
    while (1 << level) < lax.axis_size("dp"):
        value = (value.astype(F32) + swap(value, "dp", 1 << level).astype(F32)).astype(value.dtype)
        level += 1
    return value


class Reduction:
    def __init__(self, meta, other):
        self.meta = meta
        self.far = swap(other, "tp", 2)

    def arrive(self, order):
        (self.far,) = order.step(self.far)

    def first(self, order, own):
        self.own, self.far = order.then(own, self.far)
        sent = first_sum(self.meta, self.own, self.far)
        order.done(sent)
        self.arrived = swap(sent, "dp", 1)

    def wait_second(self, order):
        (self.arrived,) = order.step(self.arrived)

    def second(self, order, cost=4):
        (arrived,) = order.then(self.arrived)
        self.half = arrived.shape[0]
        self.kept, sent = second_sum(self.meta, self.own, self.far, arrived, cost)
        order.done(sent)
        self.arrived = swap(sent, "dp", 2)

    def third(self, order, cost=3):
        (arrived,) = order.then(self.arrived)
        self.kept, sent = third_sum(self.meta, [self.kept], arrived, cost)
        order.done(sent)
        self.arrived = swap(sent, "dp", 4)

    def fourth(self, order):
        (arrived,) = order.then(self.arrived)
        (piece,) = fourth_sum(self.meta, self.kept, arrived, (LOW,))
        order.done(piece)
        piece = later_groups(piece)
        self.mine, self.far = piece, swap(piece, "dp", 4)

    def spread(self, order, level):
        mine, far = order.then(self.mine, self.far)
        rows = 2 * mine.shape[0] if level == 2 else self.half
        self.mine = join(self.meta, mine, far, level, rows)
        order.done(self.mine)
        self.far = swap(self.mine, "dp", 1 << (level - 1))

    def last_halves(self, order, rows):
        mine, far = order.then(self.mine, self.far)
        results = widen_rows(self.meta, mine, far, rows)
        order.done(results[0])
        return results


def eighth(block):
    half = block.shape[0] // 2
    index = lax.axis_index("dp")
    at = (index & 1) * half + window_at((index >> 1) & 1, (index >> 2) & 1, half)
    return lax.dynamic_slice_in_dim(block, at, window_size(half), 0)


def on_device(
    cell_inputs,
    out_grad,
    lengths,
    datasets,
    norm_gain,
    norm_bias,
    qkv_weight,
    qv_bias,
    out_weight,
    out_bias,
    up_weight,
    up_bias,
    down_weight,
    dataset_table,
):
    slots, quarter, width = cell_inputs.shape
    tensor = lax.axis_index("tp")
    chip = tensor // 2
    core = tensor % 2
    blocks_per_cell = lax.axis_size("tp")
    cell = quarter * blocks_per_cell
    shard = qkv_weight.shape[2]
    ff = up_weight.shape[1]
    heads = shard // HEAD_DIM
    kept = slots // 2
    tile_cap = META_BLOCKS * BLOCK // TILE
    cap = META_BLOCKS * BLOCK
    grid = (META_BLOCKS,)
    group = lax.axis_index("dp")
    index = jnp.arange(kept, dtype=jnp.int32)

    def mine_of(rows):
        pairs = rows.reshape(kept, 2, *rows.shape[1:])
        mine = lax.dynamic_index_in_dim(pairs, chip, 1, keepdims=False)
        theirs = lax.dynamic_index_in_dim(pairs, 1 - chip, 1, keepdims=False)
        return mine, theirs

    def place_cells(mine, other):
        even = jnp.where(chip == 0, mine, other)
        odd = jnp.where(chip == 0, other, mine)
        return jnp.stack([even, odd], axis=1).reshape(slots, quarter, width)

    cell_lengths, _ = mine_of(lengths)
    cell_sets, _ = mine_of(datasets)
    cell_tiles = (cell_lengths + TILE - 1) // TILE
    ends = jnp.sum(jnp.where(index[None, :] <= index[:, None], cell_tiles[None, :], 0), axis=1)
    begins = ends - cell_tiles
    tile_count = ends[-1]
    tile = jnp.arange(tile_cap, dtype=jnp.int32)
    owner = jnp.sum((ends[None, :] <= tile[:, None]).astype(jnp.int32), axis=1)
    live = tile < tile_count
    owned = (owner[:, None] == index[None, :]) & live[:, None]

    def of_owner(values):
        return jnp.sum(jnp.where(owned, values[None, :], 0), axis=1)

    block = tile - of_owner(begins)
    shelf = jnp.where(block // 2 == chip, 0, kept) + owner
    tile_src = jnp.where(live, jnp.where(block % 2 == core, 0, slots) + shelf, 0)
    tile_set = of_owner(cell_sets)
    tile_len = jnp.clip(of_owner(cell_lengths) - block * TILE, 0, TILE) * live
    tile_dst = jnp.where(live & (block % 2 == core), shelf, -1)
    cell_count = jnp.sum((cell_lengths > 0).astype(jnp.int32))
    block_count = (tile_count + BLOCK // TILE - 1) // (BLOCK // TILE)
    grid = (META_BLOCKS,)
    head = jnp.stack([block_count, cell_count, group & 1, (group >> 1) & 1, (group >> 2) & 1])

    meta = jnp.concatenate(
        [head, jnp.zeros((3,), jnp.int32), tile_src, tile_set, tile_len, tile_dst, begins, cell_tiles * TILE]
    ).astype(jnp.int32)

    order = Sequence()
    qkv_own = qkv_weight.transpose(1, 2, 0).reshape(3 * shard, width)
    qkv_rows = -(-3 * shard // (2 * TILE)) * 2 * TILE
    vectors = jnp.concatenate([qv_bias.reshape(-1), up_bias])
    piece_source, cells_now = lax.optimization_barrier(
        (eighth(jnp.pad(qkv_own, ((0, qkv_rows - 3 * shard), (0, 0)))), cell_inputs)
    )
    qkv_piece = swap(piece_source, "tp", 2)
    in_mine, in_theirs = mine_of(cells_now)
    in_other = swap(in_theirs, "tp", 2)
    in_far = swap(in_mine, "tp", 1)
    head_rows = jnp.pad(vectors, (0, 2 * width - vectors.shape[0])).reshape(2, width)
    out_and_vectors = jnp.concatenate([out_weight, head_rows, jnp.zeros((6, width), LOW)], axis=0)
    down_piece, out_and_vectors, grad_now, _ = lax.optimization_barrier(
        (eighth(down_weight), out_and_vectors, out_grad, in_theirs)
    )
    down_piece = swap(down_piece, "tp", 2)
    out_and_vectors = swap(out_and_vectors, "tp", 2)
    grad_mine, grad_theirs = mine_of(grad_now)
    meta, qkv_own, grad_mine, grad_theirs = order.step(meta, qkv_own, grad_mine, grad_theirs)
    (qkv_piece,) = order.step(qkv_piece)
    qkv_other = gather_eighths(qkv_piece)
    in_far, in_other = order.step(in_far, in_other)
    in_other_far = swap(in_other, "tp", 1)
    grad_other = swap(order.then(grad_theirs)[0], "tp", 2)
    (in_other_far,) = order.step(in_other_far)

    def biases(vector):
        zeros = jnp.zeros((shard,), LOW)
        qkv_row = jnp.concatenate([vector[:shard], zeros, vector[shard : 2 * shard]])
        return qkv_row.astype(F32)[None], vector[2 * shard :].astype(F32)[None]

    qkv_bias_own, up_bias_own = biases(vectors)
    gains = norm_gain.astype(F32)
    shifts = norm_bias.astype(F32)
    out_rows = out_bias.astype(F32)
    table = dataset_table.astype(F32)

    def shape(rows, cols, kind=LOW):
        return jax.ShapeDtypeStruct((rows, cols), kind)

    row_f32, row_low = shape(cap, width, F32), shape(cap, width)
    row_scratch = pltpu.VMEM((BLOCK, width), F32)
    tile_scratch = [pltpu.VMEM((2 * slots, TILE, width), LOW), pltpu.SemaphoreType.DMA((4,))]

    start, normed, proj_own = call(
        functools.partial(begin_kernel, kept), meta,
        (in_mine, in_other, in_far, in_other_far, table, gains[0:1], shifts[0:1], qkv_own, qkv_bias_own),
        [ANYWHERE] * 4 + [whole(table.shape), whole((1, width)), whole((1, width)), whole((3 * shard, width)), whole((1, 3 * shard))],
        (row_f32, row_low, shape(cap, 3 * shard)),
        (rows_out(width), rows_out(width), rows_more(3 * shard)),
        grid, tile_scratch, 15, "begin",
    )
    order.done(proj_own)

    def attend_shard(projected):
        (projected,) = order.then(projected)
        context, attend = call(
            functools.partial(attention_kernel, heads, shard, cell), meta, (projected,),
            [whole((cap, 3 * shard))],
            (shape(cap, shard), jax.ShapeDtypeStruct((kept, cell, heads * cell), LOW)),
            (whole((cap, shard)), whole((kept, cell, heads * cell))),
            (1,), [pltpu.VMEM((4 * cell, 4 * cell), LOW)], 4, "attend",
        )
        order.done(context)
        return context, attend

    down_piece, out_and_vectors = order.step(down_piece, out_and_vectors)
    down_other = gather_eighths(down_piece)
    grad_now, up_now = order.then(grad_mine, up_weight)
    up_other = swap(up_now, "tp", 2)
    grad_far = swap(grad_now, "tp", 1)
    context_own, attend_own = attend_shard(proj_own)
    grad_far, grad_other = order.step(grad_far, grad_other)
    out_other = out_and_vectors[:shard]
    vectors_other = out_and_vectors[shard : shard + 2].reshape(-1)[: vectors.shape[0]]
    normed_now, qkv_now = order.then(normed, qkv_other)
    qkv_bias_other, up_bias_other = biases(vectors_other)
    (proj_other,) = call(
        project_kernel, meta, (normed_now, qkv_now, qkv_bias_other),
        [rows_spec(width), ANYWHERE, whole((1, 3 * shard))],
        (shape(cap, 3 * shard),), (rows_more(3 * shard),),
        grid, [pltpu.VMEM((qkv_rows, width), LOW), pltpu.SemaphoreType.DMA((8,))],
        6, "project",
    )
    order.done(proj_other)
    context_other, attend_other = attend_shard(proj_other)
    grad_other_far = swap(grad_other, "tp", 1)
    (context_now,) = order.then(context_other)
    attn_part = call(
        out_project_kernel, meta, (context_own, context_now, out_weight, out_other),
        [rows_spec(shard), rows_spec(shard), whole((shard, width)), whole((shard, width))],
        part_shapes(cap, width), (ANYWHERE,) * CHUNKS,
        grid, out_scratch(width), 10, "out_project",
    )
    order.done(*attn_part)
    attn_far = swap_cores(attn_part)
    (grad_other_far,) = order.step(grad_other_far)

    start_now, grad_far, grad_other_far, up_other, down_other, *attn_far = order.then(
        start, grad_far, grad_other_far, up_other, down_other, *attn_far
    )
    middle, second, grad_low, active_own, hidden_own, active_other, hidden_other, *parts, up_vecs = call(
        functools.partial(mlp_kernel, kept), meta,
        (start_now, *attn_part, *attn_far, out_rows[0:1], gains[1:2], shifts[1:2], grad_mine, grad_other, grad_far, grad_other_far,
         up_weight, up_bias_own, down_weight, up_other, up_bias_other, down_other),
        [rows_spec(width)] + [ANYWHERE] * (2 * CHUNKS) + [whole((1, width))] * 3 + [ANYWHERE] * 4
        + [whole((width, ff)), whole((1, ff)), whole((ff, width)), whole((width, ff)), whole((1, ff)), ANYWHERE],
        (row_f32, row_low, row_low, *(shape(cap, ff),) * 4, *part_shapes(cap, width), *part_shapes(cap, width), shape(8, ff, F32)),
        (rows_out(width),) * 3 + (rows_out(ff),) * 4 + (ANYWHERE,) * (2 * CHUNKS) + (whole((8, ff)),),
        grid,
        tile_scratch + parts_scratch(width) * 2
        + [pltpu.VMEM((ff, width), LOW), pltpu.SemaphoreType.DMA((8,))]
        + out_scratch(width) * 2,
        65, "mlp",
    )
    branch, second_grad = parts[:CHUNKS], parts[CHUNKS:]
    order.done(*second_grad)
    second_grad_far = swap_cores(second_grad)
    branch_far = swap_cores(branch)

    def weight_grad(*operands, rows=None):
        operands = order.then(*operands)
        pairs = len(operands) // 2
        cols = operands[1].shape[1]
        rows = rows or operands[0].shape[1]
        (result,) = call(
            functools.partial(weight_grad_kernel, pairs), meta, operands,
            [deep_spec(operand.shape[1]) for operand in operands],
            (shape(rows, cols),), (whole((rows, cols)),),
            (META_BLOCKS // 2,), [pltpu.VMEM((rows, cols), F32)], cost=13, name="weight_grad",
        )
        order.done(result)
        return result

    up_sum = Reduction(meta, weight_grad(second, hidden_other))
    down_sum = Reduction(meta, weight_grad(active_other, grad_low))

    pair_shape = jax.ShapeDtypeStruct((slots, TILE, width), LOW)
    pair_spec = whole((slots, TILE, width))

    second_grad_far = order.then(*second_grad_far)
    middle_grad, attn_grad, context_grad_own, context_grad_other, second_sums = call(
        middle_back_kernel, meta,
        (*second_grad, *second_grad_far, middle, grad_low, gains[1:2], out_weight, out_other),
        [ANYWHERE] * (2 * CHUNKS) + [rows_spec(width)] * 2 + [whole((1, width)), whole((shard, width)), whole((shard, width))],
        (row_f32, row_low, shape(cap, shard), shape(cap, shard), shape(8, width, F32)),
        (rows_out(width), rows_out(width), rows_out(shard), rows_out(shard), whole((8, width))),
        grid, parts_scratch(width) * 2, 18, "middle_back",
    )
    order.done(context_grad_other)


    branch_far = order.step(*branch_far)

    def attend_back(projected, attend, context_grad):
        projected, attend, context_grad = order.then(projected, attend, context_grad)
        grads, sums = call(
            functools.partial(attention_back_kernel, heads, shard, cell), meta,
            (projected, attend, context_grad),
            [whole((cap, 3 * shard)), whole((kept, cell, heads * cell)), whole((cap, shard))],
            (shape(cap, 3 * shard), shape(8, shard, F32)), (whole((cap, 3 * shard)), whole((8, shard))),
            (1,), (), 30, "attend_back",
        )
        order.done(grads)
        return grads, sums

    up_own = weight_grad(second, hidden_own)
    proj_grad_other, qkv_vec_other = attend_back(proj_other, attend_other, context_grad_other)
    up_sum.first(order, up_own)
    down_own = weight_grad(active_own, grad_low)

    def attn_grads(proj_grad, context):
        return weight_grad(proj_grad, normed, context, attn_grad, rows=width)

    attn_sum = Reduction(meta, attn_grads(proj_grad_other, context_other))
    down_sum.first(order, down_own)
    up_sum.second(order)
    proj_grad_own, qkv_vec_own = attend_back(proj_own, attend_own, context_grad_own)
    up_sum.third(order)
    down_sum.second(order)
    attn_own = attn_grads(proj_grad_own, context_own)
    attn_sum.first(order, attn_own)
    up_sum.fourth(order)
    down_sum.third(order)
    (first_grads,) = order.then(proj_grad_own)
    first_part = call(
        first_part_kernel, meta,
        (first_grads, proj_grad_other, qkv_own, qkv_other),
        [rows_spec(3 * shard)] * 2 + [whole((3 * shard, width)), ANYWHERE],
        part_shapes(cap, width), (ANYWHERE,) * CHUNKS,
        grid, [pltpu.VMEM((qkv_rows, width), LOW), pltpu.SemaphoreType.DMA((8,)), *out_scratch(width)],
        15, "first_part",
    )
    order.done(*first_part)
    first_far = swap_cores(first_part)
    up_sum.spread(order, 2)
    down_sum.fourth(order)
    attn_sum.second(order, 60)
    first_far = order.then(*first_far)
    input_pair, first_sums, table_grad = call(
        start_back_kernel, meta, (*first_part, *first_far, start, middle_grad, gains[0:1]),
        [ANYWHERE] * (2 * CHUNKS) + [rows_spec(width)] * 2 + [whole((1, width))],
        (pair_shape, shape(8, width, F32), shape(table.shape[0], width, F32)),
        (pair_spec, whole((8, width)), whole(table.shape)),
        grid, [row_scratch] + parts_scratch(width) * 2, 15, "start_back",
    )
    order.done(input_pair)
    up_sum.spread(order, 1)
    attn_sum.third(order)
    down_sum.spread(order, 2)
    rows_small = 8 + table.shape[0]
    vector_inputs = (first_sums, second_sums, table_grad, qkv_vec_own, qkv_vec_other, up_vecs)
    small, small_other = call(
        functools.partial(vectors_kernel, shard), meta, vector_inputs,
        [whole(value.shape) for value in vector_inputs],
        (shape(rows_small, width, F32),) * 2, (whole((rows_small, width)),) * 2, (1,), (), 2, "vectors",
    )
    small_far = swap(small_other, "tp", 2)
    input_far = swap(input_pair[kept:], "tp", 2)
    attn_sum.fourth(order)
    (small_far,) = order.step(small_far)
    small = small + small_far
    small_far = swap(small, "dp", 1)
    down_sum.spread(order, 1)
    middle_now, *branch_far = order.then(middle, *branch_far)
    (output_pair,) = call(
        finish_kernel, meta, (middle_now, *branch, *branch_far, out_rows[1:2]),
        [rows_spec(width)] + [ANYWHERE] * (2 * CHUNKS) + [whole((1, width))],
        (pair_shape,), (pair_spec,),
        grid, [row_scratch] + parts_scratch(width) * 2, 10, "finish",
    )
    order.done(output_pair)
    output_far = swap(output_pair[kept:], "tp", 2)
    attn_sum.spread(order, 2)
    (input_far,) = order.step(input_far)
    (up_total,) = up_sum.last_halves(order, (width,))
    (down_total,) = down_sum.last_halves(order, (width,))
    attn_sum.spread(order, 1)
    (small_far,) = order.step(small_far)
    small = small + small_far
    small_far = swap(small, "dp", 2)
    input_grad = place_cells(input_pair[:kept], order.then(input_far)[0])
    order.done(input_grad)
    (small_far,) = order.step(small_far)
    small = small + small_far
    small_far = swap(small, "dp", 4)
    cell_outputs = place_cells(output_pair[:kept], order.then(output_far)[0])
    order.done(cell_outputs)
    (small_far,) = order.step(small_far)
    small = later_groups(small + small_far)
    qkv_total, out_total = attn_sum.last_halves(order, (3 * shard, shard))

    return (
        cell_outputs,
        input_grad,
        small[0:2],
        small[2:4],
        qkv_total.reshape(3, shard, width).transpose(2, 0, 1),
        small[-2, : 2 * shard].reshape(2, shard),
        out_total,
        small[4:6],
        up_total,
        small[-1],
        down_total,
        small[6:-2],
    )


def solution(mesh):
    in_specs = (
        P("dp", "tp", None),
        P("dp", "tp", None),
        P("dp"),
        P("dp"),
        P(),
        P(),
        P(None, None, "tp"),
        P(None, "tp"),
        P("tp", None),
        P(),
        P(None, "tp"),
        P("tp"),
        P("tp", None),
        P(),
    )
    out_specs = (
        P("dp", "tp", None),
        P("dp", "tp", None),
        P(),
        P(),
        P(None, None, "tp"),
        P(None, "tp"),
        P("tp", None),
        P(),
        P(None, "tp"),
        P("tp"),
        P("tp", None),
        P(),
    )
    return jax.shard_map(
        on_device, mesh=mesh, in_specs=in_specs, out_specs=out_specs, check_vma=False
    )
```
